128 devices in a mesh: ctx: 16 (over z, y), pool: 2 (over x_hi), tp: 4 (over x_lo, core).
Axes of the slice: x: 4 (x_hi: 2, x_lo: 2; x = x_hi * 2 + x_lo), y: 4, z: 4, core: 2. Of those that a mesh axis runs over, the one named last changes fastest.
Arguments:
- span_hidden_states: bfloat16 [4096, 8192], P(('ctx', 'pool'), 'tp'), may hold values from -6 to 6
- span_token_queries: bfloat16 [4096, 8192], P(('ctx', 'pool'), 'tp'), as said below
- earlier_key_values: bfloat16 [8, 4096, 256], P('tp', ('ctx', 'pool')), as said below
- decode_hidden_states: bfloat16 [512, 4, 8192], P(('ctx', 'pool'), None, 'tp'), may hold values from -6 to 6
- decode_token_queries: bfloat16 [512, 4, 8192], P(('ctx', 'pool'), None, 'tp'), as said below
- decode_row_cache: bfloat16 [512, 8, 256, 256], P(('ctx', 'pool'), 'tp'), as said below
- key_value_weight: bfloat16 [8192, 2048], P('tp'), may hold values from -0.0625 to 0.0625
- adapter_down_weight: bfloat16 [8192, 128], P('tp'), may hold values from -0.0625 to 0.0625
- adapter_up_weight: bfloat16 [128, 2048], replicated, may hold values from -1.5 to 1.5
- prompt_adapter: int32 [4096], P(('ctx', 'pool')), may hold values from 0 to 7
- row_adapter_index: int32 [512], P(('ctx', 'pool')), may hold values from 0 to 7
- group_live_rows: int32 [32], P(('ctx', 'pool')), may hold values from 1 to 16, as said below
- cached_row_lengths: int32 [512], P(('ctx', 'pool')), may hold values from 2 to 256, as said below
- block_target_page: int32 [256], replicated, may hold values from 0 to 255, each once
Outputs:
- span_attention: bfloat16 [4096, 8192], P(('ctx', 'pool'), 'tp')
- handoff_pages: bfloat16 [256, 8, 16, 256], P(('ctx', 'pool'), 'tp')
- decode_attention: bfloat16 [512, 4, 8192], P(('ctx', 'pool'), None, 'tp')
The draws below stay inside these ranges and needn't reach their ends.
Inputs may be any that keep to these rules, and one draw needn't show every extreme that they name: `span_token_queries`: queries of the span. `earlier_key_values`: keys and values of the earlier tokens. `decode_token_queries`: queries of the decode tokens. `decode_row_cache`: cached keys and values; slots at or past a row's length are never read. `group_live_rows`: live rows of each group of 16 slots are its first ones; some group is full. `cached_row_lengths`: some row uses all 256 slots.
All inputs are finite; a program needn't handle non-finite values.
Results may differ from the reference program's by a relative error of at most 0.0081.
Values may be sent and summed in bfloat16 or wider, within the bound.
No kernel may reach another device: no remote copies, remote signals or barrier semaphores. Data moves between devices by JAX's collectives and lax.ppermute only.
A program may use at most 192 MiB of HBM per device.

```python
import math
import jax
import jax.numpy as jnp
from jax import lax

MODEL_WIDTH = 8192
HQ = 64
KEY_VALUE_HEADS = 8
HEAD_SIZE = 128
ADAPTER_RANK = 16
ADAPTER_COUNT = 8
BLK = 16
DECODE_STEPS = 4
ROWS_DEV = 16
CACHE = 256
GROUPS = 32
SPAN_TOKENS = 4096
PRIOR = 4096
DECODE_SLOTS = 512
NBLK = 256


def prior_keys(key):
    base_keys = jax.random.normal(key, (KEY_VALUE_HEADS, PRIOR, HEAD_SIZE), jnp.float32)
    noise_keys = jax.random.normal(jax.random.fold_in(key, 77), (KEY_VALUE_HEADS, PRIOR, HEAD_SIZE), jnp.float32)
    position = jnp.arange(PRIOR)
    strength = 100.0 + 200.0 * (position // 64 % 4) / 3.0
    spread_near = 2.0 * math.sqrt(HEAD_SIZE) / strength
    previous = jnp.roll(base_keys, 1, axis=1)
    partner = position % 64 == 6
    return jnp.where(partner[None, :, None], previous + spread_near[None, :, None] * noise_keys, base_keys)


def cache_keys(key):
    base_keys = jax.random.normal(key, (DECODE_SLOTS, KEY_VALUE_HEADS, CACHE, HEAD_SIZE), jnp.float32)
    noise_keys = jax.random.normal(jax.random.fold_in(key, 79), (DECODE_SLOTS, KEY_VALUE_HEADS, 1, HEAD_SIZE), jnp.float32)
    row_index = jnp.arange(DECODE_SLOTS)
    strength = 100.0 + 200.0 * (row_index % 4) / 3.0
    spread_near = 2.0 * math.sqrt(HEAD_SIZE) / strength
    partner = base_keys[:, :, 0:1] + spread_near[:, None, None, None] * noise_keys
    return jnp.concatenate([base_keys[:, :, 0:1], partner, base_keys[:, :, 2:]], axis=2)


def draw_earlier_key_values(key, part):
    keys_part = prior_keys(key)
    key = jax.random.fold_in(key, 3)
    values_part = jax.random.normal(key, (KEY_VALUE_HEADS, PRIOR, HEAD_SIZE), jnp.float32)
    return jnp.concatenate([keys_part, values_part], axis=2).astype(jnp.bfloat16)


def draw_span_token_queries(key, part):
    key = jax.random.fold_in(key, 5)
    base_queries = 2.0 * jax.random.normal(key, (SPAN_TOKENS, HQ, HEAD_SIZE), jnp.float32)
    return base_queries.reshape(SPAN_TOKENS, HQ * HEAD_SIZE).astype(jnp.bfloat16)


def draw_decode_row_cache(key, part):
    keys_part = cache_keys(key)
    key = jax.random.fold_in(key, 9)
    values_part = jax.random.normal(key, (DECODE_SLOTS, KEY_VALUE_HEADS, CACHE, HEAD_SIZE), jnp.float32)
    return jnp.concatenate([keys_part, values_part], axis=3).astype(jnp.bfloat16)


def draw_decode_token_queries(key, part):
    key = jax.random.fold_in(key, 13)
    base_queries = 2.0 * jax.random.normal(key, (DECODE_SLOTS, DECODE_STEPS, HQ, HEAD_SIZE), jnp.float32)
    return base_queries.reshape(DECODE_SLOTS, DECODE_STEPS, HQ * HEAD_SIZE).astype(jnp.bfloat16)


def draw_group_live_rows(key, part):
    key = jax.random.fold_in(key, 17)
    drawn_counts = jax.random.randint(key, (GROUPS,), 1, ROWS_DEV + 1)
    full_group = jax.random.randint(jax.random.fold_in(key, 1), (), 0, GROUPS)
    return jnp.where(jnp.arange(GROUPS) == full_group, ROWS_DEV, drawn_counts).astype(jnp.int32)


def draw_cached_row_lengths(key, part):
    key = jax.random.fold_in(key, 19)
    drawn_lengths = jax.random.randint(key, (DECODE_SLOTS,), 2, CACHE + 1)
    full_row = jax.random.randint(jax.random.fold_in(key, 1), (), 0, DECODE_SLOTS)
    return jnp.where(jnp.arange(DECODE_SLOTS) == full_row, CACHE, drawn_lengths).astype(jnp.int32)


def with_ends(array, stream_key, least, high):
    longest = array.shape.index(max(array.shape))
    spots = []
    for shift in (0, 1):
        where = [jax.random.randint(jax.random.fold_in(stream_key, axis), (), 0, length) for axis, length in enumerate(array.shape)]
        where[longest] = (where[longest] + shift) % array.shape[longest]
        spots.append(tuple(where))
    return array.at[spots[0]].set(least).at[spots[1]].set(high)


def block_levels(stream_key, shape, shards, low, high):
    loudness = 1.0
    for dim, blocks in shards:
        steps = jax.random.uniform(jax.random.fold_in(jax.random.fold_in(stream_key, 6), dim), (blocks,), jnp.float32, low / len(shards), high / len(shards))
        loudness = loudness * jnp.repeat(jnp.exp(steps), shape[dim] // blocks).reshape((-1,) + (1,) * (len(shape) - 1 - dim))
    return loudness


def gaussian(stream_key, dims, spread, limit, pieces=(), held_as=jnp.bfloat16):
    entries = jax.random.normal(stream_key, dims, jnp.float32) * spread
    if len(pieces) > 0:
        entries = block_levels(stream_key, dims, pieces, -0.22, 0.18) * entries
    return jnp.clip(entries, min=-limit, max=limit).astype(held_as)


def setup_inputs(seed: int = 0) -> dict:
    key_list = jax.random.split(jax.random.key(seed), 15)
    return {
        "span_hidden_states": gaussian(key_list[0], (SPAN_TOKENS, MODEL_WIDTH), 1.0, 6.0, ((0, 32), (1, 4))),
        "span_token_queries": draw_span_token_queries(jax.random.fold_in(key_list[14], 71), 0),
        "earlier_key_values": draw_earlier_key_values(jax.random.fold_in(key_list[14], 71), 0),
        "decode_hidden_states": gaussian(key_list[3], (DECODE_SLOTS, DECODE_STEPS, MODEL_WIDTH), 1.0, 6.0, ((0, 32), (2, 4))),
        "decode_token_queries": draw_decode_token_queries(jax.random.fold_in(key_list[14], 71), 0),
        "decode_row_cache": draw_decode_row_cache(jax.random.fold_in(key_list[14], 71), 0),
        "key_value_weight": gaussian(key_list[6], (MODEL_WIDTH, KEY_VALUE_HEADS * 2 * HEAD_SIZE), MODEL_WIDTH ** -0.5, 0.0625, ((0, 4),)),
        "adapter_down_weight": gaussian(key_list[7], (MODEL_WIDTH, ADAPTER_COUNT * ADAPTER_RANK), MODEL_WIDTH ** -0.5, 0.0625, ((0, 4),)),
        "adapter_up_weight": gaussian(key_list[8], (ADAPTER_COUNT * ADAPTER_RANK, KEY_VALUE_HEADS * 2 * HEAD_SIZE), ADAPTER_RANK ** -0.5, 1.5),
        "prompt_adapter": with_ends(jax.random.randint(key_list[9], (SPAN_TOKENS,), 0, ADAPTER_COUNT), jax.random.fold_in(key_list[9], 1), 0, ADAPTER_COUNT - 1).astype(jnp.int32),
        "row_adapter_index": with_ends(jax.random.randint(key_list[10], (DECODE_SLOTS,), 0, ADAPTER_COUNT), jax.random.fold_in(key_list[10], 1), 0, ADAPTER_COUNT - 1).astype(jnp.int32),
        "group_live_rows": draw_group_live_rows(jax.random.fold_in(key_list[14], 71), 0),
        "cached_row_lengths": draw_cached_row_lengths(jax.random.fold_in(key_list[14], 71), 0),
        "block_target_page": jax.random.permutation(key_list[13], NBLK).astype(jnp.int32),
    }


neg_large = -1e+30

def adapter_key_values(hidden_states, adapter_indices, key_value_weight, adapter_down_weight, adapter_up_weight):
    base_part = jnp.dot(hidden_states, key_value_weight, preferred_element_type=jnp.float32)
    narrow_rank = jnp.dot(hidden_states, adapter_down_weight, preferred_element_type=jnp.float32)
    column_holder = jnp.arange(adapter_down_weight.shape[1], dtype=jnp.int32) // ADAPTER_RANK
    masked_scores = jnp.where(column_holder[None, :] == adapter_indices[:, None], narrow_rank, jnp.zeros_like(narrow_rank))
    widen_rank = jnp.dot(masked_scores, adapter_up_weight.astype(jnp.float32), precision=lax.Precision.HIGHEST)
    return (base_part + widen_rank).astype(jnp.bfloat16)

def rounded(weights):
    return lax.optimization_barrier(weights.astype(jnp.bfloat16)).astype(jnp.float32)

def attend_all(scores, visible, values, einsum_form):
    masked_scores = jnp.where(visible, scores, neg_large)
    row_max = lax.optimization_barrier(jnp.max(masked_scores, axis=-1, keepdims=True))
    weights = jnp.where(visible, jnp.exp(masked_scores - row_max), jnp.zeros_like(masked_scores))
    row_total = lax.optimization_barrier(jnp.sum(weights, axis=-1))
    numerator = jnp.einsum(einsum_form, rounded(weights), values)
    return numerator / row_total[..., None]

def reference(span_hidden_states, span_token_queries, earlier_key_values, decode_hidden_states, decode_token_queries, decode_row_cache, key_value_weight, adapter_down_weight, adapter_up_weight, prompt_adapter, row_adapter_index, group_live_rows, cached_row_lengths, block_target_page):
    group_size = HQ // KEY_VALUE_HEADS
    scale_factor = 1.0 / math.sqrt(HEAD_SIZE)
    span_adapter_indices = prompt_adapter.astype(jnp.int32)
    span_key_values = adapter_key_values(span_hidden_states, span_adapter_indices, key_value_weight, adapter_down_weight, adapter_up_weight).reshape(SPAN_TOKENS, KEY_VALUE_HEADS, 2 * HEAD_SIZE)
    head_major = jnp.transpose(span_key_values, (1, 0, 2))
    all_keys = jnp.concatenate([earlier_key_values, head_major], axis=1)
    key_index = jnp.arange(PRIOR + SPAN_TOKENS, dtype=jnp.int32)
    queries = span_token_queries.reshape(SPAN_TOKENS, KEY_VALUE_HEADS, group_size, HEAD_SIZE)
    query_block = math.gcd(SPAN_TOKENS, 512)
    block_total = SPAN_TOKENS // query_block

    def head_output(head_index):
        head_keys = lax.dynamic_index_in_dim(all_keys, head_index, 0, keepdims=False).astype(jnp.float32)
        head_queries = lax.dynamic_index_in_dim(queries, head_index, 1, keepdims=False)

        def block_output(block_index):
            block_queries = lax.dynamic_slice_in_dim(head_queries, block_index * query_block, query_block, 0).astype(jnp.float32)
            scores = jnp.einsum('tgc,nc->tgn', block_queries, head_keys[:, :HEAD_SIZE]) * scale_factor
            query_pos = block_index * query_block + jnp.arange(query_block, dtype=jnp.int32)
            visible = (key_index[None, :] < PRIOR) | (key_index[None, :] - PRIOR <= query_pos[:, None])
            return attend_all(scores, visible[:, None, :], head_keys[:, HEAD_SIZE:], 'tgn,nc->tgc')
        outputs = lax.map(block_output, jnp.arange(block_total, dtype=jnp.int32))
        return outputs.reshape(SPAN_TOKENS, group_size, HEAD_SIZE)
    per_head = lax.map(head_output, jnp.arange(KEY_VALUE_HEADS, dtype=jnp.int32))
    span_attention = jnp.transpose(per_head, (1, 0, 2, 3)).reshape(SPAN_TOKENS, HQ * HEAD_SIZE).astype(jnp.bfloat16)
    blocks = span_key_values.reshape(NBLK, BLK, KEY_VALUE_HEADS, 2 * HEAD_SIZE)
    source = jnp.zeros((NBLK,), jnp.int32).at[block_target_page].set(jnp.arange(NBLK, dtype=jnp.int32))
    handoff_pages = jnp.transpose(blocks[source], (0, 2, 1, 3))
    decode_adapter_indices = jnp.repeat(row_adapter_index, DECODE_STEPS).astype(jnp.int32)
    newest_key_values = adapter_key_values(decode_hidden_states.reshape(DECODE_SLOTS * DECODE_STEPS, MODEL_WIDTH), decode_adapter_indices, key_value_weight, adapter_down_weight, adapter_up_weight).reshape(DECODE_SLOTS, DECODE_STEPS, KEY_VALUE_HEADS, 2 * HEAD_SIZE)
    dec_queries = decode_token_queries.reshape(DECODE_SLOTS, DECODE_STEPS, KEY_VALUE_HEADS, group_size, HEAD_SIZE)
    slot_index = jnp.arange(CACHE + DECODE_STEPS, dtype=jnp.int32)
    step_index = jnp.arange(DECODE_STEPS, dtype=jnp.int32)

    def group_output(group_index):
        first_row = group_index * ROWS_DEV
        cache_rows = lax.dynamic_slice_in_dim(decode_row_cache, first_row, ROWS_DEV, 0).astype(jnp.float32)
        fresh_rows = jnp.transpose(lax.dynamic_slice_in_dim(newest_key_values, first_row, ROWS_DEV, 0), (0, 2, 1, 3)).astype(jnp.float32)
        keys_values = jnp.concatenate([cache_rows, fresh_rows], axis=2)
        row_queries = lax.dynamic_slice_in_dim(dec_queries, first_row, ROWS_DEV, 0).astype(jnp.float32)
        scores = jnp.einsum('rshgc,rhnc->rshgn', row_queries, keys_values[..., :HEAD_SIZE]) * scale_factor
        row_lengths = lax.dynamic_slice_in_dim(cached_row_lengths, first_row, ROWS_DEV, 0)
        in_cache = (slot_index[None, None, :] < CACHE) & (slot_index[None, None, :] < row_lengths[:, None, None])
        in_fresh = (slot_index[None, None, :] >= CACHE) & (slot_index[None, None, :] - CACHE <= step_index[None, :, None])
        visible = (in_cache | in_fresh)[:, :, None, None, :]
        output = attend_all(scores, visible, keys_values[..., HEAD_SIZE:], 'rshgn,rhnc->rshgc')
        live_rows = jnp.arange(ROWS_DEV, dtype=jnp.int32) < lax.dynamic_index_in_dim(group_live_rows, group_index, 0, keepdims=False)
        return jnp.where(live_rows[:, None, None, None, None], output, jnp.zeros_like(output))
    decoded = lax.map(group_output, jnp.arange(GROUPS, dtype=jnp.int32))
    decode_attention = decoded.reshape(DECODE_SLOTS, DECODE_STEPS, HQ * HEAD_SIZE).astype(jnp.bfloat16)
    return (span_attention, handoff_pages, decode_attention)
```

```python
import functools
import math

import jax
import jax.numpy as jnp
from jax import lax
from jax.experimental import pallas as pl
from jax.experimental.pallas import tpu as pltpu
from jax.sharding import PartitionSpec as P

HQ = 64
KEY_VALUE_HEADS = 8
HEAD_SIZE = 128
ADAPTER_RANK = 16
BLK = 16
STEPS = 4
GROUP = HQ // KEY_VALUE_HEADS
SHARDS = 16
SIDE = 4
TOKENS = 128
ROWS = 16
DECODE = ROWS * STEPS
ALL_ROWS = TOKENS + DECODE
LOG2_SCALE = math.log2(math.e) / math.sqrt(HEAD_SIZE)
neg_large = -1e30
MIB = 2**20


def split3(x):
    hi = x.astype(jnp.bfloat16)
    rest = x - hi.astype(jnp.float32)
    mid = rest.astype(jnp.bfloat16)
    low = (rest - mid.astype(jnp.float32)).astype(jnp.bfloat16)
    return hi, mid, low


def project_kernel(
    block_ref, row_adapter_ref, span_ref, decode_ref, weight_ref, down_ref, up_ref, adapter_ref, out_ref, rank_ref
):
    hidden = jnp.concatenate([span_ref[...], decode_ref[...]], axis=0)

    @pl.when(pl.program_id(0) == 0)
    def _():
        narrow = jnp.dot(hidden, down_ref[...], preferred_element_type=jnp.float32)
        span_owner = jnp.transpose(jnp.broadcast_to(adapter_ref[...], (TOKENS, TOKENS)))
        row = lax.broadcasted_iota(jnp.int32, (DECODE, TOKENS), 0) // STEPS
        decode_owner = jnp.zeros((DECODE, TOKENS), jnp.int32)
        for r in range(ROWS):
            decode_owner = jnp.where(row == r, row_adapter_ref[r], decode_owner)
        owner = jnp.concatenate([span_owner, decode_owner], axis=0)
        column = lax.broadcasted_iota(jnp.int32, (ALL_ROWS, TOKENS), 1) // ADAPTER_RANK
        hi, mid, low = split3(jnp.where(column == owner, narrow, 0.0))
        rank_ref[:, :TOKENS] = hi
        rank_ref[:, TOKENS : 2 * TOKENS] = mid
        rank_ref[:, 2 * TOKENS :] = low

    up = up_ref[...]
    out_ref[0] = jnp.dot(hidden, weight_ref[...], preferred_element_type=jnp.float32) + jnp.dot(
        rank_ref[...], jnp.concatenate([up, up, up], axis=0), preferred_element_type=jnp.float32
    )


def project(blocks, row_adapter, span, decode, weight, down, up, adapter):
    count = blocks.shape[0]
    depth = span.shape[1]
    width = 2 * HEAD_SIZE
    whole = lambda i, *_: (0, 0)
    return pl.pallas_call(
        project_kernel,
        grid_spec=pltpu.PrefetchScalarGridSpec(
            num_scalar_prefetch=2,
            grid=(count,),
            in_specs=[
                pl.BlockSpec((TOKENS, depth), whole),
                pl.BlockSpec((DECODE, depth), whole),
                pl.BlockSpec((depth, width), lambda i, blocks, rows: (0, blocks[i])),
                pl.BlockSpec((depth, TOKENS), whole),
                pl.BlockSpec((TOKENS, width), lambda i, blocks, rows: (0, blocks[i])),
                pl.BlockSpec((1, TOKENS), whole),
            ],
            out_specs=pl.BlockSpec((1, ALL_ROWS, width), lambda i, *_: (i, 0, 0)),
            scratch_shapes=[pltpu.VMEM((ALL_ROWS, 3 * TOKENS), jnp.bfloat16)],
        ),
        out_shape=jax.ShapeDtypeStruct((count, ALL_ROWS, width), jnp.float32),
        compiler_params=pltpu.CompilerParams(vmem_limit_bytes=16 * MIB),
        cost_estimate=pl.CostEstimate(
            flops=2 * ALL_ROWS * depth * width * count,
            bytes_accessed=depth * width * count * 2 + 2 * MIB,
            transcendentals=0,
        ),
        name="project",
    )(blocks, row_adapter, span, decode, weight, down, up, adapter)


TILE = 2
KEYS = 1024
PER = KEYS // TOKENS


def attend_kernel(partner, visible_ref, q_ref, prior_ref, *refs):
    pieces = refs[:SIDE]
    refs = refs[SIDE:]
    if partner:
        out_ref, top_ref, acc_ref, ext_ref, key_ref = refs
    else:
        other_ref, out_ref, top_ref, acc_ref, ext_ref, key_ref = refs
    rows = TILE * TOKENS
    tiles = GROUP // TILE
    queries = [
        jnp.concatenate(
            [q_ref[:, (i * TILE + j) * HEAD_SIZE : (i * TILE + j + 1) * HEAD_SIZE] for j in range(TILE)], axis=0
        )
        for i in range(tiles)
    ]
    ext_ref[:, HEAD_SIZE:] = jnp.ones((2 * KEYS, HEAD_SIZE), jnp.bfloat16)
    lane = lax.broadcasted_iota(jnp.int32, (TOKENS, HEAD_SIZE), 1)
    if partner:
        stats = jnp.zeros((TOKENS, HEAD_SIZE), jnp.bfloat16)
    else:
        other_stats = other_ref[:, GROUP * HEAD_SIZE :].astype(jnp.float32)
    blocks = 2 * SHARDS // PER
    for b in range(blocks):
        slot = (b % 2) * KEYS
        if b < blocks // 2:
            kv = prior_ref[b * PER : (b + 1) * PER, 0].reshape(KEYS, 2 * HEAD_SIZE)
            keys = kv[:, :HEAD_SIZE]
            ext_ref[slot : slot + KEYS, :HEAD_SIZE] = kv[:, HEAD_SIZE:]
        else:
            first = (b - blocks // 2) * PER
            for n in range(PER):
                kv = pieces[(first + n) // SIDE][(first + n) % SIDE]
                seen = visible_ref[first + n] != 0
                here = slice(slot + n * TOKENS, slot + (n + 1) * TOKENS)
                key_ref[here, :] = jnp.where(seen, kv[:, :HEAD_SIZE], prior_ref[0, 0, :, :HEAD_SIZE])
                ext_ref[here, :HEAD_SIZE] = jnp.where(seen, kv[:, HEAD_SIZE:], jnp.zeros_like(kv[:, HEAD_SIZE:]))
                ext_ref[here, HEAD_SIZE:] = jnp.where(seen, 1.0, 0.0).astype(jnp.bfloat16) * jnp.ones(
                    (TOKENS, HEAD_SIZE), jnp.bfloat16
                )
            keys = key_ref[slot : slot + KEYS, :]
        for i in range(tiles):
            here = slice(i * rows, (i + 1) * rows)
            scores = lax.dot_general(
                queries[i], keys, (((1,), (1,)), ((), ())), preferred_element_type=jnp.float32
            )
            if b == blocks // 2 and not partner:
                token = lax.broadcasted_iota(jnp.int32, (rows, TOKENS), 0) % TOKENS
                key = lax.broadcasted_iota(jnp.int32, (rows, TOKENS), 1)
                scores = jnp.concatenate(
                    [jnp.where(key <= token, scores[:, :TOKENS], neg_large), scores[:, TOKENS:]], axis=1
                )
            top = jnp.max(scores, axis=1, keepdims=True) * LOG2_SCALE
            if b > 0:
                before = top_ref[here, :1]
                top = jnp.maximum(before, top)
                rescale = jnp.exp2(before - top)
            weights = jnp.exp2(scores * LOG2_SCALE - top)
            total = jnp.dot(
                weights.astype(jnp.bfloat16), ext_ref[slot : slot + KEYS, :], preferred_element_type=jnp.float32
            )
            if b > 0:
                total = acc_ref[here] * rescale + total
            if b < blocks - 1:
                acc_ref[here] = total
                top_ref[here] = jnp.broadcast_to(top, (rows, HEAD_SIZE))
                continue
            out = total[:, :HEAD_SIZE] / total[:, HEAD_SIZE:]
            level = top + jnp.log2(total[:, HEAD_SIZE:])
            for j in range(TILE):
                g = i * TILE + j
                columns = slice(g * HEAD_SIZE, (g + 1) * HEAD_SIZE)
                own = slice(j * TOKENS, (j + 1) * TOKENS)
                if partner:
                    out_ref[:, columns] = out[own].astype(jnp.bfloat16)
                    for part, piece in enumerate(split3(level[own])):
                        stats = jnp.where(lane == part * GROUP + g, piece, stats)
                else:
                    other_level = (
                        other_stats[:, g : g + 1]
                        + other_stats[:, GROUP + g : GROUP + g + 1]
                        + other_stats[:, 2 * GROUP + g : 2 * GROUP + g + 1]
                    )
                    peak = jnp.maximum(level[own], other_level)
                    mine = jnp.exp2(level[own] - peak)
                    theirs = jnp.exp2(other_level - peak)
                    mixed = mine * out[own] + theirs * other_ref[:, columns].astype(jnp.float32)
                    out_ref[:, columns] = (mixed / (mine + theirs)).astype(jnp.bfloat16)
    if partner:
        out_ref[:, GROUP * HEAD_SIZE :] = stats


def attend(visible, queries, head, prior, pieces, other=None):
    partner = other is None
    width = GROUP * HEAD_SIZE
    out_width = width + HEAD_SIZE if partner else width
    whole3 = lambda i, *_: (0, 0, 0)
    in_specs = [
        pl.BlockSpec((TOKENS, width), lambda i, *_: (0, head)),
        pl.BlockSpec((SHARDS, 1, TOKENS, 2 * HEAD_SIZE), lambda i, *_: (0, head, 0, 0)),
    ] + [pl.BlockSpec((SIDE, TOKENS, 2 * HEAD_SIZE), whole3)] * SIDE
    operands = [queries, prior] + list(pieces)
    if not partner:
        in_specs.append(pl.BlockSpec((TOKENS, width + HEAD_SIZE), lambda i, *_: (0, 0)))
        operands.append(other)
    rows = GROUP * TOKENS
    total_keys = 2 * SHARDS * TOKENS
    return pl.pallas_call(
        functools.partial(attend_kernel, partner),
        grid_spec=pltpu.PrefetchScalarGridSpec(
            num_scalar_prefetch=1,
            grid=(1,),
            in_specs=in_specs,
            out_specs=pl.BlockSpec((TOKENS, out_width), lambda i, *_: (0, 0)),
            scratch_shapes=[
                pltpu.VMEM((rows, HEAD_SIZE), jnp.float32),
                pltpu.VMEM((rows, 2 * HEAD_SIZE), jnp.float32),
                pltpu.VMEM((2 * KEYS, 2 * HEAD_SIZE), jnp.bfloat16),
                pltpu.VMEM((2 * KEYS, HEAD_SIZE), jnp.bfloat16),
            ],
        ),
        out_shape=jax.ShapeDtypeStruct((TOKENS, out_width), jnp.bfloat16),
        compiler_params=pltpu.CompilerParams(vmem_limit_bytes=32 * MIB),
        cost_estimate=pl.CostEstimate(
            flops=8 * rows * total_keys * HEAD_SIZE, bytes_accessed=3 * MIB, transcendentals=rows * total_keys
        ),
        name="attend_partner" if partner else "attend_own",
    )(visible, *operands)


ROW_BLOCK = 4


def decode_kernel(length_ref, live_ref, q_ref, cache_ref, fresh_ref, out_ref):
    first = pl.program_id(0) * ROW_BLOCK
    query_rows = STEPS * GROUP
    cache_size = cache_ref.shape[2]
    fresh_row = lax.broadcasted_iota(jnp.int32, (query_rows, DECODE), 1) // STEPS
    fresh_step = lax.broadcasted_iota(jnp.int32, (query_rows, DECODE), 1) % STEPS
    step = lax.broadcasted_iota(jnp.int32, (query_rows, DECODE), 0) // GROUP
    slot = lax.broadcasted_iota(jnp.int32, (query_rows, cache_size), 1)
    contract = (((1,), (1,)), ((), ()))
    for n in range(ROW_BLOCK):
        row = first + n
        length = length_ref[row]
        live = row < live_ref[0]
        for h in range(2):
            queries = q_ref[n, h]
            cached = lax.dot_general(
                queries, cache_ref[n, h, :, :HEAD_SIZE], contract, preferred_element_type=jnp.float32
            )
            fresh = lax.dot_general(
                queries, fresh_ref[h, :, :HEAD_SIZE], contract, preferred_element_type=jnp.float32
            )
            cached = jnp.where(slot < length, cached, neg_large)
            fresh = jnp.where((fresh_row == row) & (fresh_step <= step), fresh, neg_large)
            top = jnp.maximum(jnp.max(cached, axis=1, keepdims=True), jnp.max(fresh, axis=1, keepdims=True))
            cached = jnp.exp2((cached - top) * LOG2_SCALE)
            fresh = jnp.exp2((fresh - top) * LOG2_SCALE)
            total = jnp.sum(cached, axis=1, keepdims=True) + jnp.sum(fresh, axis=1, keepdims=True)
            out = jnp.dot(
                cached.astype(jnp.bfloat16), cache_ref[n, h, :, HEAD_SIZE:], preferred_element_type=jnp.float32
            ) + jnp.dot(
                fresh.astype(jnp.bfloat16), fresh_ref[h, :, HEAD_SIZE:], preferred_element_type=jnp.float32
            )
            out_ref[n, h] = jnp.where(live, out / total, 0.0).astype(jnp.bfloat16)


def decode_attend(lengths, live, queries, cache, fresh):
    rows, heads, query_rows, _ = queries.shape
    cache_size = cache.shape[2]
    return pl.pallas_call(
        decode_kernel,
        grid_spec=pltpu.PrefetchScalarGridSpec(
            num_scalar_prefetch=2,
            grid=(rows // ROW_BLOCK,),
            in_specs=[
                pl.BlockSpec((ROW_BLOCK, heads, query_rows, HEAD_SIZE), lambda i, *_: (i, 0, 0, 0)),
                pl.BlockSpec((ROW_BLOCK, heads, cache_size, 2 * HEAD_SIZE), lambda i, *_: (i, 0, 0, 0)),
                pl.BlockSpec((heads, DECODE, 2 * HEAD_SIZE), lambda i, *_: (0, 0, 0)),
            ],
            out_specs=pl.BlockSpec((ROW_BLOCK, heads, query_rows, HEAD_SIZE), lambda i, *_: (i, 0, 0, 0)),
        ),
        out_shape=jax.ShapeDtypeStruct(queries.shape, jnp.bfloat16),
        compiler_params=pltpu.CompilerParams(vmem_limit_bytes=16 * MIB),
        cost_estimate=pl.CostEstimate(
            flops=8 * rows * heads * query_rows * cache_size * HEAD_SIZE,
            bytes_accessed=5 * MIB,
            transcendentals=rows * heads * query_rows * cache_size,
        ),
        name="decode",
    )(lengths, live, queries, cache, fresh)


def pages_kernel(count, where_ref, *refs):
    first_head, second_head = refs[:SIDE], refs[SIDE : 2 * SIDE]
    out_ref, sems = refs[2 * SIDE :]

    def copies(n, k):
        dz, dy, block = where_ref[0, n], where_ref[1, n], where_ref[2, n]
        rows = pl.ds(pl.multiple_of(block * BLK, BLK), BLK)
        return (
            (dz, pltpu.make_async_copy(first_head[k].at[dy, rows], out_ref.at[n, 0], sems.at[n, 0])),
            (dy, pltpu.make_async_copy(second_head[k].at[dz, rows], out_ref.at[n, 1], sems.at[n, 1])),
        )

    for n in range(count):
        for k in range(SIDE):
            for piece, copy in copies(n, k):

                @pl.when(piece == k)
                def _():
                    copy.start()

    for n in range(count):
        for _, copy in copies(n, 0):
            copy.wait()


def pick_pages(where, first_head, second_head):
    count = where.shape[1]
    return pl.pallas_call(
        functools.partial(pages_kernel, count),
        grid_spec=pltpu.PrefetchScalarGridSpec(
            num_scalar_prefetch=1,
            grid=(1,),
            in_specs=[pl.BlockSpec(memory_space=pl.ANY)] * (2 * SIDE),
            out_specs=pl.BlockSpec(memory_space=pl.ANY),
            scratch_shapes=[pltpu.SemaphoreType.DMA((count, 2))],
        ),
        out_shape=jax.ShapeDtypeStruct((count, 2, BLK, 2 * HEAD_SIZE), jnp.bfloat16),
        cost_estimate=pl.CostEstimate(flops=0, bytes_accessed=MIB, transcendentals=0),
        name="pages",
    )(where, *first_head, *second_head)


def shift(x, dz, dy):
    perm = [
        (z * SIDE + y, ((z + dz) % SIDE) * SIDE + (y + dy) % SIDE) for z in range(SIDE) for y in range(SIDE)
    ]
    return lax.ppermute(x, "ctx", perm)


def swap_pool(x):
    return lax.ppermute(x, "pool", [(0, 1), (1, 0)])


def swap_tp(x, bit):
    return lax.ppermute(x, "tp", [(i, i ^ bit) for i in range(4)])


def ring(x, along_z):
    move = (lambda d: shift(x, d, 0)) if along_z else (lambda d: shift(x, 0, d))
    far = {1: move(1), 3: move(3), 2: move(2)}
    return [x, far[1], far[2], far[3]]


def per_device(
    span_hidden_states,
    span_token_queries,
    earlier_key_values,
    decode_hidden_states,
    decode_token_queries,
    decode_row_cache,
    key_value_weight,
    adapter_down_weight,
    adapter_up_weight,
    prompt_adapter,
    row_adapter_index,
    group_live_rows,
    cached_row_lengths,
    block_target_page,
):
    tp = lax.axis_index("tp")
    ctx = lax.axis_index("ctx")
    pool = lax.axis_index("pool")
    my_z, my_y = ctx // SIDE, ctx % SIDE
    depth = span_hidden_states.shape[1]

    prior = lax.all_gather(earlier_key_values, "ctx", axis=0)

    decode_hidden = decode_hidden_states.reshape(DECODE, depth)

    def heads_of(bits):
        return jnp.stack([2 * jnp.bitwise_xor(tp, bit) + j for bit in bits for j in range(2)]).astype(jnp.int32)

    def partial_kv(bits):
        return project(
            heads_of(bits),
            row_adapter_index,
            span_hidden_states,
            decode_hidden,
            key_value_weight,
            adapter_down_weight,
            adapter_up_weight,
            prompt_adapter.reshape(1, TOKENS),
        )

    from_core = swap_tp(partial_kv((1, 3)), 1)
    summed = partial_kv((0, 2)) + from_core
    from_chip = swap_tp(summed[2:].astype(jnp.bfloat16), 2)
    own_kv = (summed[:2] + from_chip.astype(jnp.float32)).astype(jnp.bfloat16)

    planes0 = ring(jnp.concatenate([p[None] for p in ring(own_kv[0, :TOKENS], False)]), True)
    planes1 = ring(jnp.concatenate([p[None] for p in ring(own_kv[1, :TOKENS], True)]), False)

    queries = decode_token_queries.reshape(ROWS, STEPS, 2, GROUP, HEAD_SIZE)
    queries = jnp.transpose(queries, (0, 2, 1, 3, 4)).reshape(ROWS, 2, STEPS * GROUP, HEAD_SIZE)
    decoded = decode_attend(
        cached_row_lengths, group_live_rows, queries, decode_row_cache, own_kv[:, TOKENS:]
    )
    decoded = jnp.transpose(decoded.reshape(ROWS, 2, STEPS, GROUP, HEAD_SIZE), (0, 2, 1, 3, 4))
    decode_attention = decoded.reshape(ROWS, STEPS, 2 * GROUP * HEAD_SIZE)

    far = jnp.arange(SIDE, dtype=jnp.int32)
    shard_z, shard_y = jnp.mod(my_z - far, SIDE), jnp.mod(my_y - far, SIDE)
    place = shard_z[:, None] * SIDE + shard_y[None, :]
    partner_sees = (place < ctx) | ((place == ctx) & (pool == 0))
    own_sees = place <= ctx
    visible = [[m.reshape(-1), m.T.reshape(-1)] for m in (partner_sees.astype(jnp.int32), own_sees.astype(jnp.int32))]
    partner_queries = swap_pool(span_token_queries)
    planes = [planes0, planes1]
    sent = [swap_pool(attend(visible[0][h], partner_queries, h, prior, planes[h])) for h in range(2)]
    span_attention = jnp.concatenate(
        [attend(visible[1][h], span_token_queries, h, prior, planes[h], sent[h]) for h in range(2)], axis=1
    )

    pages = TOKENS // BLK
    shard = ctx * 2 + pool
    partner_shard = ctx * 2 + 1 - pool
    page_ids = jnp.concatenate([shard * pages + jnp.arange(pages), partner_shard * pages + jnp.arange(pages)])
    block_ids = jnp.arange(block_target_page.shape[0], dtype=jnp.int32)
    source = jnp.sum(
        jnp.where(block_target_page[None, :] == page_ids[:, None], block_ids[None, :], 0), axis=1
    )
    source_shard = source // pages
    source_ctx = source_shard // 2
    where = jnp.stack(
        [
            jnp.mod(my_z - source_ctx // SIDE, SIDE),
            jnp.mod(my_y - source_ctx % SIDE, SIDE),
            source % pages,
        ]
    ).astype(jnp.int32)
    found = pick_pages(where, planes0, planes1)
    from_partner = swap_pool(found[pages:])
    mine = (source_shard % 2 == pool)[:pages]
    handoff_pages = jnp.where(mine[:, None, None, None], found[:pages], from_partner)
    return (span_attention, handoff_pages, decode_attention)


def solution(mesh):
    in_specs = (
        P(("ctx", "pool"), "tp"),
        P(("ctx", "pool"), "tp"),
        P("tp", ("ctx", "pool"), None),
        P(("ctx", "pool"), None, "tp"),
        P(("ctx", "pool"), None, "tp"),
        P(("ctx", "pool"), "tp", None, None),
        P("tp", None),
        P("tp", None),
        P(),
        P(("ctx", "pool")),
        P(("ctx", "pool")),
        P(("ctx", "pool")),
        P(("ctx", "pool")),
        P(),
    )
    out_specs = (
        P(("ctx", "pool"), "tp"),
        P(("ctx", "pool"), "tp", None, None),
        P(("ctx", "pool"), None, "tp"),
    )
    return jax.shard_map(
        per_device, mesh=mesh, in_specs=in_specs, out_specs=out_specs, check_vma=False
    )
```

```python
import functools
import math

import jax
import jax.numpy as jnp
from jax import lax
from jax.experimental import pallas as pl
from jax.experimental.pallas import tpu as pltpu
from jax.sharding import PartitionSpec as P

HQ = 64
KEY_VALUE_HEADS = 8
HEAD_SIZE = 128
ADAPTER_RANK = 16
BLK = 16
STEPS = 4
GROUP = HQ // KEY_VALUE_HEADS
SHARDS = 16
SIDE = 4
TOKENS = 128
ROWS = 16
DECODE = ROWS * STEPS
ALL_ROWS = TOKENS + DECODE
LOG2_SCALE = math.log2(math.e) / math.sqrt(HEAD_SIZE)
neg_large = -1e30
MIB = 2**20
WIDTH = 2 * HEAD_SIZE


def estimate(us):
    return pl.CostEstimate(flops=int(us * 1.1e9), bytes_accessed=MIB, transcendentals=0)


def split3(x):
    hi = x.astype(jnp.bfloat16)
    rest = x - hi.astype(jnp.float32)
    mid = rest.astype(jnp.bfloat16)
    low = (rest - mid.astype(jnp.float32)).astype(jnp.bfloat16)
    return hi, mid, low


def project_kernel(
    block_ref, row_adapter_ref, span_ref, decode_ref, weight_ref, down_ref, up_ref, adapter_ref, out_ref, rank_ref
):
    hidden = jnp.concatenate([span_ref[...], decode_ref[...]], axis=0)

    @pl.when(pl.program_id(0) == 0)
    def _():
        narrow = jnp.dot(hidden, down_ref[...], preferred_element_type=jnp.float32)
        span_owner = jnp.transpose(jnp.broadcast_to(adapter_ref[...], (TOKENS, TOKENS)))
        row = lax.broadcasted_iota(jnp.int32, (DECODE, TOKENS), 0) // STEPS
        decode_owner = jnp.zeros((DECODE, TOKENS), jnp.int32)
        for r in range(ROWS):
            decode_owner = jnp.where(row == r, row_adapter_ref[r], decode_owner)
        owner = jnp.concatenate([span_owner, decode_owner], axis=0)
        column = lax.broadcasted_iota(jnp.int32, (ALL_ROWS, TOKENS), 1) // ADAPTER_RANK
        hi, mid, low = split3(jnp.where(column == owner, narrow, 0.0))
        rank_ref[:, :TOKENS] = hi
        rank_ref[:, TOKENS : 2 * TOKENS] = mid
        rank_ref[:, 2 * TOKENS :] = low

    up = up_ref[...]
    out = jnp.dot(hidden, weight_ref[...], preferred_element_type=jnp.float32) + jnp.dot(
        rank_ref[...], jnp.concatenate([up, up, up], axis=0), preferred_element_type=jnp.float32
    )
    out_ref[0] = out[:, :WIDTH]
    out_ref[1] = out[:, WIDTH:]


def project(blocks, row_adapter, span, decode, weight, down, up, adapter):
    count = blocks.shape[0]
    depth = span.shape[1]
    whole = lambda i, *_: (0, 0)
    return pl.pallas_call(
        project_kernel,
        grid_spec=pltpu.PrefetchScalarGridSpec(
            num_scalar_prefetch=2,
            grid=(count,),
            in_specs=[
                pl.BlockSpec((TOKENS, depth), whole),
                pl.BlockSpec((DECODE, depth), whole),
                pl.BlockSpec((depth, 2 * WIDTH), lambda i, blocks, rows: (0, blocks[i])),
                pl.BlockSpec((depth, TOKENS), whole),
                pl.BlockSpec((TOKENS, 2 * WIDTH), lambda i, blocks, rows: (0, blocks[i])),
                pl.BlockSpec((1, TOKENS), whole),
            ],
            out_specs=pl.BlockSpec((2, ALL_ROWS, WIDTH), lambda i, *_: (i, 0, 0)),
            scratch_shapes=[pltpu.VMEM((ALL_ROWS, 3 * TOKENS), jnp.bfloat16)],
        ),
        out_shape=jax.ShapeDtypeStruct((2 * count, ALL_ROWS, WIDTH), jnp.float32),
        compiler_params=pltpu.CompilerParams(vmem_limit_bytes=56 * MIB),
        cost_estimate=estimate(3.5),
        name="project",
    )(blocks, row_adapter, span, decode, weight, down, up, adapter)


TILE = 2
TILE_ROWS = TILE * TOKENS
TILES = GROUP // TILE
KEYS = 1024
PER = KEYS // TOKENS
HEAD_ROWS = GROUP * TOKENS
HEAD_COLUMNS = GROUP * HEAD_SIZE


def query_tiles(q_ref):
    return [
        jnp.concatenate(
            [q_ref[:, (i * TILE + j) * HEAD_SIZE : (i * TILE + j + 1) * HEAD_SIZE] for j in range(TILE)], axis=0
        )
        for i in range(TILES)
    ]


def absorb(scores, values, top_before, total_before):
    top = jnp.max(scores, axis=1, keepdims=True) * LOG2_SCALE
    if top_before is not None:
        top = jnp.maximum(top_before, top)
    weights = jnp.exp2(scores * LOG2_SCALE - top).astype(jnp.bfloat16)
    total = jnp.dot(weights, values, preferred_element_type=jnp.float32)
    if top_before is not None:
        total = total_before * jnp.exp2(top_before - top) + total
    return top, total


def score(queries, keys):
    return lax.dot_general(queries, keys, (((1,), (1,)), ((), ())), preferred_element_type=jnp.float32)


def prior_kernel(q_ref, *refs):
    pieces = refs[:SIDE]
    top_ref, acc_ref, ext_ref = refs[SIDE + 1 :]
    queries = query_tiles(q_ref)
    ext_ref[:, HEAD_SIZE:] = jnp.ones((2 * KEYS, HEAD_SIZE), jnp.bfloat16)
    for b in range(SHARDS // PER):
        slot = (b % 2) * KEYS
        half = slice(slot, slot + KEYS)
        kv = jnp.concatenate(
            [pieces[b * 2 + j][:, 0].reshape(SIDE * TOKENS, WIDTH) for j in range(PER // SIDE)], axis=0
        )
        ext_ref[half, :HEAD_SIZE] = kv[:, HEAD_SIZE:]
        keys = kv[:, :HEAD_SIZE]
        for i in range(TILES):
            here = slice(i * TILE_ROWS, (i + 1) * TILE_ROWS)
            before = (top_ref[0, here, :1], acc_ref[0, here]) if b else (None, None)
            top, total = absorb(score(queries[i], keys), ext_ref[half, :], *before)
            acc_ref[0, here] = total
            top_ref[0, here] = jnp.broadcast_to(top, (TILE_ROWS, HEAD_SIZE))


def attend_prior(queries, pieces, after):
    return pl.pallas_call(
        prior_kernel,
        grid=(2,),
        in_specs=[pl.BlockSpec((TOKENS, HEAD_COLUMNS), lambda h: (0, h))]
        + [pl.BlockSpec((SIDE, 1, TOKENS, WIDTH), lambda h: (0, h, 0, 0))] * SIDE
        + [pl.BlockSpec(memory_space=pl.ANY)],
        out_specs=[
            pl.BlockSpec((1, HEAD_ROWS, HEAD_SIZE), lambda h: (h, 0, 0)),
            pl.BlockSpec((1, HEAD_ROWS, WIDTH), lambda h: (h, 0, 0)),
        ],
        out_shape=[
            jax.ShapeDtypeStruct((2, HEAD_ROWS, HEAD_SIZE), jnp.float32),
            jax.ShapeDtypeStruct((2, HEAD_ROWS, WIDTH), jnp.float32),
        ],
        scratch_shapes=[pltpu.VMEM((2 * KEYS, WIDTH), jnp.bfloat16)],
        compiler_params=pltpu.CompilerParams(vmem_limit_bytes=24 * MIB),
        cost_estimate=estimate(7),
        name="attend_prior",
    )(queries, *pieces, after)


def span_kernel(partner, visible_ref, q_ref, known_ref, top_in_ref, acc_in_ref, *refs):
    pieces = refs[:SIDE]
    out_ref, top_ref, acc_ref, ext_ref, key_ref = refs[SIDE:]
    queries = query_tiles(q_ref)
    lane = lax.broadcasted_iota(jnp.int32, (TOKENS, HEAD_SIZE), 1)
    stats = jnp.zeros((TOKENS, HEAD_SIZE), out_ref.dtype)
    blocks = SHARDS // PER
    for b in range(blocks):
        slot = (b % 2) * KEYS
        half = slice(slot, slot + KEYS)
        for n in range(PER):
            shard = b * PER + n
            kv = pieces[shard // SIDE][shard % SIDE, 0]
            seen = visible_ref[shard] != 0
            here = slice(slot + n * TOKENS, slot + (n + 1) * TOKENS)
            key_ref[here, :] = jnp.where(seen, kv[:, :HEAD_SIZE], known_ref[0, 0, :, :HEAD_SIZE])
            ext_ref[here, :HEAD_SIZE] = jnp.where(seen, kv[:, HEAD_SIZE:], jnp.zeros_like(kv[:, HEAD_SIZE:]))
            ext_ref[here, HEAD_SIZE:] = jnp.where(
                seen, jnp.ones((TOKENS, HEAD_SIZE), jnp.bfloat16), jnp.zeros((TOKENS, HEAD_SIZE), jnp.bfloat16)
            )
        keys = key_ref[half, :]
        for i in range(TILES):
            here = slice(i * TILE_ROWS, (i + 1) * TILE_ROWS)
            scores = score(queries[i], keys)
            if b == 0 and not partner:
                token = lax.broadcasted_iota(jnp.int32, (TILE_ROWS, TOKENS), 0) % TOKENS
                key = lax.broadcasted_iota(jnp.int32, (TILE_ROWS, TOKENS), 1)
                scores = jnp.concatenate(
                    [jnp.where(key <= token, scores[:, :TOKENS], neg_large), scores[:, TOKENS:]], axis=1
                )
            before = (top_ref[here, :1], acc_ref[here]) if b else (top_in_ref[0, here, :1], acc_in_ref[0, here])
            top, total = absorb(scores, ext_ref[half, :], *before)
            if b < blocks - 1:
                acc_ref[here] = total
                top_ref[here] = jnp.broadcast_to(top, (TILE_ROWS, HEAD_SIZE))
                continue
            out = total[:, :HEAD_SIZE] / total[:, HEAD_SIZE:]
            level = top + jnp.log2(total[:, HEAD_SIZE:])
            for j in range(TILE):
                g = i * TILE + j
                own = slice(j * TOKENS, (j + 1) * TOKENS)
                out_ref[:, g * HEAD_SIZE : (g + 1) * HEAD_SIZE] = out[own].astype(out_ref.dtype)
                parts = split3(level[own]) if partner else (level[own],)
                for part, piece in enumerate(parts):
                    stats = jnp.where(lane == part * GROUP + g, piece, stats)
    out_ref[:, HEAD_COLUMNS:] = stats


def attend_span(partner, visible, queries, head, known, state, pieces):
    out_width = HEAD_COLUMNS + HEAD_SIZE
    dtype = jnp.bfloat16 if partner else jnp.float32
    return pl.pallas_call(
        functools.partial(span_kernel, partner),
        grid_spec=pltpu.PrefetchScalarGridSpec(
            num_scalar_prefetch=1,
            grid=(1,),
            in_specs=[
                pl.BlockSpec((TOKENS, HEAD_COLUMNS), lambda i, *_: (0, head)),
                pl.BlockSpec((1, 1, TOKENS, WIDTH), lambda i, *_: (0, head, 0, 0)),
                pl.BlockSpec((1, HEAD_ROWS, HEAD_SIZE), lambda i, *_: (head, 0, 0)),
                pl.BlockSpec((1, HEAD_ROWS, WIDTH), lambda i, *_: (head, 0, 0)),
            ]
            + [pl.BlockSpec((SIDE, 1, TOKENS, WIDTH), lambda i, *_: (0, head, 0, 0))] * SIDE,
            out_specs=pl.BlockSpec((TOKENS, out_width), lambda i, *_: (0, 0)),
            scratch_shapes=[
                pltpu.VMEM((HEAD_ROWS, HEAD_SIZE), jnp.float32),
                pltpu.VMEM((HEAD_ROWS, WIDTH), jnp.float32),
                pltpu.VMEM((2 * KEYS, WIDTH), jnp.bfloat16),
                pltpu.VMEM((2 * KEYS, HEAD_SIZE), jnp.bfloat16),
            ],
        ),
        out_shape=jax.ShapeDtypeStruct((TOKENS, out_width), dtype),
        compiler_params=pltpu.CompilerParams(vmem_limit_bytes=24 * MIB),
        cost_estimate=estimate(4),
        name="attend_partner" if partner else "attend_own",
    )(visible, queries, known, *state, *pieces)


def combine_kernel(*refs):
    out_ref = refs[4]
    for h in range(2):
        own_ref, other_ref = refs[h], refs[2 + h]
        own_level = own_ref[:, HEAD_COLUMNS:]
        other_parts = other_ref[:, HEAD_COLUMNS:].astype(jnp.float32)
        for g in range(GROUP):
            mine = own_level[:, g : g + 1]
            theirs = (
                other_parts[:, g : g + 1]
                + other_parts[:, GROUP + g : GROUP + g + 1]
                + other_parts[:, 2 * GROUP + g : 2 * GROUP + g + 1]
            )
            peak = jnp.maximum(mine, theirs)
            mine = jnp.exp2(mine - peak)
            theirs = jnp.exp2(theirs - peak)
            whole = mine + theirs
            columns = slice(g * HEAD_SIZE, (g + 1) * HEAD_SIZE)
            mixed = (mine / whole) * own_ref[:, columns] + (theirs / whole) * other_ref[:, columns].astype(
                jnp.float32
            )
            out_ref[:, h * HEAD_COLUMNS + g * HEAD_SIZE : h * HEAD_COLUMNS + (g + 1) * HEAD_SIZE] = mixed.astype(
                jnp.bfloat16
            )


def combine(own, other):
    return pl.pallas_call(
        combine_kernel,
        out_shape=jax.ShapeDtypeStruct((TOKENS, 2 * HEAD_COLUMNS), jnp.bfloat16),
        compiler_params=pltpu.CompilerParams(vmem_limit_bytes=16 * MIB),
        cost_estimate=estimate(1.5),
        name="combine",
    )(*own, *other)


ROW_BLOCK = 4


def decode_kernel(length_ref, live_ref, q_ref, cache_ref, fresh_ref, out_ref):
    first = pl.program_id(0) * ROW_BLOCK
    query_rows = STEPS * GROUP
    cache_size = cache_ref.shape[2]
    fresh_row = lax.broadcasted_iota(jnp.int32, (query_rows, DECODE), 1) // STEPS
    fresh_step = lax.broadcasted_iota(jnp.int32, (query_rows, DECODE), 1) % STEPS
    step = lax.broadcasted_iota(jnp.int32, (query_rows, DECODE), 0) // GROUP
    slot = lax.broadcasted_iota(jnp.int32, (query_rows, cache_size), 1)
    contract = (((1,), (1,)), ((), ()))
    for n in range(ROW_BLOCK):
        row = first + n
        length = length_ref[row]
        live = row < live_ref[0]
        for h in range(2):
            queries = q_ref[n, h]
            cached = lax.dot_general(
                queries, cache_ref[n, h, :, :HEAD_SIZE], contract, preferred_element_type=jnp.float32
            )
            fresh = lax.dot_general(
                queries, fresh_ref[h, :, :HEAD_SIZE], contract, preferred_element_type=jnp.float32
            )
            cached = jnp.where(slot < length, cached, neg_large)
            fresh = jnp.where((fresh_row == row) & (fresh_step <= step), fresh, neg_large)
            top = jnp.maximum(jnp.max(cached, axis=1, keepdims=True), jnp.max(fresh, axis=1, keepdims=True))
            cached = jnp.exp2((cached - top) * LOG2_SCALE)
            fresh = jnp.exp2((fresh - top) * LOG2_SCALE)
            total = jnp.sum(cached, axis=1, keepdims=True) + jnp.sum(fresh, axis=1, keepdims=True)
            out = jnp.dot(
                cached.astype(jnp.bfloat16), cache_ref[n, h, :, HEAD_SIZE:], preferred_element_type=jnp.float32
            ) + jnp.dot(
                fresh.astype(jnp.bfloat16), fresh_ref[h, :, HEAD_SIZE:], preferred_element_type=jnp.float32
            )
            out_ref[n, h] = jnp.where(live, out / total, 0.0).astype(jnp.bfloat16)


def decode_attend(lengths, live, queries, cache, fresh):
    rows, heads, query_rows, _ = queries.shape
    cache_size = cache.shape[2]
    return pl.pallas_call(
        decode_kernel,
        grid_spec=pltpu.PrefetchScalarGridSpec(
            num_scalar_prefetch=2,
            grid=(rows // ROW_BLOCK,),
            in_specs=[
                pl.BlockSpec((ROW_BLOCK, heads, query_rows, HEAD_SIZE), lambda i, *_: (i, 0, 0, 0)),
                pl.BlockSpec((ROW_BLOCK, heads, cache_size, 2 * HEAD_SIZE), lambda i, *_: (i, 0, 0, 0)),
                pl.BlockSpec((heads, DECODE, 2 * HEAD_SIZE), lambda i, *_: (0, 0, 0)),
            ],
            out_specs=pl.BlockSpec((ROW_BLOCK, heads, query_rows, HEAD_SIZE), lambda i, *_: (i, 0, 0, 0)),
        ),
        out_shape=jax.ShapeDtypeStruct(queries.shape, jnp.bfloat16),
        compiler_params=pltpu.CompilerParams(vmem_limit_bytes=16 * MIB),
        cost_estimate=estimate(8),
        name="decode",
    )(lengths, live, queries, cache, fresh)


def pages_kernel(where_ref, *refs):
    pieces = refs[:SIDE]
    out_ref = refs[SIDE]
    for n in range(out_ref.shape[0]):
        dy, dz = where_ref[0, n], where_ref[1, n]
        rows = pl.ds(pl.multiple_of(where_ref[2, n] * BLK, BLK), BLK)
        for h in range(2):
            page = pieces[0][dz, h, rows, :]
            for k in range(1, SIDE):
                page = jnp.where(dy == k, pieces[k][dz, h, rows, :], page)
            out_ref[n, h] = page


def pick_pages(where, pieces):
    count = where.shape[1]
    return pl.pallas_call(
        pages_kernel,
        grid_spec=pltpu.PrefetchScalarGridSpec(
            num_scalar_prefetch=1,
            grid=(1,),
            in_specs=[pl.BlockSpec((SIDE, 2, TOKENS, WIDTH), lambda i, *_: (0, 0, 0, 0))] * SIDE,
            out_specs=pl.BlockSpec((count, 2, BLK, WIDTH), lambda i, *_: (0, 0, 0, 0)),
        ),
        out_shape=jax.ShapeDtypeStruct((count, 2, BLK, WIDTH), jnp.bfloat16),
        compiler_params=pltpu.CompilerParams(vmem_limit_bytes=16 * MIB),
        cost_estimate=estimate(1.5),
        name="pages",
    )(where, *pieces)


def shift(x, dz, dy):
    perm = [
        (z * SIDE + y, ((z + dz) % SIDE) * SIDE + (y + dy) % SIDE) for z in range(SIDE) for y in range(SIDE)
    ]
    return lax.ppermute(x, "ctx", perm)


def swap_pool(x):
    return lax.ppermute(x, "pool", [(0, 1), (1, 0)])


def swap_tp(x, bit):
    return lax.ppermute(x, "tp", [(i, i ^ bit) for i in range(4)])


def ring(x, along_z):
    move = (lambda d: shift(x, d, 0)) if along_z else (lambda d: shift(x, 0, d))
    far = {1: move(1), 3: move(3), 2: move(2)}
    return [x, far[1], far[2], far[3]]


def per_device(
    span_hidden_states,
    span_token_queries,
    earlier_key_values,
    decode_hidden_states,
    decode_token_queries,
    decode_row_cache,
    key_value_weight,
    adapter_down_weight,
    adapter_up_weight,
    prompt_adapter,
    row_adapter_index,
    group_live_rows,
    cached_row_lengths,
    block_target_page,
):
    tp = lax.axis_index("tp")
    ctx = lax.axis_index("ctx")
    pool = lax.axis_index("pool")
    my_z, my_y = ctx // SIDE, ctx % SIDE
    depth = span_hidden_states.shape[1]

    prior = ring(jnp.stack(ring(earlier_key_values, False)), True)

    decode_hidden = decode_hidden_states.reshape(DECODE, depth)

    def partial_kv(bits):
        return project(
            jnp.stack([jnp.bitwise_xor(tp, bit) for bit in bits]).astype(jnp.int32),
            row_adapter_index,
            span_hidden_states,
            decode_hidden,
            key_value_weight,
            adapter_down_weight,
            adapter_up_weight,
            prompt_adapter.reshape(1, TOKENS),
        )

    from_core = swap_tp(partial_kv((1, 3)), 1)
    kept = partial_kv((0, 2))

    def owned(rows):
        from_chip = swap_tp(kept[2:, rows] + from_core[2:, rows], 2)
        return (kept[:2, rows] + from_core[:2, rows] + from_chip).astype(jnp.bfloat16)

    span_kv = owned(slice(0, TOKENS))
    decode_kv = owned(slice(TOKENS, ALL_ROWS))

    column = jnp.stack(ring(span_kv, True))
    planes = ring(column, False)

    queries = decode_token_queries.reshape(ROWS, STEPS, 2, GROUP, HEAD_SIZE)
    queries = jnp.transpose(queries, (0, 2, 1, 3, 4)).reshape(ROWS, 2, STEPS * GROUP, HEAD_SIZE)
    decoded = decode_attend(cached_row_lengths, group_live_rows, queries, decode_row_cache, decode_kv)
    decoded = jnp.transpose(decoded.reshape(ROWS, 2, STEPS, GROUP, HEAD_SIZE), (0, 2, 1, 3, 4))
    decode_attention = decoded.reshape(ROWS, STEPS, 2 * GROUP * HEAD_SIZE)

    partner_queries = swap_pool(span_token_queries)
    own_state = attend_prior(span_token_queries, prior, column)
    partner_state = attend_prior(partner_queries, prior, column)

    pages = TOKENS // BLK
    shard = ctx * 2 + pool
    partner_shard = ctx * 2 + 1 - pool
    page_ids = jnp.concatenate([shard * pages + jnp.arange(pages), partner_shard * pages + jnp.arange(pages)])
    block_ids = jnp.arange(block_target_page.shape[0], dtype=jnp.int32)
    source = jnp.sum(
        jnp.where(block_target_page[None, :] == page_ids[:, None], block_ids[None, :], 0), axis=1
    )
    source_shard = source // pages
    source_ctx = source_shard // 2
    where = jnp.stack(
        [
            jnp.mod(my_y - source_ctx % SIDE, SIDE),
            jnp.mod(my_z - source_ctx // SIDE, SIDE),
            source % pages,
        ]
    ).astype(jnp.int32)
    planes, own_state, partner_state, decode_attention = lax.optimization_barrier(
        (planes, own_state, partner_state, decode_attention)
    )
    found = pick_pages(where, planes)
    found, planes = lax.optimization_barrier((found, planes))
    from_partner = swap_pool(found[pages:])
    mine = (source_shard % 2 == pool)[:pages]
    handoff_pages = jnp.where(mine[:, None, None, None], found[:pages], from_partner)

    far = jnp.arange(SIDE, dtype=jnp.int32)
    shard_z, shard_y = jnp.mod(my_z - far, SIDE), jnp.mod(my_y - far, SIDE)
    place = shard_z[None, :] * SIDE + shard_y[:, None]
    partner_sees = ((place < ctx) | ((place == ctx) & (pool == 0))).astype(jnp.int32).reshape(-1)
    own_sees = (place <= ctx).astype(jnp.int32).reshape(-1)
    other = [
        swap_pool(attend_span(True, partner_sees, partner_queries, h, prior[0], partner_state, planes))
        for h in range(2)
    ]
    own = [attend_span(False, own_sees, span_token_queries, h, prior[0], own_state, planes) for h in range(2)]
    span_attention = combine(own, other)
    return (span_attention, handoff_pages, decode_attention)


def solution(mesh):
    in_specs = (
        P(("ctx", "pool"), "tp"),
        P(("ctx", "pool"), "tp"),
        P("tp", ("ctx", "pool"), None),
        P(("ctx", "pool"), None, "tp"),
        P(("ctx", "pool"), None, "tp"),
        P(("ctx", "pool"), "tp", None, None),
        P("tp", None),
        P("tp", None),
        P(),
        P(("ctx", "pool")),
        P(("ctx", "pool")),
        P(("ctx", "pool")),
        P(("ctx", "pool")),
        P(),
    )
    out_specs = (
        P(("ctx", "pool"), "tp"),
        P(("ctx", "pool"), "tp", None, None),
        P(("ctx", "pool"), None, "tp"),
    )
    return jax.shard_map(
        per_device, mesh=mesh, in_specs=in_specs, out_specs=out_specs, check_vma=False
    )
```

```python
import functools
import math

import jax
import jax.numpy as jnp
from jax import lax
from jax.experimental import pallas as pl
from jax.experimental.pallas import tpu as pltpu
from jax.sharding import PartitionSpec as P

HQ = 64
KEY_VALUE_HEADS = 8
HEAD_SIZE = 128
ADAPTER_RANK = 16
BLK = 16
STEPS = 4
GROUP = HQ // KEY_VALUE_HEADS
SHARDS = 16
SIDE = 4
TOKENS = 128
ROWS = 16
DECODE = ROWS * STEPS
ALL_ROWS = TOKENS + DECODE
LOG2_SCALE = math.log2(math.e) / math.sqrt(HEAD_SIZE)
neg_large = -1e30
MIB = 2**20
WIDTH = 2 * HEAD_SIZE


def estimate(us):
    return pl.CostEstimate(flops=int(us * 1.1e9), bytes_accessed=MIB, transcendentals=0)


def split3(x):
    hi = x.astype(jnp.bfloat16)
    rest = x - hi.astype(jnp.float32)
    mid = rest.astype(jnp.bfloat16)
    low = (rest - mid.astype(jnp.float32)).astype(jnp.bfloat16)
    return hi, mid, low

PROJECT_US, ATTEND_US, DECODE_US = 1, 1, 1


def project_kernel(
    tp_ref, row_adapter_ref, span_ref, decode_ref, weight_ref, down_ref, up_ref, adapter_ref, after_ref, out_ref, rank_ref
):
    hidden = jnp.concatenate([span_ref[...], decode_ref[...].reshape(DECODE, decode_ref.shape[2])], axis=0)

    @pl.when(pl.program_id(0) == 0)
    def _():
        narrow = jnp.dot(hidden, down_ref[...], preferred_element_type=jnp.float32)
        span_owner = jnp.transpose(jnp.broadcast_to(adapter_ref[...], (TOKENS, TOKENS)))
        row = lax.broadcasted_iota(jnp.int32, (DECODE, TOKENS), 0) // STEPS
        decode_owner = jnp.zeros((DECODE, TOKENS), jnp.int32)
        for r in range(ROWS):
            decode_owner = jnp.where(row == r, row_adapter_ref[r], decode_owner)
        owner = jnp.concatenate([span_owner, decode_owner], axis=0)
        column = lax.broadcasted_iota(jnp.int32, (ALL_ROWS, TOKENS), 1) // ADAPTER_RANK
        hi, mid, low = split3(jnp.where(column == owner, narrow, 0.0))
        rank_ref[:, :TOKENS] = hi
        rank_ref[:, TOKENS : 2 * TOKENS] = mid
        rank_ref[:, 2 * TOKENS :] = low

    up = up_ref[...]
    out = jnp.dot(hidden, weight_ref[...], preferred_element_type=jnp.float32) + jnp.dot(
        rank_ref[...], jnp.concatenate([up, up, up], axis=0), preferred_element_type=jnp.float32
    )
    out_ref[0] = out[:, :WIDTH]
    out_ref[1] = out[:, WIDTH:]


def project(first, tp, row_adapter, span, decode, weight, down, up, adapter, after):
    count = 2
    depth = span.shape[1]
    whole = lambda i, *_: (0, 0)
    return pl.pallas_call(
        project_kernel,
        grid_spec=pltpu.PrefetchScalarGridSpec(
            num_scalar_prefetch=2,
            grid=(count,),
            in_specs=[
                pl.BlockSpec((TOKENS, depth), whole),
                pl.BlockSpec((ROWS, STEPS, depth), lambda i, *_: (0, 0, 0)),
                pl.BlockSpec((depth, 2 * WIDTH), lambda i, tp, rows: (0, jnp.bitwise_xor(tp[0], first + 2 * i))),
                pl.BlockSpec((depth, TOKENS), whole),
                pl.BlockSpec((TOKENS, 2 * WIDTH), lambda i, tp, rows: (0, jnp.bitwise_xor(tp[0], first + 2 * i))),
                pl.BlockSpec((1, TOKENS), whole),
                pl.BlockSpec(memory_space=pl.ANY),
            ],
            out_specs=pl.BlockSpec((2, ALL_ROWS, WIDTH), lambda i, *_: (i, 0, 0)),
            scratch_shapes=[pltpu.VMEM((ALL_ROWS, 3 * TOKENS), jnp.bfloat16)],
        ),
        out_shape=jax.ShapeDtypeStruct((2 * count, ALL_ROWS, WIDTH), jnp.float32),
        compiler_params=pltpu.CompilerParams(vmem_limit_bytes=56 * MIB),
        cost_estimate=estimate(PROJECT_US),
        name="project",
    )(tp, row_adapter, span, decode, weight, down, up, adapter, after)


def finish_kernel(kept_ref, core_ref, chip_ref, *refs):
    out_ref = refs[-1]
    out_ref[...] = (kept_ref[...] + core_ref[...] + chip_ref[...]).astype(jnp.bfloat16)


def finish(kept, from_core, from_chip, after):
    heads, rows, width = from_chip.shape
    block = pl.BlockSpec((heads, rows, width), lambda i: (0, 0, 0))
    return pl.pallas_call(
        finish_kernel,
        grid=(1,),
        in_specs=[block] * 3 + [pl.BlockSpec(memory_space=pl.ANY)] * len(after),
        out_specs=block,
        out_shape=jax.ShapeDtypeStruct(from_chip.shape, jnp.bfloat16),
        compiler_params=pltpu.CompilerParams(vmem_limit_bytes=8 * MIB),
        cost_estimate=estimate(0.5),
        name="finish",
    )(kept, from_core, from_chip, *after)


TILE = 2
TILE_ROWS = TILE * TOKENS
TILES = GROUP // TILE
HEAD_ROWS = GROUP * TOKENS
HEAD_COLUMNS = GROUP * HEAD_SIZE


def attend_kernel(blocks, diagonal, has_state, final, partner, visible_ref, q_ref, known_ref, *refs):
    pieces, refs = refs[: blocks[-1][-1][0] + 1], refs[blocks[-1][-1][0] + 1 :]
    if has_state:
        state_ref, refs = refs[0], refs[1:]
    else:
        refs = refs[1:]
    out_ref, top_ref, acc_ref, ext_ref, key_ref = refs
    queries = [
        jnp.concatenate(
            [q_ref[:, (i * TILE + j) * HEAD_SIZE : (i * TILE + j + 1) * HEAD_SIZE] for j in range(TILE)], axis=0
        )
        for i in range(TILES)
    ]
    wide = lax.broadcasted_iota(jnp.int32, (TILE_ROWS, HEAD_SIZE), 1)
    lane = wide[:TOKENS]
    one = jnp.ones((TOKENS, HEAD_SIZE), jnp.bfloat16)
    zero = jnp.zeros((TOKENS, HEAD_SIZE), jnp.bfloat16)
    if final:
        stats = jnp.zeros((TOKENS, HEAD_SIZE), out_ref.dtype)
    start = 0
    for b, shards in enumerate(blocks):
        stop = start + len(shards) * TOKENS
        block = slice(start, stop)
        for n, (piece, index, place) in enumerate(shards):
            kv = pieces[piece][index, 0]
            keys, values, ones = kv[:, :HEAD_SIZE], kv[:, HEAD_SIZE:], one
            if place is not None:
                seen = visible_ref[place] != 0
                keys = jnp.where(seen, keys, known_ref[0, 0, :, :HEAD_SIZE])
                values = jnp.where(seen, values, zero)
                ones = jnp.where(seen, one, zero)
            here = slice(start + n * TOKENS, start + (n + 1) * TOKENS)
            key_ref[here, :] = keys
            ext_ref[here, :HEAD_SIZE] = values
            ext_ref[here, HEAD_SIZE:] = ones
        for i in range(TILES):
            here = slice(i * TILE_ROWS, (i + 1) * TILE_ROWS)
            scores = lax.dot_general(
                queries[i], key_ref[block, :], (((1,), (1,)), ((), ())), preferred_element_type=jnp.float32
            )
            if diagonal is not None and diagonal in shards:
                at = shards.index(diagonal) * TOKENS
                token = lax.broadcasted_iota(jnp.int32, (TILE_ROWS, TOKENS), 0) % TOKENS
                parts = [scores[:, :at]] if at else []
                parts.append(jnp.where(wide <= token, scores[:, at : at + TOKENS], neg_large))
                if at + TOKENS < scores.shape[1]:
                    parts.append(scores[:, at + TOKENS :])
                scores = jnp.concatenate(parts, axis=1)
            top = jnp.max(scores, axis=1, keepdims=True) * LOG2_SCALE
            if b or has_state:
                if b:
                    top_before, before = top_ref[here, :1], acc_ref[here]
                else:
                    top_before = state_ref[0, here, HEAD_SIZE : HEAD_SIZE + 1]
                    total_before = state_ref[0, here, WIDTH - 1 :]
                    before = jnp.concatenate(
                        [state_ref[0, here, :HEAD_SIZE], jnp.broadcast_to(total_before, (TILE_ROWS, HEAD_SIZE))],
                        axis=1,
                    )
                top = jnp.maximum(top_before, top)
            weights = jnp.exp2(scores * LOG2_SCALE - top).astype(jnp.bfloat16)
            total = jnp.dot(weights, ext_ref[block, :], preferred_element_type=jnp.float32)
            if b or has_state:
                total = before * jnp.exp2(top_before - top) + total
            if b < len(blocks) - 1:
                acc_ref[here] = total
                top_ref[here] = jnp.broadcast_to(top, (TILE_ROWS, HEAD_SIZE))
                continue
            if not final:
                out_ref[0, here, :HEAD_SIZE] = total[:, :HEAD_SIZE]
                out_ref[0, here, HEAD_SIZE:] = jnp.where(wide < HEAD_SIZE // 2, top, total[:, HEAD_SIZE:])
                continue
            out = total[:, :HEAD_SIZE] / total[:, HEAD_SIZE:]
            level = top + jnp.log2(total[:, HEAD_SIZE:])
            for j in range(TILE):
                g = i * TILE + j
                own = slice(j * TOKENS, (j + 1) * TOKENS)
                out_ref[0, :, g * HEAD_SIZE : (g + 1) * HEAD_SIZE] = out[own].astype(out_ref.dtype)
                parts = split3(level[own]) if partner else (level[own],)
                for part, piece in enumerate(parts):
                    stats = jnp.where(lane == part * GROUP + g, piece, stats)
        start = stop
    if final:
        out_ref[0, :, HEAD_COLUMNS:] = stats


def attend(visible, queries, known, pieces, blocks, after, heads, diagonal=None, state=None, final=False, partner=False):
    first, count = heads
    head = lambda h: first + h
    shards = sum(len(block) for block in blocks)
    if final:
        out_shape = (count, TOKENS, HEAD_COLUMNS + HEAD_SIZE)
    else:
        out_shape = (count, HEAD_ROWS, WIDTH)
    in_specs = [
        pl.BlockSpec((TOKENS, HEAD_COLUMNS), lambda h, *_: (0, head(h))),
        pl.BlockSpec((1, 1, TOKENS, WIDTH), lambda h, *_: (0, head(h), 0, 0)),
    ] + [pl.BlockSpec((SIDE, 1, TOKENS, WIDTH), lambda h, *_: (0, head(h), 0, 0))] * len(pieces)
    if state is None:
        in_specs.append(pl.BlockSpec(memory_space=pl.ANY))
    else:
        in_specs.append(pl.BlockSpec((1, HEAD_ROWS, WIDTH), lambda h, *_: (head(h), 0, 0)))
    return pl.pallas_call(
        functools.partial(attend_kernel, blocks, diagonal, state is not None, final, partner),
        grid_spec=pltpu.PrefetchScalarGridSpec(
            num_scalar_prefetch=1,
            grid=(count,),
            in_specs=in_specs,
            out_specs=pl.BlockSpec((1,) + out_shape[1:], lambda h, *_: (h, 0, 0)),
            scratch_shapes=[
                pltpu.VMEM((HEAD_ROWS, HEAD_SIZE), jnp.float32),
                pltpu.VMEM((HEAD_ROWS, WIDTH), jnp.float32),
                pltpu.VMEM((shards * TOKENS, WIDTH), jnp.bfloat16),
                pltpu.VMEM((shards * TOKENS, HEAD_SIZE), jnp.bfloat16),
            ],
        ),
        out_shape=jax.ShapeDtypeStruct(out_shape, jnp.bfloat16 if partner and final else jnp.float32),
        compiler_params=pltpu.CompilerParams(vmem_limit_bytes=24 * MIB),
        cost_estimate=estimate(ATTEND_US * count * shards / 16),
        name="attend_last" if final else "attend_first",
    )(visible, queries, known, *pieces, after if state is None else state)


def combine_kernel(*refs):
    own_ref, out_ref = refs[0], refs[3]
    for h in range(2):
        other_ref = refs[1 + h]
        own_level = own_ref[h, :, HEAD_COLUMNS:]
        other_parts = other_ref[0, :, HEAD_COLUMNS:].astype(jnp.float32)
        for g in range(GROUP):
            mine = own_level[:, g : g + 1]
            theirs = (
                other_parts[:, g : g + 1]
                + other_parts[:, GROUP + g : GROUP + g + 1]
                + other_parts[:, 2 * GROUP + g : 2 * GROUP + g + 1]
            )
            peak = jnp.maximum(mine, theirs)
            mine = jnp.exp2(mine - peak)
            theirs = jnp.exp2(theirs - peak)
            whole = mine + theirs
            columns = slice(g * HEAD_SIZE, (g + 1) * HEAD_SIZE)
            mixed = (mine / whole) * own_ref[h, :, columns] + (theirs / whole) * other_ref[0, :, columns].astype(
                jnp.float32
            )
            out_ref[:, h * HEAD_COLUMNS + g * HEAD_SIZE : h * HEAD_COLUMNS + (g + 1) * HEAD_SIZE] = mixed.astype(
                jnp.bfloat16
            )


def combine(own, other):
    return pl.pallas_call(
        combine_kernel,
        out_shape=jax.ShapeDtypeStruct((TOKENS, 2 * HEAD_COLUMNS), jnp.bfloat16),
        compiler_params=pltpu.CompilerParams(vmem_limit_bytes=16 * MIB),
        cost_estimate=estimate(1),
        name="combine",
    )(own, *other)


ROW_BLOCK = 8


def decode_kernel(length_ref, live_ref, q_ref, cache_ref, fresh_ref, after_ref, out_ref):
    first = pl.program_id(0) * ROW_BLOCK
    query_rows = STEPS * GROUP
    rows = ROW_BLOCK * query_rows
    contract = (((1,), (1,)), ((), ()))
    slot = lax.broadcasted_iota(jnp.int32, (query_rows, cache_ref.shape[2]), 1)
    fresh_row = lax.broadcasted_iota(jnp.int32, (rows, DECODE), 1) // STEPS
    fresh_step = lax.broadcasted_iota(jnp.int32, (rows, DECODE), 1) % STEPS
    row = lax.broadcasted_iota(jnp.int32, (rows, DECODE), 0) // query_rows
    step = lax.broadcasted_iota(jnp.int32, (rows, DECODE), 0) % query_rows // GROUP
    fresh_seen = (fresh_row == row + first) & (fresh_step <= step)
    cached, fresh = [], []
    for h in range(2):
        scores = lax.dot_general(
            q_ref[:, h].reshape(rows, HEAD_SIZE),
            fresh_ref[h, :, :HEAD_SIZE],
            contract,
            preferred_element_type=jnp.float32,
        )
        fresh.append(jnp.where(fresh_seen, scores, neg_large))
        for n in range(ROW_BLOCK):
            scores = lax.dot_general(
                q_ref[n, h], cache_ref[n, h, :, :HEAD_SIZE], contract, preferred_element_type=jnp.float32
            )
            cached.append(jnp.where(slot < length_ref[first + n], scores, neg_large))
    cached = jnp.concatenate(cached, axis=0)
    fresh = jnp.concatenate(fresh, axis=0)
    top = jnp.maximum(jnp.max(cached, axis=1, keepdims=True), jnp.max(fresh, axis=1, keepdims=True))
    cached = jnp.exp2((cached - top) * LOG2_SCALE)
    fresh = jnp.exp2((fresh - top) * LOG2_SCALE)
    total = jnp.sum(cached, axis=1, keepdims=True) + jnp.sum(fresh, axis=1, keepdims=True)
    cached = cached.astype(jnp.bfloat16)
    fresh = fresh.astype(jnp.bfloat16)
    for h in range(2):
        of_fresh = jnp.dot(
            fresh[h * rows : (h + 1) * rows], fresh_ref[h, :, HEAD_SIZE:], preferred_element_type=jnp.float32
        )
        for n in range(ROW_BLOCK):
            here = slice(h * rows + n * query_rows, h * rows + (n + 1) * query_rows)
            out = jnp.dot(cached[here], cache_ref[n, h, :, HEAD_SIZE:], preferred_element_type=jnp.float32)
            out = (out + of_fresh[n * query_rows : (n + 1) * query_rows]) / total[here]
            out_ref[n, h] = jnp.where(first + n < live_ref[0], out, 0.0).astype(jnp.bfloat16)


def decode_attend(lengths, live, queries, cache, fresh, after):
    rows, heads, query_rows, _ = queries.shape
    cache_size = cache.shape[2]
    return pl.pallas_call(
        decode_kernel,
        grid_spec=pltpu.PrefetchScalarGridSpec(
            num_scalar_prefetch=2,
            grid=(rows // ROW_BLOCK,),
            in_specs=[
                pl.BlockSpec((ROW_BLOCK, heads, query_rows, HEAD_SIZE), lambda i, *_: (i, 0, 0, 0)),
                pl.BlockSpec((ROW_BLOCK, heads, cache_size, 2 * HEAD_SIZE), lambda i, *_: (i, 0, 0, 0)),
                pl.BlockSpec((heads, DECODE, 2 * HEAD_SIZE), lambda i, *_: (0, 0, 0)),
                pl.BlockSpec(memory_space=pl.ANY),
            ],
            out_specs=pl.BlockSpec((ROW_BLOCK, heads, query_rows, HEAD_SIZE), lambda i, *_: (i, 0, 0, 0)),
        ),
        out_shape=jax.ShapeDtypeStruct(queries.shape, jnp.bfloat16),
        compiler_params=pltpu.CompilerParams(vmem_limit_bytes=24 * MIB),
        cost_estimate=estimate(DECODE_US),
        name="decode",
    )(lengths, live, queries, cache, fresh, after)


def pages_kernel(where_ref, *refs):
    pieces = refs[:SIDE]
    out_ref = refs[SIDE]
    for n in range(out_ref.shape[0]):
        dz, dy = where_ref[0, n], where_ref[1, n]
        rows = pl.ds(pl.multiple_of(where_ref[2, n] * BLK, BLK), BLK)
        for h in range(2):
            page = pieces[0][dy, h, rows, :]
            for k in range(1, SIDE):
                page = jnp.where(dz == k, pieces[k][dy, h, rows, :], page)
            out_ref[n, h] = page


def pick_pages(where, pieces):
    count = where.shape[1]
    return pl.pallas_call(
        pages_kernel,
        grid_spec=pltpu.PrefetchScalarGridSpec(
            num_scalar_prefetch=1,
            grid=(1,),
            in_specs=[pl.BlockSpec((SIDE, 2, TOKENS, WIDTH), lambda i, *_: (0, 0, 0, 0))] * SIDE,
            out_specs=pl.BlockSpec((count, 2, BLK, WIDTH), lambda i, *_: (0, 0, 0, 0)),
        ),
        out_shape=jax.ShapeDtypeStruct((count, 2, BLK, WIDTH), jnp.bfloat16),
        compiler_params=pltpu.CompilerParams(vmem_limit_bytes=16 * MIB),
        cost_estimate=estimate(1.5),
        name="pages",
    )(where, *pieces)


def shift(x, dz, dy):
    perm = [
        (z * SIDE + y, ((z + dz) % SIDE) * SIDE + (y + dy) % SIDE) for z in range(SIDE) for y in range(SIDE)
    ]
    return lax.ppermute(x, "ctx", perm)


def swap_pool(x):
    return lax.ppermute(x, "pool", [(0, 1), (1, 0)])


def swap_tp(x, bit):
    return lax.ppermute(x, "tp", [(i, i ^ bit) for i in range(4)])


def ring(x, along_z):
    move = (lambda d: shift(x, d, 0)) if along_z else (lambda d: shift(x, 0, d))
    far = {1: move(1), 3: move(3), 2: move(2)}
    return [x, far[1], far[2], far[3]]


def per_device(
    span_hidden_states,
    span_token_queries,
    earlier_key_values,
    decode_hidden_states,
    decode_token_queries,
    decode_row_cache,
    key_value_weight,
    adapter_down_weight,
    adapter_up_weight,
    prompt_adapter,
    row_adapter_index,
    group_live_rows,
    cached_row_lengths,
    block_target_page,
):
    tp = lax.axis_index("tp")
    ctx = lax.axis_index("ctx")
    pool = lax.axis_index("pool")
    my_z, my_y = ctx // SIDE, ctx % SIDE

    prior = ring(jnp.stack(ring(earlier_key_values, False)), True)

    def partial_kv(first, after):
        return project(
            first,
            tp.astype(jnp.int32).reshape(1),
            row_adapter_index,
            span_hidden_states,
            decode_hidden_states,
            key_value_weight,
            adapter_down_weight,
            adapter_up_weight,
            prompt_adapter.reshape(1, TOKENS),
            after,
        )

    from_core = swap_tp(partial_kv(1, row_adapter_index), 1)
    kept = partial_kv(0, prior[0])

    def from_chip(rows):
        return swap_tp(kept[2:, rows] + from_core[2:, rows], 2)

    span_rows, decode_rows = slice(0, TOKENS), slice(TOKENS, ALL_ROWS)
    span_kv = finish(kept, from_core, from_chip(span_rows), (prior[1], prior[3]))
    decode_kv = (kept[:2, decode_rows] + from_core[:2, decode_rows] + from_chip(decode_rows)).astype(jnp.bfloat16)

    column = jnp.stack(ring(span_kv, False))
    planes = ring(column, True)

    queries = decode_token_queries.reshape(ROWS, STEPS, 2, GROUP, HEAD_SIZE)
    queries = jnp.transpose(queries, (0, 2, 1, 3, 4)).reshape(ROWS, 2, STEPS * GROUP, HEAD_SIZE)
    decoded = decode_attend(cached_row_lengths, group_live_rows, queries, decode_row_cache, decode_kv, prior[2])
    decoded = jnp.transpose(decoded.reshape(ROWS, 2, STEPS, GROUP, HEAD_SIZE), (0, 2, 1, 3, 4))
    decode_attention = decoded.reshape(ROWS, STEPS, 2 * GROUP * HEAD_SIZE)

    far = jnp.arange(SIDE, dtype=jnp.int32)
    shard_z, shard_y = jnp.mod(my_z - far, SIDE), jnp.mod(my_y - far, SIDE)
    place = shard_z[:, None] * SIDE + shard_y[None, :]
    partner_sees = ((place < ctx) | ((place == ctx) & (pool == 0))).astype(jnp.int32).reshape(-1)
    own_sees = (place <= ctx).astype(jnp.int32).reshape(-1)
    earlier = [(p, k, None) for p in range(SIDE) for k in range(SIDE)]
    first_blocks = (tuple(earlier[:8]), tuple(earlier[8:]), tuple((SIDE, k, k) for k in range(SIDE)))
    others = [(p, k, (p + 1) * SIDE + k) for p in range(SIDE - 1) for k in range(SIDE)]
    last_blocks = (tuple(others[:6]), tuple(others[6:]))
    both = (0, 2)
    first_pieces = prior + [column]
    partner_queries = swap_pool(span_token_queries)
    own_state = attend(
        own_sees, span_token_queries, prior[0], first_pieces, first_blocks, column, both, diagonal=(SIDE, 0, 0)
    )
    partner_state = attend(partner_sees, partner_queries, prior[0], first_pieces, first_blocks, column, both)

    pages = TOKENS // BLK
    shard = ctx * 2 + pool
    partner_shard = ctx * 2 + 1 - pool
    page_ids = jnp.concatenate([shard * pages + jnp.arange(pages), partner_shard * pages + jnp.arange(pages)])
    block_ids = jnp.arange(block_target_page.shape[0], dtype=jnp.int32)
    source = jnp.sum(
        jnp.where(block_target_page[None, :] == page_ids[:, None], block_ids[None, :], 0), axis=1
    )
    source_shard = source // pages
    source_ctx = source_shard // 2
    where = jnp.stack(
        [
            jnp.mod(my_z - source_ctx // SIDE, SIDE),
            jnp.mod(my_y - source_ctx % SIDE, SIDE),
            source % pages,
        ]
    ).astype(jnp.int32)
    found = pick_pages(where, planes)
    from_partner = swap_pool(found[pages:])
    mine = (source_shard % 2 == pool)[:pages]
    handoff_pages = jnp.where(mine[:, None, None, None], found[:pages], from_partner)

    other = [
        swap_pool(
            attend(
                partner_sees,
                partner_queries,
                prior[0],
                planes[1:],
                last_blocks,
                None,
                (h, 1),
                state=partner_state,
                final=True,
                partner=True,
            )
        )
        for h in range(2)
    ]
    own = attend(
        own_sees, span_token_queries, prior[0], planes[1:], last_blocks, None, both, state=own_state, final=True
    )
    span_attention = combine(own, other)
    return (span_attention, handoff_pages, decode_attention)


def solution(mesh):
    in_specs = (
        P(("ctx", "pool"), "tp"),
        P(("ctx", "pool"), "tp"),
        P("tp", ("ctx", "pool"), None),
        P(("ctx", "pool"), None, "tp"),
        P(("ctx", "pool"), None, "tp"),
        P(("ctx", "pool"), "tp", None, None),
        P("tp", None),
        P("tp", None),
        P(),
        P(("ctx", "pool")),
        P(("ctx", "pool")),
        P(("ctx", "pool")),
        P(("ctx", "pool")),
        P(),
    )
    out_specs = (
        P(("ctx", "pool"), "tp"),
        P(("ctx", "pool"), "tp", None, None),
        P(("ctx", "pool"), None, "tp"),
    )
    return jax.shard_map(
        per_device, mesh=mesh, in_specs=in_specs, out_specs=out_specs, check_vma=False
    )
```

```python
import functools
import math

import jax
import jax.numpy as jnp
from jax import lax
from jax.experimental import pallas as pl
from jax.experimental.pallas import tpu as pltpu
from jax.sharding import PartitionSpec as P

HQ = 64
KEY_VALUE_HEADS = 8
HEAD_SIZE = 128
ADAPTER_RANK = 16
BLK = 16
STEPS = 4
GROUP = HQ // KEY_VALUE_HEADS
SHARDS = 16
SIDE = 4
TOKENS = 128
ROWS = 16
DECODE = ROWS * STEPS
ALL_ROWS = TOKENS + DECODE
LOG2_SCALE = math.log2(math.e) / math.sqrt(HEAD_SIZE)
neg_large = -1e30
MIB = 2**20
WIDTH = 2 * HEAD_SIZE


def estimate(us):
    return pl.CostEstimate(flops=int(us * 1.1e9), bytes_accessed=MIB, transcendentals=0)


def split3(x):
    hi = x.astype(jnp.bfloat16)
    rest = x - hi.astype(jnp.float32)
    mid = rest.astype(jnp.bfloat16)
    low = (rest - mid.astype(jnp.float32)).astype(jnp.bfloat16)
    return hi, mid, low

PROJECT_US, ATTEND_US, DECODE_US = 1, 1, 1


def project_kernel(
    tp_ref, row_adapter_ref, span_ref, decode_ref, weight_ref, down_ref, up_ref, adapter_ref, after_ref, out_ref, rank_ref
):
    hidden = jnp.concatenate([span_ref[...], decode_ref[...].reshape(DECODE, decode_ref.shape[2])], axis=0)

    @pl.when(pl.program_id(0) == 0)
    def _():
        narrow = jnp.dot(hidden, down_ref[...], preferred_element_type=jnp.float32)
        span_owner = jnp.transpose(jnp.broadcast_to(adapter_ref[...], (TOKENS, TOKENS)))
        row = lax.broadcasted_iota(jnp.int32, (DECODE, TOKENS), 0) // STEPS
        decode_owner = jnp.zeros((DECODE, TOKENS), jnp.int32)
        for r in range(ROWS):
            decode_owner = jnp.where(row == r, row_adapter_ref[r], decode_owner)
        owner = jnp.concatenate([span_owner, decode_owner], axis=0)
        column = lax.broadcasted_iota(jnp.int32, (ALL_ROWS, TOKENS), 1) // ADAPTER_RANK
        hi, mid, low = split3(jnp.where(column == owner, narrow, 0.0))
        rank_ref[:, :TOKENS] = hi
        rank_ref[:, TOKENS : 2 * TOKENS] = mid
        rank_ref[:, 2 * TOKENS :] = low

    up = up_ref[...]
    out = jnp.dot(hidden, weight_ref[...], preferred_element_type=jnp.float32) + jnp.dot(
        rank_ref[...], jnp.concatenate([up, up, up], axis=0), preferred_element_type=jnp.float32
    )
    out_ref[0] = out[:, :WIDTH]
    out_ref[1] = out[:, WIDTH:]


def project(first, tp, row_adapter, span, decode, weight, down, up, adapter, after):
    count = 2
    depth = span.shape[1]
    whole = lambda i, *_: (0, 0)
    return pl.pallas_call(
        project_kernel,
        grid_spec=pltpu.PrefetchScalarGridSpec(
            num_scalar_prefetch=2,
            grid=(count,),
            in_specs=[
                pl.BlockSpec((TOKENS, depth), whole),
                pl.BlockSpec((ROWS, STEPS, depth), lambda i, *_: (0, 0, 0)),
                pl.BlockSpec((depth, 2 * WIDTH), lambda i, tp, rows: (0, jnp.bitwise_xor(tp[0], first + 2 * i))),
                pl.BlockSpec((depth, TOKENS), whole),
                pl.BlockSpec((TOKENS, 2 * WIDTH), lambda i, tp, rows: (0, jnp.bitwise_xor(tp[0], first + 2 * i))),
                pl.BlockSpec((1, TOKENS), whole),
                pl.BlockSpec(memory_space=pl.ANY),
            ],
            out_specs=pl.BlockSpec((2, ALL_ROWS, WIDTH), lambda i, *_: (i, 0, 0)),
            scratch_shapes=[pltpu.VMEM((ALL_ROWS, 3 * TOKENS), jnp.bfloat16)],
        ),
        out_shape=jax.ShapeDtypeStruct((2 * count, ALL_ROWS, WIDTH), jnp.float32),
        compiler_params=pltpu.CompilerParams(vmem_limit_bytes=56 * MIB),
        cost_estimate=estimate(PROJECT_US),
        name="project",
    )(tp, row_adapter, span, decode, weight, down, up, adapter, after)


def finish_kernel(kept_ref, core_ref, chip_ref, *refs):
    out_ref = refs[-1]
    out_ref[...] = (kept_ref[...] + core_ref[...] + chip_ref[...]).astype(jnp.bfloat16)


def finish(kept, from_core, from_chip, after):
    heads, rows, width = from_chip.shape
    block = pl.BlockSpec((heads, rows, width), lambda i: (0, 0, 0))
    return pl.pallas_call(
        finish_kernel,
        grid=(1,),
        in_specs=[block] * 3 + [pl.BlockSpec(memory_space=pl.ANY)] * len(after),
        out_specs=block,
        out_shape=jax.ShapeDtypeStruct(from_chip.shape, jnp.bfloat16),
        compiler_params=pltpu.CompilerParams(vmem_limit_bytes=8 * MIB),
        cost_estimate=estimate(0.5),
        name="finish",
    )(kept, from_core, from_chip, *after)


TILE = 2
TILE_ROWS = TILE * TOKENS
TILES = GROUP // TILE
HEAD_ROWS = GROUP * TOKENS
HEAD_COLUMNS = GROUP * HEAD_SIZE


def attend_kernel(blocks, diagonal, has_state, final, partner, visible_ref, q_ref, known_ref, *refs):
    pieces, refs = refs[: blocks[-1][-1][0] + 1], refs[blocks[-1][-1][0] + 1 :]
    if has_state:
        state_ref, refs = refs[0], refs[1:]
    else:
        refs = refs[1:]
    out_ref, top_ref, acc_ref, ext_ref, key_ref = refs
    queries = [
        jnp.concatenate(
            [q_ref[:, (i * TILE + j) * HEAD_SIZE : (i * TILE + j + 1) * HEAD_SIZE] for j in range(TILE)], axis=0
        )
        for i in range(TILES)
    ]
    wide = lax.broadcasted_iota(jnp.int32, (TILE_ROWS, HEAD_SIZE), 1)
    lane = wide[:TOKENS]
    one = jnp.ones((TOKENS, HEAD_SIZE), jnp.bfloat16)
    zero = jnp.zeros((TOKENS, HEAD_SIZE), jnp.bfloat16)
    if final:
        stats = jnp.zeros((TOKENS, HEAD_SIZE), out_ref.dtype)
    start = 0
    for b, shards in enumerate(blocks):
        stop = start + len(shards) * TOKENS
        block = slice(start, stop)
        for n, (piece, index, place) in enumerate(shards):
            kv = pieces[piece][index, 0]
            keys, values, ones = kv[:, :HEAD_SIZE], kv[:, HEAD_SIZE:], one
            if place is not None:
                seen = visible_ref[place] != 0
                keys = jnp.where(seen, keys, known_ref[0, 0, :, :HEAD_SIZE])
                values = jnp.where(seen, values, zero)
                ones = jnp.where(seen, one, zero)
            here = slice(start + n * TOKENS, start + (n + 1) * TOKENS)
            key_ref[here, :] = keys
            ext_ref[here, :HEAD_SIZE] = values
            ext_ref[here, HEAD_SIZE:] = ones
        for i in range(TILES):
            here = slice(i * TILE_ROWS, (i + 1) * TILE_ROWS)
            scores = lax.dot_general(
                queries[i], key_ref[block, :], (((1,), (1,)), ((), ())), preferred_element_type=jnp.float32
            )
            if diagonal is not None and diagonal in shards:
                at = shards.index(diagonal) * TOKENS
                token = lax.broadcasted_iota(jnp.int32, (TILE_ROWS, TOKENS), 0) % TOKENS
                parts = [scores[:, :at]] if at else []
                parts.append(jnp.where(wide <= token, scores[:, at : at + TOKENS], neg_large))
                if at + TOKENS < scores.shape[1]:
                    parts.append(scores[:, at + TOKENS :])
                scores = jnp.concatenate(parts, axis=1)
            top = jnp.max(scores, axis=1, keepdims=True) * LOG2_SCALE
            if b or has_state:
                if b:
                    top_before, before = top_ref[here, :1], acc_ref[here]
                else:
                    top_before = state_ref[0, here, HEAD_SIZE : HEAD_SIZE + 1]
                    total_before = state_ref[0, here, WIDTH - 1 :]
                    before = jnp.concatenate(
                        [state_ref[0, here, :HEAD_SIZE], jnp.broadcast_to(total_before, (TILE_ROWS, HEAD_SIZE))],
                        axis=1,
                    )
                top = jnp.maximum(top_before, top)
            weights = jnp.exp2(scores * LOG2_SCALE - top).astype(jnp.bfloat16)
            total = jnp.dot(weights, ext_ref[block, :], preferred_element_type=jnp.float32)
            if b or has_state:
                total = before * jnp.exp2(top_before - top) + total
            if b < len(blocks) - 1:
                acc_ref[here] = total
                top_ref[here] = jnp.broadcast_to(top, (TILE_ROWS, HEAD_SIZE))
                continue
            if not final:
                out_ref[0, here, :HEAD_SIZE] = total[:, :HEAD_SIZE]
                out_ref[0, here, HEAD_SIZE:] = jnp.where(wide < HEAD_SIZE // 2, top, total[:, HEAD_SIZE:])
                continue
            out = total[:, :HEAD_SIZE] / total[:, HEAD_SIZE:]
            level = top + jnp.log2(total[:, HEAD_SIZE:])
            for j in range(TILE):
                g = i * TILE + j
                own = slice(j * TOKENS, (j + 1) * TOKENS)
                out_ref[0, :, g * HEAD_SIZE : (g + 1) * HEAD_SIZE] = out[own].astype(out_ref.dtype)
                parts = split3(level[own]) if partner else (level[own],)
                for part, piece in enumerate(parts):
                    stats = jnp.where(lane == part * GROUP + g, piece, stats)
        start = stop
    if final:
        out_ref[0, :, HEAD_COLUMNS:] = stats


def attend(visible, queries, known, pieces, blocks, after, heads, diagonal=None, state=None, final=False, partner=False):
    first, count = heads
    head = lambda h: first + h
    shards = sum(len(block) for block in blocks)
    if final:
        out_shape = (count, TOKENS, HEAD_COLUMNS + HEAD_SIZE)
    else:
        out_shape = (count, HEAD_ROWS, WIDTH)
    in_specs = [
        pl.BlockSpec((TOKENS, HEAD_COLUMNS), lambda h, *_: (0, head(h))),
        pl.BlockSpec((1, 1, TOKENS, WIDTH), lambda h, *_: (0, head(h), 0, 0)),
    ] + [pl.BlockSpec((SIDE, 1, TOKENS, WIDTH), lambda h, *_: (0, head(h), 0, 0))] * len(pieces)
    if state is None:
        in_specs.append(pl.BlockSpec(memory_space=pl.ANY))
    else:
        in_specs.append(pl.BlockSpec((1, HEAD_ROWS, WIDTH), lambda h, *_: (head(h), 0, 0)))
    return pl.pallas_call(
        functools.partial(attend_kernel, blocks, diagonal, state is not None, final, partner),
        grid_spec=pltpu.PrefetchScalarGridSpec(
            num_scalar_prefetch=1,
            grid=(count,),
            in_specs=in_specs,
            out_specs=pl.BlockSpec((1,) + out_shape[1:], lambda h, *_: (h, 0, 0)),
            scratch_shapes=[
                pltpu.VMEM((HEAD_ROWS, HEAD_SIZE), jnp.float32),
                pltpu.VMEM((HEAD_ROWS, WIDTH), jnp.float32),
                pltpu.VMEM((shards * TOKENS, WIDTH), jnp.bfloat16),
                pltpu.VMEM((shards * TOKENS, HEAD_SIZE), jnp.bfloat16),
            ],
        ),
        out_shape=jax.ShapeDtypeStruct(out_shape, jnp.bfloat16 if partner and final else jnp.float32),
        compiler_params=pltpu.CompilerParams(vmem_limit_bytes=24 * MIB),
        cost_estimate=estimate(ATTEND_US * count * shards / 16),
        name="attend_last" if final else "attend_first",
    )(visible, queries, known, *pieces, after if state is None else state)


def combine_kernel(*refs):
    own_ref, out_ref = refs[0], refs[3]
    for h in range(2):
        other_ref = refs[1 + h]
        own_level = own_ref[h, :, HEAD_COLUMNS:]
        other_parts = other_ref[0, :, HEAD_COLUMNS:].astype(jnp.float32)
        for g in range(GROUP):
            mine = own_level[:, g : g + 1]
            theirs = (
                other_parts[:, g : g + 1]
                + other_parts[:, GROUP + g : GROUP + g + 1]
                + other_parts[:, 2 * GROUP + g : 2 * GROUP + g + 1]
            )
            peak = jnp.maximum(mine, theirs)
            mine = jnp.exp2(mine - peak)
            theirs = jnp.exp2(theirs - peak)
            whole = mine + theirs
            columns = slice(g * HEAD_SIZE, (g + 1) * HEAD_SIZE)
            mixed = (mine / whole) * own_ref[h, :, columns] + (theirs / whole) * other_ref[0, :, columns].astype(
                jnp.float32
            )
            out_ref[:, h * HEAD_COLUMNS + g * HEAD_SIZE : h * HEAD_COLUMNS + (g + 1) * HEAD_SIZE] = mixed.astype(
                jnp.bfloat16
            )


def combine(own, other):
    return pl.pallas_call(
        combine_kernel,
        out_shape=jax.ShapeDtypeStruct((TOKENS, 2 * HEAD_COLUMNS), jnp.bfloat16),
        compiler_params=pltpu.CompilerParams(vmem_limit_bytes=16 * MIB),
        cost_estimate=estimate(1),
        name="combine",
    )(own, *other)


ROW_BLOCK = 8


def decode_kernel(length_ref, live_ref, q_ref, cache_ref, fresh_ref, after_ref, out_ref):
    first = pl.program_id(0) * ROW_BLOCK
    query_rows = STEPS * GROUP
    rows = ROW_BLOCK * query_rows
    contract = (((1,), (1,)), ((), ()))
    slot = lax.broadcasted_iota(jnp.int32, (query_rows, cache_ref.shape[2]), 1)
    fresh_row = lax.broadcasted_iota(jnp.int32, (rows, DECODE), 1) // STEPS
    fresh_step = lax.broadcasted_iota(jnp.int32, (rows, DECODE), 1) % STEPS
    row = lax.broadcasted_iota(jnp.int32, (rows, DECODE), 0) // query_rows
    step = lax.broadcasted_iota(jnp.int32, (rows, DECODE), 0) % query_rows // GROUP
    fresh_seen = (fresh_row == row + first) & (fresh_step <= step)
    cached, fresh = [], []
    for h in range(2):
        scores = lax.dot_general(
            q_ref[:, h].reshape(rows, HEAD_SIZE),
            fresh_ref[h, :, :HEAD_SIZE],
            contract,
            preferred_element_type=jnp.float32,
        )
        fresh.append(jnp.where(fresh_seen, scores, neg_large))
        for n in range(ROW_BLOCK):
            scores = lax.dot_general(
                q_ref[n, h], cache_ref[n, h, :, :HEAD_SIZE], contract, preferred_element_type=jnp.float32
            )
            cached.append(jnp.where(slot < length_ref[first + n], scores, neg_large))
    cached = jnp.concatenate(cached, axis=0)
    fresh = jnp.concatenate(fresh, axis=0)
    top = jnp.maximum(jnp.max(cached, axis=1, keepdims=True), jnp.max(fresh, axis=1, keepdims=True))
    cached = jnp.exp2((cached - top) * LOG2_SCALE)
    fresh = jnp.exp2((fresh - top) * LOG2_SCALE)
    total = jnp.sum(cached, axis=1, keepdims=True) + jnp.sum(fresh, axis=1, keepdims=True)
    cached = cached.astype(jnp.bfloat16)
    fresh = fresh.astype(jnp.bfloat16)
    for h in range(2):
        of_fresh = jnp.dot(
            fresh[h * rows : (h + 1) * rows], fresh_ref[h, :, HEAD_SIZE:], preferred_element_type=jnp.float32
        )
        for n in range(ROW_BLOCK):
            here = slice(h * rows + n * query_rows, h * rows + (n + 1) * query_rows)
            out = jnp.dot(cached[here], cache_ref[n, h, :, HEAD_SIZE:], preferred_element_type=jnp.float32)
            out = (out + of_fresh[n * query_rows : (n + 1) * query_rows]) / total[here]
            out_ref[n, h] = jnp.where(first + n < live_ref[0], out, 0.0).astype(jnp.bfloat16)


def decode_attend(lengths, live, queries, cache, fresh, after):
    rows, heads, query_rows, _ = queries.shape
    cache_size = cache.shape[2]
    return pl.pallas_call(
        decode_kernel,
        grid_spec=pltpu.PrefetchScalarGridSpec(
            num_scalar_prefetch=2,
            grid=(rows // ROW_BLOCK,),
            in_specs=[
                pl.BlockSpec((ROW_BLOCK, heads, query_rows, HEAD_SIZE), lambda i, *_: (i, 0, 0, 0)),
                pl.BlockSpec((ROW_BLOCK, heads, cache_size, 2 * HEAD_SIZE), lambda i, *_: (i, 0, 0, 0)),
                pl.BlockSpec((heads, DECODE, 2 * HEAD_SIZE), lambda i, *_: (0, 0, 0)),
                pl.BlockSpec(memory_space=pl.ANY),
            ],
            out_specs=pl.BlockSpec((ROW_BLOCK, heads, query_rows, HEAD_SIZE), lambda i, *_: (i, 0, 0, 0)),
        ),
        out_shape=jax.ShapeDtypeStruct(queries.shape, jnp.bfloat16),
        compiler_params=pltpu.CompilerParams(vmem_limit_bytes=24 * MIB),
        cost_estimate=estimate(DECODE_US),
        name="decode",
    )(lengths, live, queries, cache, fresh, after)


def pages_kernel(where_ref, *refs):
    pieces = refs[:SIDE]
    out_ref = refs[SIDE]
    for n in range(out_ref.shape[0]):
        dz, dy = where_ref[0, n], where_ref[1, n]
        rows = pl.ds(pl.multiple_of(where_ref[2, n] * BLK, BLK), BLK)
        for h in range(2):
            page = pieces[0][dy, h, rows, :]
            for k in range(1, SIDE):
                page = jnp.where(dz == k, pieces[k][dy, h, rows, :], page)
            out_ref[n, h] = page


def pick_pages(where, pieces):
    count = where.shape[1]
    return pl.pallas_call(
        pages_kernel,
        grid_spec=pltpu.PrefetchScalarGridSpec(
            num_scalar_prefetch=1,
            grid=(1,),
            in_specs=[pl.BlockSpec((SIDE, 2, TOKENS, WIDTH), lambda i, *_: (0, 0, 0, 0))] * SIDE,
            out_specs=pl.BlockSpec((count, 2, BLK, WIDTH), lambda i, *_: (0, 0, 0, 0)),
        ),
        out_shape=jax.ShapeDtypeStruct((count, 2, BLK, WIDTH), jnp.bfloat16),
        compiler_params=pltpu.CompilerParams(vmem_limit_bytes=16 * MIB),
        cost_estimate=estimate(1.5),
        name="pages",
    )(where, *pieces)


def shift(x, dz, dy):
    perm = [
        (z * SIDE + y, ((z + dz) % SIDE) * SIDE + (y + dy) % SIDE) for z in range(SIDE) for y in range(SIDE)
    ]
    return lax.ppermute(x, "ctx", perm)


def swap_pool(x):
    return lax.ppermute(x, "pool", [(0, 1), (1, 0)])


def swap_tp(x, bit):
    return lax.ppermute(x, "tp", [(i, i ^ bit) for i in range(4)])


def ring(x, along_z):
    move = (lambda d: shift(x, d, 0)) if along_z else (lambda d: shift(x, 0, d))
    far = {1: move(1), 3: move(3), 2: move(2)}
    return [x, far[1], far[2], far[3]]


def per_device(
    span_hidden_states,
    span_token_queries,
    earlier_key_values,
    decode_hidden_states,
    decode_token_queries,
    decode_row_cache,
    key_value_weight,
    adapter_down_weight,
    adapter_up_weight,
    prompt_adapter,
    row_adapter_index,
    group_live_rows,
    cached_row_lengths,
    block_target_page,
):
    tp = lax.axis_index("tp")
    ctx = lax.axis_index("ctx")
    pool = lax.axis_index("pool")
    my_z, my_y = ctx // SIDE, ctx % SIDE

    prior = ring(jnp.stack(ring(earlier_key_values, False)), True)

    def partial_kv(first, after):
        return project(
            first,
            tp.astype(jnp.int32).reshape(1),
            row_adapter_index,
            span_hidden_states,
            decode_hidden_states,
            key_value_weight,
            adapter_down_weight,
            adapter_up_weight,
            prompt_adapter.reshape(1, TOKENS),
            after,
        )

    from_core = swap_tp(partial_kv(1, row_adapter_index), 1)
    kept = partial_kv(0, row_adapter_index)

    def from_chip(rows):
        return swap_tp(kept[2:, rows] + from_core[2:, rows], 2)

    span_rows, decode_rows = slice(0, TOKENS), slice(TOKENS, ALL_ROWS)
    span_kv = finish(kept, from_core, from_chip(span_rows), ())
    decode_kv = (kept[:2, decode_rows] + from_core[:2, decode_rows] + from_chip(decode_rows)).astype(jnp.bfloat16)

    column = jnp.stack(ring(span_kv, False))
    planes = ring(column, True)

    queries = decode_token_queries.reshape(ROWS, STEPS, 2, GROUP, HEAD_SIZE)
    queries = jnp.transpose(queries, (0, 2, 1, 3, 4)).reshape(ROWS, 2, STEPS * GROUP, HEAD_SIZE)
    decoded = decode_attend(cached_row_lengths, group_live_rows, queries, decode_row_cache, decode_kv, row_adapter_index)
    decoded = jnp.transpose(decoded.reshape(ROWS, 2, STEPS, GROUP, HEAD_SIZE), (0, 2, 1, 3, 4))
    decode_attention = decoded.reshape(ROWS, STEPS, 2 * GROUP * HEAD_SIZE)

    far = jnp.arange(SIDE, dtype=jnp.int32)
    shard_z, shard_y = jnp.mod(my_z - far, SIDE), jnp.mod(my_y - far, SIDE)
    place = shard_z[:, None] * SIDE + shard_y[None, :]
    partner_sees = ((place < ctx) | ((place == ctx) & (pool == 0))).astype(jnp.int32).reshape(-1)
    own_sees = (place <= ctx).astype(jnp.int32).reshape(-1)
    earlier = [(p, k, None) for p in range(SIDE) for k in range(SIDE)]
    seen_first = earlier + [(SIDE, k, k) for k in range(SIDE)]
    first_blocks = (tuple(seen_first[:10]), tuple(seen_first[10:]))
    others = [(p, k, (p + 1) * SIDE + k) for p in range(SIDE - 1) for k in range(SIDE)]
    last_blocks = (tuple(others),)
    both = (0, 2)
    first_pieces = prior + [column]
    partner_queries = swap_pool(span_token_queries)
    own_state = attend(
        own_sees, span_token_queries, prior[0], first_pieces, first_blocks, column, both, diagonal=(SIDE, 0, 0)
    )
    partner_state = attend(partner_sees, partner_queries, prior[0], first_pieces, first_blocks, column, both)

    pages = TOKENS // BLK
    shard = ctx * 2 + pool
    partner_shard = ctx * 2 + 1 - pool
    page_ids = jnp.concatenate([shard * pages + jnp.arange(pages), partner_shard * pages + jnp.arange(pages)])
    block_ids = jnp.arange(block_target_page.shape[0], dtype=jnp.int32)
    source = jnp.sum(
        jnp.where(block_target_page[None, :] == page_ids[:, None], block_ids[None, :], 0), axis=1
    )
    source_shard = source // pages
    source_ctx = source_shard // 2
    where = jnp.stack(
        [
            jnp.mod(my_z - source_ctx // SIDE, SIDE),
            jnp.mod(my_y - source_ctx % SIDE, SIDE),
            source % pages,
        ]
    ).astype(jnp.int32)
    found = pick_pages(where, planes)
    from_partner = swap_pool(found[pages:])
    mine = (source_shard % 2 == pool)[:pages]
    handoff_pages = jnp.where(mine[:, None, None, None], found[:pages], from_partner)

    other = [
        swap_pool(
            attend(
                partner_sees,
                partner_queries,
                prior[0],
                planes[1:],
                last_blocks,
                None,
                (h, 1),
                state=partner_state,
                final=True,
                partner=True,
            )
        )
        for h in range(2)
    ]
    own = attend(
        own_sees, span_token_queries, prior[0], planes[1:], last_blocks, None, both, state=own_state, final=True
    )
    span_attention = combine(own, other)
    return (span_attention, handoff_pages, decode_attention)


def solution(mesh):
    in_specs = (
        P(("ctx", "pool"), "tp"),
        P(("ctx", "pool"), "tp"),
        P("tp", ("ctx", "pool"), None),
        P(("ctx", "pool"), None, "tp"),
        P(("ctx", "pool"), None, "tp"),
        P(("ctx", "pool"), "tp", None, None),
        P("tp", None),
        P("tp", None),
        P(),
        P(("ctx", "pool")),
        P(("ctx", "pool")),
        P(("ctx", "pool")),
        P(("ctx", "pool")),
        P(),
    )
    out_specs = (
        P(("ctx", "pool"), "tp"),
        P(("ctx", "pool"), "tp", None, None),
        P(("ctx", "pool"), None, "tp"),
    )
    return jax.shard_map(
        per_device, mesh=mesh, in_specs=in_specs, out_specs=out_specs, check_vma=False
    )
```

```python
import functools
import math

import jax
import jax.numpy as jnp
from jax import lax
from jax.experimental import pallas as pl
from jax.experimental.pallas import tpu as pltpu
from jax.sharding import PartitionSpec as P

HQ = 64
KEY_VALUE_HEADS = 8
HEAD_SIZE = 128
ADAPTER_RANK = 16
BLK = 16
STEPS = 4
GROUP = HQ // KEY_VALUE_HEADS
SHARDS = 16
SIDE = 4
TOKENS = 128
ROWS = 16
DECODE = ROWS * STEPS
ALL_ROWS = TOKENS + DECODE
LOG2_SCALE = math.log2(math.e) / math.sqrt(HEAD_SIZE)
neg_large = -1e30
MIB = 2**20
WIDTH = 2 * HEAD_SIZE


def estimate(us):
    return pl.CostEstimate(flops=int(us * 1.1e9), bytes_accessed=MIB, transcendentals=0)


def split3(x):
    hi = x.astype(jnp.bfloat16)
    rest = x - hi.astype(jnp.float32)
    mid = rest.astype(jnp.bfloat16)
    low = (rest - mid.astype(jnp.float32)).astype(jnp.bfloat16)
    return hi, mid, low

PROJECT_US, ATTEND_US, DECODE_US = 1, 1, 1
ATTEND_VMEM = 24


def project_kernel(
    tp_ref, row_adapter_ref, span_ref, decode_ref, weight_ref, down_ref, up_ref, adapter_ref, after_ref, out_ref, rank_ref
):
    hidden = jnp.concatenate([span_ref[...], decode_ref[...].reshape(DECODE, decode_ref.shape[2])], axis=0)

    @pl.when(pl.program_id(0) == 0)
    def _():
        narrow = jnp.dot(hidden, down_ref[...], preferred_element_type=jnp.float32)
        span_owner = jnp.transpose(jnp.broadcast_to(adapter_ref[...], (TOKENS, TOKENS)))
        row = lax.broadcasted_iota(jnp.int32, (DECODE, TOKENS), 0) // STEPS
        decode_owner = jnp.zeros((DECODE, TOKENS), jnp.int32)
        for r in range(ROWS):
            decode_owner = jnp.where(row == r, row_adapter_ref[r], decode_owner)
        owner = jnp.concatenate([span_owner, decode_owner], axis=0)
        column = lax.broadcasted_iota(jnp.int32, (ALL_ROWS, TOKENS), 1) // ADAPTER_RANK
        hi, mid, low = split3(jnp.where(column == owner, narrow, 0.0))
        rank_ref[:, :TOKENS] = hi
        rank_ref[:, TOKENS : 2 * TOKENS] = mid
        rank_ref[:, 2 * TOKENS :] = low

    up = up_ref[...]
    out = jnp.dot(hidden, weight_ref[...], preferred_element_type=jnp.float32) + jnp.dot(
        rank_ref[...], jnp.concatenate([up, up, up], axis=0), preferred_element_type=jnp.float32
    )
    out_ref[0] = out[:, :WIDTH]
    out_ref[1] = out[:, WIDTH:]


def project(first, tp, row_adapter, span, decode, weight, down, up, adapter, after):
    count = 2
    depth = span.shape[1]
    whole = lambda i, *_: (0, 0)
    return pl.pallas_call(
        project_kernel,
        grid_spec=pltpu.PrefetchScalarGridSpec(
            num_scalar_prefetch=2,
            grid=(count,),
            in_specs=[
                pl.BlockSpec((TOKENS, depth), whole),
                pl.BlockSpec((ROWS, STEPS, depth), lambda i, *_: (0, 0, 0)),
                pl.BlockSpec((depth, 2 * WIDTH), lambda i, tp, rows: (0, jnp.bitwise_xor(tp[0], first + 2 * i))),
                pl.BlockSpec((depth, TOKENS), whole),
                pl.BlockSpec((TOKENS, 2 * WIDTH), lambda i, tp, rows: (0, jnp.bitwise_xor(tp[0], first + 2 * i))),
                pl.BlockSpec((1, TOKENS), whole),
                pl.BlockSpec(memory_space=pl.ANY),
            ],
            out_specs=pl.BlockSpec((2, ALL_ROWS, WIDTH), lambda i, *_: (i, 0, 0)),
            scratch_shapes=[pltpu.VMEM((ALL_ROWS, 3 * TOKENS), jnp.bfloat16)],
        ),
        out_shape=jax.ShapeDtypeStruct((2 * count, ALL_ROWS, WIDTH), jnp.float32),
        compiler_params=pltpu.CompilerParams(vmem_limit_bytes=56 * MIB),
        cost_estimate=estimate(PROJECT_US),
        name="project",
    )(tp, row_adapter, span, decode, weight, down, up, adapter, after)


def finish_kernel(kept_ref, core_ref, chip_ref, *refs):
    out_ref = refs[-1]
    out_ref[...] = (kept_ref[...] + core_ref[...] + chip_ref[...]).astype(jnp.bfloat16)


def finish(kept, from_core, from_chip, after):
    heads, rows, width = from_chip.shape
    block = pl.BlockSpec((heads, rows, width), lambda i: (0, 0, 0))
    return pl.pallas_call(
        finish_kernel,
        grid=(1,),
        in_specs=[block] * 3 + [pl.BlockSpec(memory_space=pl.ANY)] * len(after),
        out_specs=block,
        out_shape=jax.ShapeDtypeStruct(from_chip.shape, jnp.bfloat16),
        compiler_params=pltpu.CompilerParams(vmem_limit_bytes=8 * MIB),
        cost_estimate=estimate(0.5),
        name="finish",
    )(kept, from_core, from_chip, *after)


TILE = 2
TILE_ROWS = TILE * TOKENS
TILES = GROUP // TILE
HEAD_ROWS = GROUP * TOKENS
HEAD_COLUMNS = GROUP * HEAD_SIZE


def attend_kernel(heads, blocks, diagonal, has_state, final, partner, visible_ref, q_ref, known_ref, *refs):
    pieces, refs = refs[: blocks[-1][-1][0] + 1], refs[blocks[-1][-1][0] + 1 :]
    state_ref, out_ref, key_ref, ext_ref = refs
    wide = lax.broadcasted_iota(jnp.int32, (TILE_ROWS, HEAD_SIZE), 1)
    lane = wide[:TOKENS]
    one = jnp.ones((TOKENS, HEAD_SIZE), jnp.bfloat16)
    zero = jnp.zeros((TOKENS, HEAD_SIZE), jnp.bfloat16)
    bounds = [0]
    for shards in blocks:
        bounds.append(bounds[-1] + len(shards) * TOKENS)
    for slot, h in enumerate(heads):
        for b, shards in enumerate(blocks):
            for n, (piece, index, place) in enumerate(shards):
                kv = pieces[piece][index, h]
                keys, values, ones = kv[:, :HEAD_SIZE], kv[:, HEAD_SIZE:], one
                if place is not None:
                    seen = visible_ref[place] != 0
                    keys = jnp.where(seen, keys, known_ref[0, h, :, :HEAD_SIZE])
                    values = jnp.where(seen, values, zero)
                    ones = jnp.where(seen, one, zero)
                here = slice(bounds[b] + n * TOKENS, bounds[b] + (n + 1) * TOKENS)
                key_ref[slot, here, :] = keys
                ext_ref[slot, here, :HEAD_SIZE] = values
                ext_ref[slot, here, HEAD_SIZE:] = ones
        queries = [
            jnp.concatenate(
                [
                    q_ref[:, h * HEAD_COLUMNS + g * HEAD_SIZE : h * HEAD_COLUMNS + (g + 1) * HEAD_SIZE]
                    for g in range(i * TILE, (i + 1) * TILE)
                ],
                axis=0,
            )
            for i in range(TILES)
        ]

        def score(i, b):
            scores = lax.dot_general(
                queries[i],
                key_ref[slot, bounds[b] : bounds[b + 1], :],
                (((1,), (1,)), ((), ())),
                preferred_element_type=jnp.float32,
            )
            if diagonal is not None and diagonal in blocks[b]:
                at = blocks[b].index(diagonal) * TOKENS
                token = lax.broadcasted_iota(jnp.int32, (TILE_ROWS, TOKENS), 0) % TOKENS
                parts = [scores[:, :at]] if at else []
                parts.append(jnp.where(wide <= token, scores[:, at : at + TOKENS], neg_large))
                if at + TOKENS < scores.shape[1]:
                    parts.append(scores[:, at + TOKENS :])
                scores = jnp.concatenate(parts, axis=1)
            return scores, jnp.max(scores, axis=1, keepdims=True) * LOG2_SCALE

        steps = [(i, b) for i in range(TILES) for b in range(len(blocks))]
        if final:
            stats = jnp.zeros((TOKENS, HEAD_SIZE), out_ref.dtype)
        coming = score(*steps[0])
        for n, (i, b) in enumerate(steps):
            scores, top = coming
            if n + 1 < len(steps):
                coming = score(*steps[n + 1])
            here = slice(i * TILE_ROWS, (i + 1) * TILE_ROWS)
            if b or has_state:
                if not b:
                    top_before = state_ref[h, here, HEAD_SIZE : HEAD_SIZE + 1]
                    total = jnp.concatenate(
                        [
                            state_ref[h, here, :HEAD_SIZE],
                            jnp.broadcast_to(state_ref[h, here, WIDTH - 1 :], (TILE_ROWS, HEAD_SIZE)),
                        ],
                        axis=1,
                    )
                top = jnp.maximum(top_before, top)
                total = total * jnp.exp2(top_before - top)
            weights = jnp.exp2(scores * LOG2_SCALE - top).astype(jnp.bfloat16)
            added = jnp.dot(
                weights, ext_ref[slot, bounds[b] : bounds[b + 1], :], preferred_element_type=jnp.float32
            )
            total = total + added if b or has_state else added
            top_before = top
            if b < len(blocks) - 1:
                continue
            if not final:
                out_ref[slot, here, :HEAD_SIZE] = total[:, :HEAD_SIZE]
                out_ref[slot, here, HEAD_SIZE:] = jnp.where(wide < HEAD_SIZE // 2, top, total[:, HEAD_SIZE:])
                continue
            out = total[:, :HEAD_SIZE] / total[:, HEAD_SIZE:]
            level = top + jnp.log2(total[:, HEAD_SIZE:])
            for j in range(TILE):
                g = i * TILE + j
                own = slice(j * TOKENS, (j + 1) * TOKENS)
                out_ref[slot, :, g * HEAD_SIZE : (g + 1) * HEAD_SIZE] = out[own].astype(out_ref.dtype)
                parts = split3(level[own]) if partner else (level[own],)
                for part, piece in enumerate(parts):
                    stats = jnp.where(lane == part * GROUP + g, piece, stats)
        if final:
            out_ref[slot, :, HEAD_COLUMNS:] = stats


def attend(visible, queries, known, pieces, blocks, after, heads, diagonal=None, state=None, final=False, partner=False):
    shards = sum(len(block) for block in blocks)
    count = len(heads)
    if final:
        out_shape = (count, TOKENS, HEAD_COLUMNS + HEAD_SIZE)
    else:
        out_shape = (count, HEAD_ROWS, WIDTH)
    local = pl.BlockSpec(memory_space=pltpu.VMEM)
    return pl.pallas_call(
        functools.partial(attend_kernel, heads, blocks, diagonal, state is not None, final, partner),
        in_specs=[pl.BlockSpec(memory_space=pltpu.SMEM)]
        + [local] * (2 + len(pieces))
        + [pl.BlockSpec(memory_space=pl.ANY) if state is None else local],
        out_specs=local,
        scratch_shapes=[
            pltpu.VMEM((count, shards * TOKENS, HEAD_SIZE), jnp.bfloat16),
            pltpu.VMEM((count, shards * TOKENS, WIDTH), jnp.bfloat16),
        ],
        out_shape=jax.ShapeDtypeStruct(out_shape, jnp.bfloat16 if partner and final else jnp.float32),
        compiler_params=pltpu.CompilerParams(vmem_limit_bytes=ATTEND_VMEM * MIB),
        cost_estimate=estimate(ATTEND_US * count * shards / 16),
        name="attend_last" if final else "attend_first",
    )(visible, queries, known, *pieces, after if state is None else state)


def combine_kernel(*refs):
    own_ref, out_ref = refs[0], refs[3]
    for h in range(2):
        other_ref = refs[1 + h]
        own_level = own_ref[h, :, HEAD_COLUMNS:]
        other_parts = other_ref[0, :, HEAD_COLUMNS:].astype(jnp.float32)
        for g in range(GROUP):
            mine = own_level[:, g : g + 1]
            theirs = (
                other_parts[:, g : g + 1]
                + other_parts[:, GROUP + g : GROUP + g + 1]
                + other_parts[:, 2 * GROUP + g : 2 * GROUP + g + 1]
            )
            peak = jnp.maximum(mine, theirs)
            mine = jnp.exp2(mine - peak)
            theirs = jnp.exp2(theirs - peak)
            whole = mine + theirs
            columns = slice(g * HEAD_SIZE, (g + 1) * HEAD_SIZE)
            mixed = (mine / whole) * own_ref[h, :, columns] + (theirs / whole) * other_ref[0, :, columns].astype(
                jnp.float32
            )
            out_ref[:, h * HEAD_COLUMNS + g * HEAD_SIZE : h * HEAD_COLUMNS + (g + 1) * HEAD_SIZE] = mixed.astype(
                jnp.bfloat16
            )


def combine(own, other):
    return pl.pallas_call(
        combine_kernel,
        out_shape=jax.ShapeDtypeStruct((TOKENS, 2 * HEAD_COLUMNS), jnp.bfloat16),
        compiler_params=pltpu.CompilerParams(vmem_limit_bytes=16 * MIB),
        cost_estimate=estimate(1),
        name="combine",
    )(own, *other)


ROW_BLOCK = 8


def decode_kernel(length_ref, live_ref, q_ref, cache_ref, fresh_ref, after_ref, out_ref):
    first = pl.program_id(0) * ROW_BLOCK
    query_rows = STEPS * GROUP
    rows = ROW_BLOCK * query_rows
    contract = (((1,), (1,)), ((), ()))
    slot = lax.broadcasted_iota(jnp.int32, (query_rows, cache_ref.shape[2]), 1)
    fresh_row = lax.broadcasted_iota(jnp.int32, (rows, DECODE), 1) // STEPS
    fresh_step = lax.broadcasted_iota(jnp.int32, (rows, DECODE), 1) % STEPS
    row = lax.broadcasted_iota(jnp.int32, (rows, DECODE), 0) // query_rows
    step = lax.broadcasted_iota(jnp.int32, (rows, DECODE), 0) % query_rows // GROUP
    fresh_seen = (fresh_row == row + first) & (fresh_step <= step)
    cached, fresh = [], []
    for h in range(2):
        scores = lax.dot_general(
            q_ref[:, h].reshape(rows, HEAD_SIZE),
            fresh_ref[h, :, :HEAD_SIZE],
            contract,
            preferred_element_type=jnp.float32,
        )
        fresh.append(jnp.where(fresh_seen, scores, neg_large))
        for n in range(ROW_BLOCK):
            scores = lax.dot_general(
                q_ref[n, h], cache_ref[n, h, :, :HEAD_SIZE], contract, preferred_element_type=jnp.float32
            )
            cached.append(jnp.where(slot < length_ref[first + n], scores, neg_large))
    cached = jnp.concatenate(cached, axis=0)
    fresh = jnp.concatenate(fresh, axis=0)
    top = jnp.maximum(jnp.max(cached, axis=1, keepdims=True), jnp.max(fresh, axis=1, keepdims=True))
    cached = jnp.exp2((cached - top) * LOG2_SCALE)
    fresh = jnp.exp2((fresh - top) * LOG2_SCALE)
    total = jnp.sum(cached, axis=1, keepdims=True) + jnp.sum(fresh, axis=1, keepdims=True)
    cached = cached.astype(jnp.bfloat16)
    fresh = fresh.astype(jnp.bfloat16)
    for h in range(2):
        of_fresh = jnp.dot(
            fresh[h * rows : (h + 1) * rows], fresh_ref[h, :, HEAD_SIZE:], preferred_element_type=jnp.float32
        )
        for n in range(ROW_BLOCK):
            here = slice(h * rows + n * query_rows, h * rows + (n + 1) * query_rows)
            out = jnp.dot(cached[here], cache_ref[n, h, :, HEAD_SIZE:], preferred_element_type=jnp.float32)
            out = (out + of_fresh[n * query_rows : (n + 1) * query_rows]) / total[here]
            out_ref[n, h] = jnp.where(first + n < live_ref[0], out, 0.0).astype(jnp.bfloat16)


def decode_attend(lengths, live, queries, cache, fresh, after):
    rows, heads, query_rows, _ = queries.shape
    cache_size = cache.shape[2]
    return pl.pallas_call(
        decode_kernel,
        grid_spec=pltpu.PrefetchScalarGridSpec(
            num_scalar_prefetch=2,
            grid=(rows // ROW_BLOCK,),
            in_specs=[
                pl.BlockSpec((ROW_BLOCK, heads, query_rows, HEAD_SIZE), lambda i, *_: (i, 0, 0, 0)),
                pl.BlockSpec((ROW_BLOCK, heads, cache_size, 2 * HEAD_SIZE), lambda i, *_: (i, 0, 0, 0)),
                pl.BlockSpec((heads, DECODE, 2 * HEAD_SIZE), lambda i, *_: (0, 0, 0)),
                pl.BlockSpec(memory_space=pl.ANY),
            ],
            out_specs=pl.BlockSpec((ROW_BLOCK, heads, query_rows, HEAD_SIZE), lambda i, *_: (i, 0, 0, 0)),
        ),
        out_shape=jax.ShapeDtypeStruct(queries.shape, jnp.bfloat16),
        compiler_params=pltpu.CompilerParams(vmem_limit_bytes=24 * MIB),
        cost_estimate=estimate(DECODE_US),
        name="decode",
    )(lengths, live, queries, cache, fresh, after)


def pages_kernel(where_ref, *refs):
    pieces = refs[:SIDE]
    out_ref = refs[SIDE]
    for n in range(out_ref.shape[0]):
        dz, dy = where_ref[0, n], where_ref[1, n]
        rows = pl.ds(pl.multiple_of(where_ref[2, n] * BLK, BLK), BLK)
        for h in range(2):
            page = pieces[0][dy, h, rows, :]
            for k in range(1, SIDE):
                page = jnp.where(dz == k, pieces[k][dy, h, rows, :], page)
            out_ref[n, h] = page


def pick_pages(where, pieces):
    count = where.shape[1]
    return pl.pallas_call(
        pages_kernel,
        grid_spec=pltpu.PrefetchScalarGridSpec(
            num_scalar_prefetch=1,
            grid=(1,),
            in_specs=[pl.BlockSpec((SIDE, 2, TOKENS, WIDTH), lambda i, *_: (0, 0, 0, 0))] * SIDE,
            out_specs=pl.BlockSpec((count, 2, BLK, WIDTH), lambda i, *_: (0, 0, 0, 0)),
        ),
        out_shape=jax.ShapeDtypeStruct((count, 2, BLK, WIDTH), jnp.bfloat16),
        compiler_params=pltpu.CompilerParams(vmem_limit_bytes=16 * MIB),
        cost_estimate=estimate(1.5),
        name="pages",
    )(where, *pieces)


def shift(x, dz, dy):
    perm = [
        (z * SIDE + y, ((z + dz) % SIDE) * SIDE + (y + dy) % SIDE) for z in range(SIDE) for y in range(SIDE)
    ]
    return lax.ppermute(x, "ctx", perm)


def swap_pool(x):
    return lax.ppermute(x, "pool", [(0, 1), (1, 0)])


def swap_tp(x, bit):
    return lax.ppermute(x, "tp", [(i, i ^ bit) for i in range(4)])


def ring(x, along_z):
    move = (lambda d: shift(x, d, 0)) if along_z else (lambda d: shift(x, 0, d))
    far = {1: move(1), 3: move(3), 2: move(2)}
    return [x, far[1], far[2], far[3]]


def per_device(
    span_hidden_states,
    span_token_queries,
    earlier_key_values,
    decode_hidden_states,
    decode_token_queries,
    decode_row_cache,
    key_value_weight,
    adapter_down_weight,
    adapter_up_weight,
    prompt_adapter,
    row_adapter_index,
    group_live_rows,
    cached_row_lengths,
    block_target_page,
):
    tp = lax.axis_index("tp")
    ctx = lax.axis_index("ctx")
    pool = lax.axis_index("pool")
    my_z, my_y = ctx // SIDE, ctx % SIDE

    prior = ring(jnp.stack(ring(earlier_key_values, False)), True)

    def partial_kv(first, after):
        return project(
            first,
            tp.astype(jnp.int32).reshape(1),
            row_adapter_index,
            span_hidden_states,
            decode_hidden_states,
            key_value_weight,
            adapter_down_weight,
            adapter_up_weight,
            prompt_adapter.reshape(1, TOKENS),
            after,
        )

    from_core = swap_tp(partial_kv(1, row_adapter_index), 1)
    kept = partial_kv(0, row_adapter_index)

    def from_chip(rows):
        return swap_tp(kept[2:, rows] + from_core[2:, rows], 2)

    span_rows, decode_rows = slice(0, TOKENS), slice(TOKENS, ALL_ROWS)
    span_kv = finish(kept, from_core, from_chip(span_rows), ())
    decode_kv = (kept[:2, decode_rows] + from_core[:2, decode_rows] + from_chip(decode_rows)).astype(jnp.bfloat16)

    column = jnp.stack(ring(span_kv, False))
    planes = ring(column, True)

    queries = decode_token_queries.reshape(ROWS, STEPS, 2, GROUP, HEAD_SIZE)
    queries = jnp.transpose(queries, (0, 2, 1, 3, 4)).reshape(ROWS, 2, STEPS * GROUP, HEAD_SIZE)
    decoded = decode_attend(cached_row_lengths, group_live_rows, queries, decode_row_cache, decode_kv, row_adapter_index)
    decoded = jnp.transpose(decoded.reshape(ROWS, 2, STEPS, GROUP, HEAD_SIZE), (0, 2, 1, 3, 4))
    decode_attention = decoded.reshape(ROWS, STEPS, 2 * GROUP * HEAD_SIZE)

    far = jnp.arange(SIDE, dtype=jnp.int32)
    shard_z, shard_y = jnp.mod(my_z - far, SIDE), jnp.mod(my_y - far, SIDE)
    place = shard_z[:, None] * SIDE + shard_y[None, :]
    partner_sees = ((place < ctx) | ((place == ctx) & (pool == 0))).astype(jnp.int32).reshape(-1)
    own_sees = (place <= ctx).astype(jnp.int32).reshape(-1)
    earlier = [(p, k, None) for p in range(SIDE) for k in range(SIDE)]
    seen_first = earlier + [(SIDE, k, k) for k in range(SIDE)]
    first_blocks = (tuple(seen_first[:10]), tuple(seen_first[10:]))
    others = [(p, k, (p + 1) * SIDE + k) for p in range(SIDE - 1) for k in range(SIDE)]
    last_blocks = (tuple(others),)
    both = (0, 1)
    first_pieces = prior + [column]
    partner_queries = swap_pool(span_token_queries)
    own_state = attend(
        own_sees, span_token_queries, prior[0], first_pieces, first_blocks, column, both, diagonal=(SIDE, 0, 0)
    )
    partner_state = attend(partner_sees, partner_queries, prior[0], first_pieces, first_blocks, column, both)

    pages = TOKENS // BLK
    shard = ctx * 2 + pool
    partner_shard = ctx * 2 + 1 - pool
    page_ids = jnp.concatenate([shard * pages + jnp.arange(pages), partner_shard * pages + jnp.arange(pages)])
    block_ids = jnp.arange(block_target_page.shape[0], dtype=jnp.int32)
    source = jnp.sum(
        jnp.where(block_target_page[None, :] == page_ids[:, None], block_ids[None, :], 0), axis=1
    )
    source_shard = source // pages
    source_ctx = source_shard // 2
    where = jnp.stack(
        [
            jnp.mod(my_z - source_ctx // SIDE, SIDE),
            jnp.mod(my_y - source_ctx % SIDE, SIDE),
            source % pages,
        ]
    ).astype(jnp.int32)
    found = pick_pages(where, planes)
    from_partner = swap_pool(found[pages:])
    mine = (source_shard % 2 == pool)[:pages]
    handoff_pages = jnp.where(mine[:, None, None, None], found[:pages], from_partner)

    other = [
        swap_pool(
            attend(
                partner_sees,
                partner_queries,
                prior[0],
                planes[1:],
                last_blocks,
                None,
                (h,),
                state=partner_state,
                final=True,
                partner=True,
            )
        )
        for h in range(2)
    ]
    own = attend(
        own_sees, span_token_queries, prior[0], planes[1:], last_blocks, None, both, state=own_state, final=True
    )
    span_attention = combine(own, other)
    return (span_attention, handoff_pages, decode_attention)


def solution(mesh):
    in_specs = (
        P(("ctx", "pool"), "tp"),
        P(("ctx", "pool"), "tp"),
        P("tp", ("ctx", "pool"), None),
        P(("ctx", "pool"), None, "tp"),
        P(("ctx", "pool"), None, "tp"),
        P(("ctx", "pool"), "tp", None, None),
        P("tp", None),
        P("tp", None),
        P(),
        P(("ctx", "pool")),
        P(("ctx", "pool")),
        P(("ctx", "pool")),
        P(("ctx", "pool")),
        P(),
    )
    out_specs = (
        P(("ctx", "pool"), "tp"),
        P(("ctx", "pool"), "tp", None, None),
        P(("ctx", "pool"), None, "tp"),
    )
    return jax.shard_map(
        per_device, mesh=mesh, in_specs=in_specs, out_specs=out_specs, check_vma=False
    )
```

```python
import functools
import math

import jax
import jax.numpy as jnp
from jax import lax
from jax.experimental import pallas as pl
from jax.experimental.pallas import tpu as pltpu
from jax.sharding import PartitionSpec as P

HQ = 64
KEY_VALUE_HEADS = 8
HEAD_SIZE = 128
ADAPTER_RANK = 16
BLK = 16
STEPS = 4
GROUP = HQ // KEY_VALUE_HEADS
SHARDS = 16
SIDE = 4
TOKENS = 128
ROWS = 16
DECODE = ROWS * STEPS
ALL_ROWS = TOKENS + DECODE
LOG2_SCALE = math.log2(math.e) / math.sqrt(HEAD_SIZE)
neg_large = -1e30
MIB = 2**20
WIDTH = 2 * HEAD_SIZE


def estimate(us):
    return pl.CostEstimate(flops=int(us * 1.1e9), bytes_accessed=MIB, transcendentals=0)


def split3(x):
    hi = x.astype(jnp.bfloat16)
    rest = x - hi.astype(jnp.float32)
    mid = rest.astype(jnp.bfloat16)
    low = (rest - mid.astype(jnp.float32)).astype(jnp.bfloat16)
    return hi, mid, low

PROJECT_US, ATTEND_US, DECODE_US = 1, 3.4, 1
ATTEND_VMEM, PROJECT_VMEM, DECODE_VMEM = 24, 56, 24


CHUNKS = 4


def weight_copies(first, tp, weight_ref, buffer_ref, sems):
    depth = weight_ref.shape[0] // CHUNKS
    copies = []
    for i in range(2):
        column = pl.multiple_of(jnp.bitwise_xor(tp, first + 2 * i) * 2 * WIDTH, 2 * WIDTH)
        copies.append(
            [
                pltpu.make_async_copy(
                    weight_ref.at[pl.ds(k * depth, depth), pl.ds(column, 2 * WIDTH)],
                    buffer_ref.at[i, pl.ds(k * depth, depth)],
                    sems.at[i, k],
                )
                for k in range(CHUNKS)
            ]
        )
    return copies


def project_columns(first, tp, copies, hidden_ref, rank_ref, up_ref, buffer_ref, out_ref):
    depth = hidden_ref.shape[1] // CHUNKS
    for i in range(2):
        column = pl.multiple_of(jnp.bitwise_xor(tp, first + 2 * i) * 2 * WIDTH, 2 * WIDTH)
        up = up_ref[:, pl.ds(column, 2 * WIDTH)]
        out = jnp.dot(rank_ref[...], jnp.concatenate([up, up, up], axis=0), preferred_element_type=jnp.float32)
        for k in range(CHUNKS):
            copies[i][k].wait()
            here = slice(k * depth, (k + 1) * depth)
            out = out + jnp.dot(hidden_ref[:, here], buffer_ref[i, here, :], preferred_element_type=jnp.float32)
        out_ref[2 * i] = out[:, :WIDTH]
        out_ref[2 * i + 1] = out[:, WIDTH:]


def project_first_kernel(
    first,
    tp_ref,
    row_adapter_ref,
    adapter_ref,
    span_ref,
    decode_ref,
    weight_ref,
    down_ref,
    up_ref,
    out_ref,
    hidden_ref,
    rank_ref,
    buffer_ref,
    decode_buffer,
    down_buffer,
    up_buffer,
    sems,
    small_sems,
):
    tp = tp_ref[0]
    small = [
        pltpu.make_async_copy(span_ref, hidden_ref.at[pl.ds(0, TOKENS)], small_sems.at[0]),
        pltpu.make_async_copy(decode_ref, decode_buffer, small_sems.at[1]),
        pltpu.make_async_copy(down_ref, down_buffer, small_sems.at[2]),
        pltpu.make_async_copy(up_ref, up_buffer, small_sems.at[3]),
    ]
    for copy in small:
        copy.start()
    copies = weight_copies(first, tp, weight_ref, buffer_ref, sems)
    for i in range(2):
        for copy in copies[i]:
            copy.start()
    span_owner = jnp.transpose(jnp.broadcast_to(adapter_ref[...], (TOKENS, TOKENS)))
    row = lax.broadcasted_iota(jnp.int32, (DECODE, TOKENS), 0) // STEPS
    decode_owner = jnp.zeros((DECODE, TOKENS), jnp.int32)
    for r in range(ROWS):
        decode_owner = jnp.where(row == r, row_adapter_ref[r], decode_owner)
    owner = jnp.concatenate([span_owner, decode_owner], axis=0)
    column = lax.broadcasted_iota(jnp.int32, (ALL_ROWS, TOKENS), 1) // ADAPTER_RANK
    for copy in small:
        copy.wait()
    hidden_ref[TOKENS:, :] = decode_buffer[...].reshape(DECODE, decode_buffer.shape[2])
    narrow = jnp.dot(hidden_ref[...], down_buffer[...], preferred_element_type=jnp.float32)
    for part, piece in enumerate(split3(jnp.where(column == owner, narrow, 0.0))):
        rank_ref[:, part * TOKENS : (part + 1) * TOKENS] = piece
    project_columns(first, tp, copies, hidden_ref, rank_ref, up_buffer, buffer_ref, out_ref)


def project_second_kernel(first, tp_ref, hidden_ref, rank_ref, up_ref, weight_ref, after_ref, out_ref, buffer_ref, sems):
    tp = tp_ref[0]
    copies = weight_copies(first, tp, weight_ref, buffer_ref, sems)
    for i in range(2):
        for copy in copies[i]:
            copy.start()
    project_columns(first, tp, copies, hidden_ref, rank_ref, up_ref, buffer_ref, out_ref)


def project_first(first, tp, row_adapter, adapter, span, decode, weight, down, up):
    depth = span.shape[1]
    scalar = pl.BlockSpec(memory_space=pltpu.SMEM)
    local = pl.BlockSpec(memory_space=pltpu.VMEM)
    far = pl.BlockSpec(memory_space=pl.ANY)
    return pl.pallas_call(
        functools.partial(project_first_kernel, first),
        in_specs=[scalar, scalar, local] + [far] * 5,
        out_specs=[local] * 3,
        out_shape=[
            jax.ShapeDtypeStruct((4, ALL_ROWS, WIDTH), jnp.float32),
            jax.ShapeDtypeStruct((ALL_ROWS, depth), jnp.bfloat16),
            jax.ShapeDtypeStruct((ALL_ROWS, 3 * TOKENS), jnp.bfloat16),
        ],
        scratch_shapes=[
            pltpu.VMEM((2, depth, 2 * WIDTH), jnp.bfloat16),
            pltpu.VMEM(decode.shape, jnp.bfloat16),
            pltpu.VMEM(down.shape, jnp.bfloat16),
            pltpu.VMEM(up.shape, jnp.bfloat16),
            pltpu.SemaphoreType.DMA((2, CHUNKS)),
            pltpu.SemaphoreType.DMA((4,)),
        ],
        compiler_params=pltpu.CompilerParams(vmem_limit_bytes=PROJECT_VMEM * MIB),
        cost_estimate=estimate(PROJECT_US),
        name="project_first",
    )(tp, row_adapter, adapter, span, decode, weight, down, up)


def project_second(first, tp, hidden, rank, up, weight, after):
    depth = hidden.shape[1]
    local = pl.BlockSpec(memory_space=pltpu.VMEM)
    far = pl.BlockSpec(memory_space=pl.ANY)
    return pl.pallas_call(
        functools.partial(project_second_kernel, first),
        in_specs=[pl.BlockSpec(memory_space=pltpu.SMEM), local, local, local, far, far],
        out_specs=local,
        out_shape=jax.ShapeDtypeStruct((4, ALL_ROWS, WIDTH), jnp.float32),
        scratch_shapes=[
            pltpu.VMEM((2, depth, 2 * WIDTH), jnp.bfloat16),
            pltpu.SemaphoreType.DMA((2, CHUNKS)),
        ],
        compiler_params=pltpu.CompilerParams(vmem_limit_bytes=PROJECT_VMEM * MIB),
        cost_estimate=estimate(PROJECT_US),
        name="project_second",
    )(tp, hidden, rank, up, weight, after)


def finish_kernel(kept_ref, core_ref, chip_ref, *refs):
    span_ref, decode_ref = refs[-2:]
    total = (kept_ref[:2] + core_ref[:2] + chip_ref[...]).astype(jnp.bfloat16)
    span_ref[...] = total[:, :TOKENS]
    decode_ref[...] = total[:, TOKENS:]


def finish(kept, from_core, from_chip, after):
    heads, _, width = from_chip.shape
    local = pl.BlockSpec(memory_space=pltpu.VMEM)
    return pl.pallas_call(
        finish_kernel,
        in_specs=[local] * 3 + [pl.BlockSpec(memory_space=pl.ANY)] * len(after),
        out_specs=[local] * 2,
        out_shape=[
            jax.ShapeDtypeStruct((heads, TOKENS, width), jnp.bfloat16),
            jax.ShapeDtypeStruct((heads, DECODE, width), jnp.bfloat16),
        ],
        compiler_params=pltpu.CompilerParams(vmem_limit_bytes=8 * MIB),
        cost_estimate=estimate(0.5),
        name="finish",
    )(kept, from_core, from_chip, *after)


TILE = 2
TILE_ROWS = TILE * TOKENS
TILES = GROUP // TILE
HEAD_ROWS = GROUP * TOKENS
HEAD_COLUMNS = GROUP * HEAD_SIZE


def attend_kernel(heads, blocks, diagonal, has_state, final, partner, visible_ref, q_ref, known_ref, *refs):
    pieces, refs = refs[: blocks[-1][-1][0] + 1], refs[blocks[-1][-1][0] + 1 :]
    state_ref, out_ref, key_ref, ext_ref = refs
    wide = lax.broadcasted_iota(jnp.int32, (TILE_ROWS, HEAD_SIZE), 1)
    lane = wide[:TOKENS]
    one = jnp.ones((TOKENS, HEAD_SIZE), jnp.bfloat16)
    zero = jnp.zeros((TOKENS, HEAD_SIZE), jnp.bfloat16)
    bounds = [0]
    for shards in blocks:
        bounds.append(bounds[-1] + len(shards) * TOKENS)
    for slot, h in enumerate(heads):
        for b, shards in enumerate(blocks):
            for n, (piece, index, place) in enumerate(shards):
                kv = pieces[piece][index, h]
                keys, values, ones = kv[:, :HEAD_SIZE], kv[:, HEAD_SIZE:], one
                if place is not None:
                    seen = visible_ref[place] != 0
                    keys = jnp.where(seen, keys, known_ref[0, h, :, :HEAD_SIZE])
                    values = jnp.where(seen, values, zero)
                    ones = jnp.where(seen, one, zero)
                here = slice(bounds[b] + n * TOKENS, bounds[b] + (n + 1) * TOKENS)
                key_ref[slot, here, :] = keys
                ext_ref[slot, here, :HEAD_SIZE] = values
                ext_ref[slot, here, HEAD_SIZE:] = ones
        queries = [
            jnp.concatenate(
                [
                    q_ref[:, h * HEAD_COLUMNS + g * HEAD_SIZE : h * HEAD_COLUMNS + (g + 1) * HEAD_SIZE]
                    for g in range(i * TILE, (i + 1) * TILE)
                ],
                axis=0,
            )
            for i in range(TILES)
        ]

        def score(i, b):
            scores = lax.dot_general(
                queries[i],
                key_ref[slot, bounds[b] : bounds[b + 1], :],
                (((1,), (1,)), ((), ())),
                preferred_element_type=jnp.float32,
            )
            if diagonal is not None and diagonal in blocks[b]:
                at = blocks[b].index(diagonal) * TOKENS
                token = lax.broadcasted_iota(jnp.int32, (TILE_ROWS, TOKENS), 0) % TOKENS
                parts = [scores[:, :at]] if at else []
                parts.append(jnp.where(wide <= token, scores[:, at : at + TOKENS], neg_large))
                if at + TOKENS < scores.shape[1]:
                    parts.append(scores[:, at + TOKENS :])
                scores = jnp.concatenate(parts, axis=1)
            return scores, jnp.max(scores, axis=1, keepdims=True) * LOG2_SCALE

        steps = [(i, b) for i in range(TILES) for b in range(len(blocks))]
        if final:
            stats = jnp.zeros((TOKENS, HEAD_SIZE), out_ref.dtype)
        coming = score(*steps[0])
        for n, (i, b) in enumerate(steps):
            scores, top = coming
            if n + 1 < len(steps):
                coming = score(*steps[n + 1])
            here = slice(i * TILE_ROWS, (i + 1) * TILE_ROWS)
            if b or has_state:
                if not b:
                    top_before = state_ref[h, here, HEAD_SIZE : HEAD_SIZE + 1]
                    total = jnp.concatenate(
                        [
                            state_ref[h, here, :HEAD_SIZE],
                            jnp.broadcast_to(state_ref[h, here, WIDTH - 1 :], (TILE_ROWS, HEAD_SIZE)),
                        ],
                        axis=1,
                    )
                top = jnp.maximum(top_before, top)
                total = total * jnp.exp2(top_before - top)
            weights = jnp.exp2(scores * LOG2_SCALE - top).astype(jnp.bfloat16)
            added = jnp.dot(
                weights, ext_ref[slot, bounds[b] : bounds[b + 1], :], preferred_element_type=jnp.float32
            )
            total = total + added if b or has_state else added
            top_before = top
            if b < len(blocks) - 1:
                continue
            if not final:
                out_ref[slot, here, :HEAD_SIZE] = total[:, :HEAD_SIZE]
                out_ref[slot, here, HEAD_SIZE:] = jnp.where(wide < HEAD_SIZE // 2, top, total[:, HEAD_SIZE:])
                continue
            out = total[:, :HEAD_SIZE] / total[:, HEAD_SIZE:]
            level = top + jnp.log2(total[:, HEAD_SIZE:])
            for j in range(TILE):
                g = i * TILE + j
                own = slice(j * TOKENS, (j + 1) * TOKENS)
                out_ref[slot, :, g * HEAD_SIZE : (g + 1) * HEAD_SIZE] = out[own].astype(out_ref.dtype)
                parts = split3(level[own]) if partner else (level[own],)
                for part, piece in enumerate(parts):
                    stats = jnp.where(lane == part * GROUP + g, piece, stats)
        if final:
            out_ref[slot, :, HEAD_COLUMNS:] = stats


def attend(visible, queries, known, pieces, blocks, after, heads, diagonal=None, state=None, final=False, partner=False):
    shards = sum(len(block) for block in blocks)
    count = len(heads)
    if final:
        out_shape = (count, TOKENS, HEAD_COLUMNS + HEAD_SIZE)
    else:
        out_shape = (count, HEAD_ROWS, WIDTH)
    local = pl.BlockSpec(memory_space=pltpu.VMEM)
    return pl.pallas_call(
        functools.partial(attend_kernel, heads, blocks, diagonal, state is not None, final, partner),
        in_specs=[pl.BlockSpec(memory_space=pltpu.SMEM)]
        + [local] * (2 + len(pieces))
        + [pl.BlockSpec(memory_space=pl.ANY) if state is None else local],
        out_specs=local,
        scratch_shapes=[
            pltpu.VMEM((count, shards * TOKENS, HEAD_SIZE), jnp.bfloat16),
            pltpu.VMEM((count, shards * TOKENS, WIDTH), jnp.bfloat16),
        ],
        out_shape=jax.ShapeDtypeStruct(out_shape, jnp.bfloat16 if partner and final else jnp.float32),
        compiler_params=pltpu.CompilerParams(vmem_limit_bytes=ATTEND_VMEM * MIB),
        cost_estimate=estimate(ATTEND_US * count * shards / 16),
        name="attend_last" if final else "attend_first",
    )(visible, queries, known, *pieces, after if state is None else state)


def combine_kernel(*refs):
    own_ref, out_ref = refs[0], refs[3]
    for h in range(2):
        other_ref = refs[1 + h]
        own_level = own_ref[h, :, HEAD_COLUMNS:]
        other_parts = other_ref[0, :, HEAD_COLUMNS:].astype(jnp.float32)
        for g in range(GROUP):
            mine = own_level[:, g : g + 1]
            theirs = (
                other_parts[:, g : g + 1]
                + other_parts[:, GROUP + g : GROUP + g + 1]
                + other_parts[:, 2 * GROUP + g : 2 * GROUP + g + 1]
            )
            peak = jnp.maximum(mine, theirs)
            mine = jnp.exp2(mine - peak)
            theirs = jnp.exp2(theirs - peak)
            whole = mine + theirs
            columns = slice(g * HEAD_SIZE, (g + 1) * HEAD_SIZE)
            mixed = (mine / whole) * own_ref[h, :, columns] + (theirs / whole) * other_ref[0, :, columns].astype(
                jnp.float32
            )
            out_ref[:, h * HEAD_COLUMNS + g * HEAD_SIZE : h * HEAD_COLUMNS + (g + 1) * HEAD_SIZE] = mixed.astype(
                jnp.bfloat16
            )


def combine(own, other):
    return pl.pallas_call(
        combine_kernel,
        out_shape=jax.ShapeDtypeStruct((TOKENS, 2 * HEAD_COLUMNS), jnp.bfloat16),
        compiler_params=pltpu.CompilerParams(vmem_limit_bytes=16 * MIB),
        cost_estimate=estimate(1),
        name="combine",
    )(own, *other)


ROW_BLOCK = 8


def decode_kernel(length_ref, live_ref, q_ref, cache_ref, fresh_ref, *refs):
    out_ref = refs[-1]
    first = pl.program_id(0) * ROW_BLOCK
    query_rows = STEPS * GROUP
    rows = ROW_BLOCK * query_rows
    contract = (((1,), (1,)), ((), ()))
    slot = lax.broadcasted_iota(jnp.int32, (query_rows, cache_ref.shape[2]), 1)
    fresh_row = lax.broadcasted_iota(jnp.int32, (rows, DECODE), 1) // STEPS
    fresh_step = lax.broadcasted_iota(jnp.int32, (rows, DECODE), 1) % STEPS
    row = lax.broadcasted_iota(jnp.int32, (rows, DECODE), 0) // query_rows
    step = lax.broadcasted_iota(jnp.int32, (rows, DECODE), 0) % query_rows // GROUP
    fresh_seen = (fresh_row == row + first) & (fresh_step <= step)
    cached, fresh = [], []
    for h in range(2):
        scores = lax.dot_general(
            q_ref[:, h].reshape(rows, HEAD_SIZE),
            fresh_ref[h, :, :HEAD_SIZE],
            contract,
            preferred_element_type=jnp.float32,
        )
        fresh.append(jnp.where(fresh_seen, scores, neg_large))
        for n in range(ROW_BLOCK):
            scores = lax.dot_general(
                q_ref[n, h], cache_ref[n, h, :, :HEAD_SIZE], contract, preferred_element_type=jnp.float32
            )
            cached.append(jnp.where(slot < length_ref[first + n], scores, neg_large))
    cached = jnp.concatenate(cached, axis=0)
    fresh = jnp.concatenate(fresh, axis=0)
    top = jnp.maximum(jnp.max(cached, axis=1, keepdims=True), jnp.max(fresh, axis=1, keepdims=True))
    cached = jnp.exp2((cached - top) * LOG2_SCALE)
    fresh = jnp.exp2((fresh - top) * LOG2_SCALE)
    total = jnp.sum(cached, axis=1, keepdims=True) + jnp.sum(fresh, axis=1, keepdims=True)
    cached = cached.astype(jnp.bfloat16)
    fresh = fresh.astype(jnp.bfloat16)
    for h in range(2):
        of_fresh = jnp.dot(
            fresh[h * rows : (h + 1) * rows], fresh_ref[h, :, HEAD_SIZE:], preferred_element_type=jnp.float32
        )
        for n in range(ROW_BLOCK):
            here = slice(h * rows + n * query_rows, h * rows + (n + 1) * query_rows)
            out = jnp.dot(cached[here], cache_ref[n, h, :, HEAD_SIZE:], preferred_element_type=jnp.float32)
            out = (out + of_fresh[n * query_rows : (n + 1) * query_rows]) / total[here]
            out_ref[n, h] = jnp.where(first + n < live_ref[0], out, 0.0).astype(jnp.bfloat16)


def decode_attend(lengths, live, queries, cache, fresh, after):
    rows, heads, query_rows, _ = queries.shape
    cache_size = cache.shape[2]
    return pl.pallas_call(
        decode_kernel,
        grid_spec=pltpu.PrefetchScalarGridSpec(
            num_scalar_prefetch=2,
            grid=(rows // ROW_BLOCK,),
            in_specs=[
                pl.BlockSpec((ROW_BLOCK, heads, query_rows, HEAD_SIZE), lambda i, *_: (i, 0, 0, 0)),
                pl.BlockSpec((ROW_BLOCK, heads, cache_size, 2 * HEAD_SIZE), lambda i, *_: (i, 0, 0, 0)),
                pl.BlockSpec((heads, DECODE, 2 * HEAD_SIZE), lambda i, *_: (0, 0, 0)),
            ]
            + [pl.BlockSpec(memory_space=pl.ANY)] * len(after),
            out_specs=pl.BlockSpec((ROW_BLOCK, heads, query_rows, HEAD_SIZE), lambda i, *_: (i, 0, 0, 0)),
        ),
        out_shape=jax.ShapeDtypeStruct(queries.shape, jnp.bfloat16),
        compiler_params=pltpu.CompilerParams(vmem_limit_bytes=DECODE_VMEM * MIB),
        cost_estimate=estimate(DECODE_US),
        name="decode",
    )(lengths, live, queries, cache, fresh, *after)


def pages_kernel(where_ref, *refs):
    pieces = refs[:SIDE]
    out_ref = refs[SIDE]
    for n in range(out_ref.shape[0]):
        dz, dy = where_ref[0, n], where_ref[1, n]
        rows = pl.ds(pl.multiple_of(where_ref[2, n] * BLK, BLK), BLK)
        for h in range(2):
            page = pieces[0][dy, h, rows, :]
            for k in range(1, SIDE):
                page = jnp.where(dz == k, pieces[k][dy, h, rows, :], page)
            out_ref[n, h] = page


def pick_pages(where, pieces):
    count = where.shape[1]
    return pl.pallas_call(
        pages_kernel,
        grid_spec=pltpu.PrefetchScalarGridSpec(
            num_scalar_prefetch=1,
            grid=(1,),
            in_specs=[pl.BlockSpec((SIDE, 2, TOKENS, WIDTH), lambda i, *_: (0, 0, 0, 0))] * SIDE,
            out_specs=pl.BlockSpec((count, 2, BLK, WIDTH), lambda i, *_: (0, 0, 0, 0)),
        ),
        out_shape=jax.ShapeDtypeStruct((count, 2, BLK, WIDTH), jnp.bfloat16),
        compiler_params=pltpu.CompilerParams(vmem_limit_bytes=16 * MIB),
        cost_estimate=estimate(1.5),
        name="pages",
    )(where, *pieces)


def shift(x, dz, dy):
    perm = [
        (z * SIDE + y, ((z + dz) % SIDE) * SIDE + (y + dy) % SIDE) for z in range(SIDE) for y in range(SIDE)
    ]
    return lax.ppermute(x, "ctx", perm)


def swap_pool(x):
    return lax.ppermute(x, "pool", [(0, 1), (1, 0)])


def swap_tp(x, bit):
    return lax.ppermute(x, "tp", [(i, i ^ bit) for i in range(4)])


def ring(x, along_z):
    move = (lambda d: shift(x, d, 0)) if along_z else (lambda d: shift(x, 0, d))
    far = {1: move(1), 3: move(3), 2: move(2)}
    return [x, far[1], far[2], far[3]]


def per_device(
    span_hidden_states,
    span_token_queries,
    earlier_key_values,
    decode_hidden_states,
    decode_token_queries,
    decode_row_cache,
    key_value_weight,
    adapter_down_weight,
    adapter_up_weight,
    prompt_adapter,
    row_adapter_index,
    group_live_rows,
    cached_row_lengths,
    block_target_page,
):
    tp = lax.axis_index("tp")
    ctx = lax.axis_index("ctx")
    pool = lax.axis_index("pool")
    my_z, my_y = ctx // SIDE, ctx % SIDE

    prior = ring(jnp.stack(ring(earlier_key_values, False)), True)

    my_tp = tp.astype(jnp.int32).reshape(1)
    for_core, hidden, rank = project_first(
        1,
        my_tp,
        row_adapter_index,
        prompt_adapter.reshape(1, TOKENS),
        span_hidden_states,
        decode_hidden_states,
        key_value_weight,
        adapter_down_weight,
        adapter_up_weight,
    )
    from_core = swap_tp(for_core, 1)
    kept = project_second(0, my_tp, hidden, rank, adapter_up_weight, key_value_weight, prior[0])
    from_chip = swap_tp(kept[2:] + from_core[2:], 2)
    span_kv, decode_kv = finish(kept, from_core, from_chip, (prior[1],))

    column = jnp.stack(ring(span_kv, False))
    planes = ring(column, True)

    queries = decode_token_queries.reshape(ROWS, STEPS, 2, GROUP, HEAD_SIZE)
    queries = jnp.transpose(queries, (0, 2, 1, 3, 4)).reshape(ROWS, 2, STEPS * GROUP, HEAD_SIZE)
    decoded = decode_attend(cached_row_lengths, group_live_rows, queries, decode_row_cache, decode_kv, (prior[2], prior[3]))
    decoded = jnp.transpose(decoded.reshape(ROWS, 2, STEPS, GROUP, HEAD_SIZE), (0, 2, 1, 3, 4))
    decode_attention = decoded.reshape(ROWS, STEPS, 2 * GROUP * HEAD_SIZE)

    far = jnp.arange(SIDE, dtype=jnp.int32)
    shard_z, shard_y = jnp.mod(my_z - far, SIDE), jnp.mod(my_y - far, SIDE)
    place = shard_z[:, None] * SIDE + shard_y[None, :]
    partner_sees = ((place < ctx) | ((place == ctx) & (pool == 0))).astype(jnp.int32).reshape(-1)
    own_sees = (place <= ctx).astype(jnp.int32).reshape(-1)
    earlier = [(p, k, None) for p in range(SIDE) for k in range(SIDE)]
    seen_first = earlier + [(SIDE, k, k) for k in range(SIDE)]
    first_blocks = (tuple(seen_first[:10]), tuple(seen_first[10:]))
    others = [(p, k, (p + 1) * SIDE + k) for p in range(SIDE - 1) for k in range(SIDE)]
    last_blocks = (tuple(others),)
    both = (0, 1)
    first_pieces = prior + [column]
    partner_queries = swap_pool(span_token_queries)
    own_state = attend(
        own_sees, span_token_queries, prior[0], first_pieces, first_blocks, column, both, diagonal=(SIDE, 0, 0)
    )
    partner_state = attend(partner_sees, partner_queries, prior[0], first_pieces, first_blocks, column, both)

    pages = TOKENS // BLK
    shard = ctx * 2 + pool
    partner_shard = ctx * 2 + 1 - pool
    page_ids = jnp.concatenate([shard * pages + jnp.arange(pages), partner_shard * pages + jnp.arange(pages)])
    block_ids = jnp.arange(block_target_page.shape[0], dtype=jnp.int32)
    source = jnp.sum(
        jnp.where(block_target_page[None, :] == page_ids[:, None], block_ids[None, :], 0), axis=1
    )
    source_shard = source // pages
    source_ctx = source_shard // 2
    where = jnp.stack(
        [
            jnp.mod(my_z - source_ctx // SIDE, SIDE),
            jnp.mod(my_y - source_ctx % SIDE, SIDE),
            source % pages,
        ]
    ).astype(jnp.int32)
    found = pick_pages(where, planes)
    from_partner = swap_pool(found[pages:])
    mine = (source_shard % 2 == pool)[:pages]
    handoff_pages = jnp.where(mine[:, None, None, None], found[:pages], from_partner)

    other = [
        swap_pool(
            attend(
                partner_sees,
                partner_queries,
                prior[0],
                planes[1:],
                last_blocks,
                None,
                (h,),
                state=partner_state,
                final=True,
                partner=True,
            )
        )
        for h in range(2)
    ]
    own = attend(
        own_sees, span_token_queries, prior[0], planes[1:], last_blocks, None, both, state=own_state, final=True
    )
    span_attention = combine(own, other)
    return (span_attention, handoff_pages, decode_attention)


def solution(mesh):
    in_specs = (
        P(("ctx", "pool"), "tp"),
        P(("ctx", "pool"), "tp"),
        P("tp", ("ctx", "pool"), None),
        P(("ctx", "pool"), None, "tp"),
        P(("ctx", "pool"), None, "tp"),
        P(("ctx", "pool"), "tp", None, None),
        P("tp", None),
        P("tp", None),
        P(),
        P(("ctx", "pool")),
        P(("ctx", "pool")),
        P(("ctx", "pool")),
        P(("ctx", "pool")),
        P(),
    )
    out_specs = (
        P(("ctx", "pool"), "tp"),
        P(("ctx", "pool"), "tp", None, None),
        P(("ctx", "pool"), None, "tp"),
    )
    return jax.shard_map(
        per_device, mesh=mesh, in_specs=in_specs, out_specs=out_specs, check_vma=False
    )
```

```python
import functools
import math

import jax
import jax.numpy as jnp
from jax import lax
from jax.experimental import pallas as pl
from jax.experimental.pallas import tpu as pltpu
from jax.sharding import PartitionSpec as P

HQ = 64
KEY_VALUE_HEADS = 8
HEAD_SIZE = 128
ADAPTER_RANK = 16
BLK = 16
STEPS = 4
GROUP = HQ // KEY_VALUE_HEADS
SHARDS = 16
SIDE = 4
TOKENS = 128
ROWS = 16
DECODE = ROWS * STEPS
ALL_ROWS = TOKENS + DECODE
LOG2_SCALE = math.log2(math.e) / math.sqrt(HEAD_SIZE)
neg_large = -1e30
MIB = 2**20
WIDTH = 2 * HEAD_SIZE


def estimate(us):
    return pl.CostEstimate(flops=int(us * 1.1e9), bytes_accessed=MIB, transcendentals=0)


def split3(x):
    hi = x.astype(jnp.bfloat16)
    rest = x - hi.astype(jnp.float32)
    mid = rest.astype(jnp.bfloat16)
    low = (rest - mid.astype(jnp.float32)).astype(jnp.bfloat16)
    return hi, mid, low

PROJECT_US, ATTEND_US, DECODE_US = 1, 3.4, 1
ATTEND_VMEM, PROJECT_VMEM, DECODE_VMEM = 24, 56, 24


CHUNKS = 4
OWNERS = (1, 3, 0, 2)


def project_kernel(
    tp_ref,
    row_adapter_ref,
    adapter_ref,
    span_ref,
    decode_ref,
    weight_ref,
    down_ref,
    up_ref,
    core_ref,
    kept_ref,
    hidden_ref,
    rank_ref,
    buffer_ref,
    decode_buffer,
    down_buffer,
    up_buffer,
    sems,
    small_sems,
):
    tp = tp_ref[0]
    depth = weight_ref.shape[0] // CHUNKS
    small = [
        pltpu.make_async_copy(span_ref, hidden_ref.at[pl.ds(0, TOKENS)], small_sems.at[0]),
        pltpu.make_async_copy(decode_ref, decode_buffer, small_sems.at[1]),
        pltpu.make_async_copy(down_ref, down_buffer, small_sems.at[2]),
        pltpu.make_async_copy(up_ref, up_buffer, small_sems.at[3]),
    ]
    for copy in small:
        copy.start()
    columns = [pl.multiple_of(jnp.bitwise_xor(tp, bit) * 2 * WIDTH, 2 * WIDTH) for bit in OWNERS]
    copies = [
        [
            pltpu.make_async_copy(
                weight_ref.at[pl.ds(k * depth, depth), pl.ds(column, 2 * WIDTH)],
                buffer_ref.at[i, pl.ds(k * depth, depth)],
                sems.at[i, k],
            )
            for k in range(CHUNKS)
        ]
        for i, column in enumerate(columns)
    ]
    for group in copies:
        for copy in group:
            copy.start()
    span_owner = jnp.transpose(jnp.broadcast_to(adapter_ref[...], (TOKENS, TOKENS)))
    row = lax.broadcasted_iota(jnp.int32, (DECODE, TOKENS), 0) // STEPS
    decode_owner = jnp.zeros((DECODE, TOKENS), jnp.int32)
    for r in range(ROWS):
        decode_owner = jnp.where(row == r, row_adapter_ref[r], decode_owner)
    owner = jnp.concatenate([span_owner, decode_owner], axis=0)
    column = lax.broadcasted_iota(jnp.int32, (ALL_ROWS, TOKENS), 1) // ADAPTER_RANK
    for copy in small:
        copy.wait()
    hidden_ref[TOKENS:, :] = decode_buffer[...].reshape(DECODE, decode_buffer.shape[2])
    narrow = jnp.dot(hidden_ref[...], down_buffer[...], preferred_element_type=jnp.float32)
    for part, piece in enumerate(split3(jnp.where(column == owner, narrow, 0.0))):
        rank_ref[:, part * TOKENS : (part + 1) * TOKENS] = piece
    for i, first in enumerate(columns):
        up = up_buffer[:, pl.ds(first, 2 * WIDTH)]
        out = jnp.dot(rank_ref[...], jnp.concatenate([up, up, up], axis=0), preferred_element_type=jnp.float32)
        for k in range(CHUNKS):
            copies[i][k].wait()
            here = slice(k * depth, (k + 1) * depth)
            out = out + jnp.dot(hidden_ref[:, here], buffer_ref[i, here, :], preferred_element_type=jnp.float32)
        out_ref = core_ref if i < 2 else kept_ref
        out_ref[2 * (i % 2)] = out[:, :WIDTH]
        out_ref[2 * (i % 2) + 1] = out[:, WIDTH:]


def project(tp, row_adapter, adapter, span, decode, weight, down, up):
    depth = span.shape[1]
    scalar = pl.BlockSpec(memory_space=pltpu.SMEM)
    local = pl.BlockSpec(memory_space=pltpu.VMEM)
    far = pl.BlockSpec(memory_space=pl.ANY)
    return pl.pallas_call(
        project_kernel,
        in_specs=[scalar, scalar, local] + [far] * 5,
        out_specs=[local] * 2,
        out_shape=[jax.ShapeDtypeStruct((4, ALL_ROWS, WIDTH), jnp.float32)] * 2,
        scratch_shapes=[
            pltpu.VMEM((ALL_ROWS, depth), jnp.bfloat16),
            pltpu.VMEM((ALL_ROWS, 3 * TOKENS), jnp.bfloat16),
            pltpu.VMEM((4, depth, 2 * WIDTH), jnp.bfloat16),
            pltpu.VMEM(decode.shape, jnp.bfloat16),
            pltpu.VMEM(down.shape, jnp.bfloat16),
            pltpu.VMEM(up.shape, jnp.bfloat16),
            pltpu.SemaphoreType.DMA((4, CHUNKS)),
            pltpu.SemaphoreType.DMA((4,)),
        ],
        compiler_params=pltpu.CompilerParams(vmem_limit_bytes=PROJECT_VMEM * MIB),
        cost_estimate=estimate(PROJECT_US),
        name="project",
    )(tp, row_adapter, adapter, span, decode, weight, down, up)


def finish_kernel(own_ref, chip_ref, queries_ref, *refs):
    span_ref, decode_ref, late_ref = refs[-3:]
    late_ref[...] = queries_ref[...]
    total = (own_ref[...] + chip_ref[...]).astype(jnp.bfloat16)
    span_ref[...] = total[:, :TOKENS]
    decode_ref[...] = total[:, TOKENS:]


def finish(own_sum, from_chip, queries, after):
    heads, _, width = from_chip.shape
    local = pl.BlockSpec(memory_space=pltpu.VMEM)
    return pl.pallas_call(
        finish_kernel,
        in_specs=[local] * 3 + [pl.BlockSpec(memory_space=pl.ANY)] * len(after),
        out_specs=[local] * 3,
        out_shape=[
            jax.ShapeDtypeStruct((heads, TOKENS, width), jnp.bfloat16),
            jax.ShapeDtypeStruct((heads, DECODE, width), jnp.bfloat16),
            jax.ShapeDtypeStruct(queries.shape, jnp.bfloat16),
        ],
        compiler_params=pltpu.CompilerParams(vmem_limit_bytes=8 * MIB),
        cost_estimate=estimate(0.5),
        name="finish",
    )(own_sum, from_chip, queries, *after)


TILE = 2
TILE_ROWS = TILE * TOKENS
TILES = GROUP // TILE
HEAD_ROWS = GROUP * TOKENS
HEAD_COLUMNS = GROUP * HEAD_SIZE


def attend_kernel(heads, blocks, diagonal, has_state, final, partner, visible_ref, q_ref, known_ref, *refs):
    pieces, refs = refs[:-4], refs[-4:]
    state_ref, out_ref, key_ref, ext_ref = refs
    wide = lax.broadcasted_iota(jnp.int32, (TILE_ROWS, HEAD_SIZE), 1)
    lane = wide[:TOKENS]
    one = jnp.ones((TOKENS, HEAD_SIZE), jnp.bfloat16)
    zero = jnp.zeros((TOKENS, HEAD_SIZE), jnp.bfloat16)
    bounds = [0]
    for shards in blocks:
        bounds.append(bounds[-1] + len(shards) * TOKENS)
    for slot, h in enumerate(heads):
        for b, shards in enumerate(blocks):
            for n, (piece, index, place) in enumerate(shards):
                kv = pieces[piece][index, h]
                keys, values, ones = kv[:, :HEAD_SIZE], kv[:, HEAD_SIZE:], one
                if place is not None:
                    seen = visible_ref[place] != 0
                    keys = jnp.where(seen, keys, known_ref[0, h, :, :HEAD_SIZE])
                    values = jnp.where(seen, values, zero)
                    ones = jnp.where(seen, one, zero)
                here = slice(bounds[b] + n * TOKENS, bounds[b] + (n + 1) * TOKENS)
                key_ref[slot, here, :] = keys
                ext_ref[slot, here, :HEAD_SIZE] = values
                ext_ref[slot, here, HEAD_SIZE:] = ones
        queries = [
            jnp.concatenate(
                [
                    q_ref[:, h * HEAD_COLUMNS + g * HEAD_SIZE : h * HEAD_COLUMNS + (g + 1) * HEAD_SIZE]
                    for g in range(i * TILE, (i + 1) * TILE)
                ],
                axis=0,
            )
            for i in range(TILES)
        ]

        def score(i, b):
            scores = lax.dot_general(
                queries[i],
                key_ref[slot, bounds[b] : bounds[b + 1], :],
                (((1,), (1,)), ((), ())),
                preferred_element_type=jnp.float32,
            )
            if diagonal is not None and diagonal in blocks[b]:
                at = blocks[b].index(diagonal) * TOKENS
                token = lax.broadcasted_iota(jnp.int32, (TILE_ROWS, TOKENS), 0) % TOKENS
                parts = [scores[:, :at]] if at else []
                parts.append(jnp.where(wide <= token, scores[:, at : at + TOKENS], neg_large))
                if at + TOKENS < scores.shape[1]:
                    parts.append(scores[:, at + TOKENS :])
                scores = jnp.concatenate(parts, axis=1)
            return scores, jnp.max(scores, axis=1, keepdims=True) * LOG2_SCALE

        steps = [(i, b) for i in range(TILES) for b in range(len(blocks))]
        if final:
            stats = jnp.zeros((TOKENS, HEAD_SIZE), out_ref.dtype)
        coming = score(*steps[0])
        for n, (i, b) in enumerate(steps):
            scores, top = coming
            if n + 1 < len(steps):
                coming = score(*steps[n + 1])
            here = slice(i * TILE_ROWS, (i + 1) * TILE_ROWS)
            if b or has_state:
                if not b:
                    top_before = state_ref[h, here, HEAD_SIZE : HEAD_SIZE + 1]
                    total = jnp.concatenate(
                        [
                            state_ref[h, here, :HEAD_SIZE],
                            jnp.broadcast_to(state_ref[h, here, WIDTH - 1 :], (TILE_ROWS, HEAD_SIZE)),
                        ],
                        axis=1,
                    )
                top = jnp.maximum(top_before, top)
                total = total * jnp.exp2(top_before - top)
            weights = jnp.exp2(scores * LOG2_SCALE - top).astype(jnp.bfloat16)
            added = jnp.dot(
                weights, ext_ref[slot, bounds[b] : bounds[b + 1], :], preferred_element_type=jnp.float32
            )
            total = total + added if b or has_state else added
            top_before = top
            if b < len(blocks) - 1:
                continue
            if not final:
                out_ref[slot, here, :HEAD_SIZE] = total[:, :HEAD_SIZE]
                out_ref[slot, here, HEAD_SIZE:] = jnp.where(wide < HEAD_SIZE // 2, top, total[:, HEAD_SIZE:])
                continue
            out = total[:, :HEAD_SIZE] / total[:, HEAD_SIZE:]
            level = top + jnp.log2(total[:, HEAD_SIZE:])
            for j in range(TILE):
                g = i * TILE + j
                own = slice(j * TOKENS, (j + 1) * TOKENS)
                out_ref[slot, :, g * HEAD_SIZE : (g + 1) * HEAD_SIZE] = out[own].astype(out_ref.dtype)
                parts = split3(level[own]) if partner else (level[own],)
                for part, piece in enumerate(parts):
                    stats = jnp.where(lane == part * GROUP + g, piece, stats)
        if final:
            out_ref[slot, :, HEAD_COLUMNS:] = stats


def attend(visible, queries, known, pieces, blocks, after, heads, diagonal=None, state=None, final=False, partner=False):
    shards = sum(len(block) for block in blocks)
    count = len(heads)
    if final:
        out_shape = (count, TOKENS, HEAD_COLUMNS + HEAD_SIZE)
    else:
        out_shape = (count, HEAD_ROWS, WIDTH)
    local = pl.BlockSpec(memory_space=pltpu.VMEM)
    return pl.pallas_call(
        functools.partial(attend_kernel, heads, blocks, diagonal, state is not None, final, partner),
        in_specs=[pl.BlockSpec(memory_space=pltpu.SMEM)]
        + [local] * (2 + len(pieces))
        + [pl.BlockSpec(memory_space=pl.ANY) if state is None else local],
        out_specs=local,
        scratch_shapes=[
            pltpu.VMEM((count, shards * TOKENS, HEAD_SIZE), jnp.bfloat16),
            pltpu.VMEM((count, shards * TOKENS, WIDTH), jnp.bfloat16),
        ],
        out_shape=jax.ShapeDtypeStruct(out_shape, jnp.bfloat16 if partner and final else jnp.float32),
        compiler_params=pltpu.CompilerParams(vmem_limit_bytes=ATTEND_VMEM * MIB),
        cost_estimate=estimate(ATTEND_US * count * shards / 16),
        name="attend_last" if final else "attend_first",
    )(visible, queries, known, *pieces, after if state is None else state)


def combine_kernel(*refs):
    own_ref, out_ref = refs[0], refs[3]
    for h in range(2):
        other_ref = refs[1 + h]
        own_level = own_ref[h, :, HEAD_COLUMNS:]
        other_parts = other_ref[0, :, HEAD_COLUMNS:].astype(jnp.float32)
        for g in range(GROUP):
            mine = own_level[:, g : g + 1]
            theirs = (
                other_parts[:, g : g + 1]
                + other_parts[:, GROUP + g : GROUP + g + 1]
                + other_parts[:, 2 * GROUP + g : 2 * GROUP + g + 1]
            )
            peak = jnp.maximum(mine, theirs)
            mine = jnp.exp2(mine - peak)
            theirs = jnp.exp2(theirs - peak)
            whole = mine + theirs
            columns = slice(g * HEAD_SIZE, (g + 1) * HEAD_SIZE)
            mixed = (mine / whole) * own_ref[h, :, columns] + (theirs / whole) * other_ref[0, :, columns].astype(
                jnp.float32
            )
            out_ref[:, h * HEAD_COLUMNS + g * HEAD_SIZE : h * HEAD_COLUMNS + (g + 1) * HEAD_SIZE] = mixed.astype(
                jnp.bfloat16
            )


def combine(own, other):
    return pl.pallas_call(
        combine_kernel,
        out_shape=jax.ShapeDtypeStruct((TOKENS, 2 * HEAD_COLUMNS), jnp.bfloat16),
        compiler_params=pltpu.CompilerParams(vmem_limit_bytes=16 * MIB),
        cost_estimate=estimate(1),
        name="combine",
    )(own, *other)


ROW_BLOCK = 8


def decode_kernel(length_ref, live_ref, q_ref, cache_ref, fresh_ref, *refs):
    out_ref = refs[-1]
    first = pl.program_id(0) * ROW_BLOCK
    query_rows = STEPS * GROUP
    rows = ROW_BLOCK * query_rows
    contract = (((1,), (1,)), ((), ()))
    slot = lax.broadcasted_iota(jnp.int32, (query_rows, cache_ref.shape[2]), 1)
    fresh_row = lax.broadcasted_iota(jnp.int32, (rows, DECODE), 1) // STEPS
    fresh_step = lax.broadcasted_iota(jnp.int32, (rows, DECODE), 1) % STEPS
    row = lax.broadcasted_iota(jnp.int32, (rows, DECODE), 0) // query_rows
    step = lax.broadcasted_iota(jnp.int32, (rows, DECODE), 0) % query_rows // GROUP
    fresh_seen = (fresh_row == row + first) & (fresh_step <= step)
    cached, fresh = [], []
    for h in range(2):
        scores = lax.dot_general(
            q_ref[:, h].reshape(rows, HEAD_SIZE),
            fresh_ref[h, :, :HEAD_SIZE],
            contract,
            preferred_element_type=jnp.float32,
        )
        fresh.append(jnp.where(fresh_seen, scores, neg_large))
        for n in range(ROW_BLOCK):
            scores = lax.dot_general(
                q_ref[n, h], cache_ref[n, h, :, :HEAD_SIZE], contract, preferred_element_type=jnp.float32
            )
            cached.append(jnp.where(slot < length_ref[first + n], scores, neg_large))
    cached = jnp.concatenate(cached, axis=0)
    fresh = jnp.concatenate(fresh, axis=0)
    top = jnp.maximum(jnp.max(cached, axis=1, keepdims=True), jnp.max(fresh, axis=1, keepdims=True))
    cached = jnp.exp2((cached - top) * LOG2_SCALE)
    fresh = jnp.exp2((fresh - top) * LOG2_SCALE)
    total = jnp.sum(cached, axis=1, keepdims=True) + jnp.sum(fresh, axis=1, keepdims=True)
    cached = cached.astype(jnp.bfloat16)
    fresh = fresh.astype(jnp.bfloat16)
    for h in range(2):
        of_fresh = jnp.dot(
            fresh[h * rows : (h + 1) * rows], fresh_ref[h, :, HEAD_SIZE:], preferred_element_type=jnp.float32
        )
        for n in range(ROW_BLOCK):
            here = slice(h * rows + n * query_rows, h * rows + (n + 1) * query_rows)
            out = jnp.dot(cached[here], cache_ref[n, h, :, HEAD_SIZE:], preferred_element_type=jnp.float32)
            out = (out + of_fresh[n * query_rows : (n + 1) * query_rows]) / total[here]
            out_ref[n, h] = jnp.where(first + n < live_ref[0], out, 0.0).astype(jnp.bfloat16)


def decode_attend(lengths, live, queries, cache, fresh, after):
    rows, heads, query_rows, _ = queries.shape
    cache_size = cache.shape[2]
    return pl.pallas_call(
        decode_kernel,
        grid_spec=pltpu.PrefetchScalarGridSpec(
            num_scalar_prefetch=2,
            grid=(rows // ROW_BLOCK,),
            in_specs=[
                pl.BlockSpec((ROW_BLOCK, heads, query_rows, HEAD_SIZE), lambda i, *_: (i, 0, 0, 0)),
                pl.BlockSpec((ROW_BLOCK, heads, cache_size, 2 * HEAD_SIZE), lambda i, *_: (i, 0, 0, 0)),
                pl.BlockSpec((heads, DECODE, 2 * HEAD_SIZE), lambda i, *_: (0, 0, 0)),
            ]
            + [pl.BlockSpec(memory_space=pl.ANY)] * len(after),
            out_specs=pl.BlockSpec((ROW_BLOCK, heads, query_rows, HEAD_SIZE), lambda i, *_: (i, 0, 0, 0)),
        ),
        out_shape=jax.ShapeDtypeStruct(queries.shape, jnp.bfloat16),
        compiler_params=pltpu.CompilerParams(vmem_limit_bytes=DECODE_VMEM * MIB),
        cost_estimate=estimate(DECODE_US),
        name="decode",
    )(lengths, live, queries, cache, fresh, *after)


def pages_kernel(where_ref, column_ref, up_ref, down_ref, *refs):
    ring_refs, out_ref = refs[:SIDE], refs[SIDE]
    for n in range(out_ref.shape[0]):
        dz, dy = where_ref[0, n], where_ref[1, n]
        rows = pl.ds(pl.multiple_of(where_ref[2, n] * BLK, BLK), BLK)
        for h in range(2):
            page = column_ref[dy, h, rows, :]
            page = jnp.where(dz == 1, up_ref[dy, h, rows, :], page)
            page = jnp.where(dz == 3, down_ref[dy, h, rows, :], page)
            for k in range(SIDE):
                page = jnp.where((dz == 2) & (dy == k), ring_refs[k][1, h, rows, :], page)
            out_ref[n, h] = page


def pick_pages(where, column, up, down, rings):
    count = where.shape[1]
    local = pl.BlockSpec(memory_space=pltpu.VMEM)
    return pl.pallas_call(
        pages_kernel,
        in_specs=[pl.BlockSpec(memory_space=pltpu.SMEM)] + [local] * (3 + SIDE),
        out_specs=local,
        out_shape=jax.ShapeDtypeStruct((count, 2, BLK, WIDTH), jnp.bfloat16),
        compiler_params=pltpu.CompilerParams(vmem_limit_bytes=16 * MIB),
        cost_estimate=estimate(1),
        name="pages",
    )(where, column, up, down, *rings)


def shift(x, dz, dy):
    perm = [
        (z * SIDE + y, ((z + dz) % SIDE) * SIDE + (y + dy) % SIDE) for z in range(SIDE) for y in range(SIDE)
    ]
    return lax.ppermute(x, "ctx", perm)


def swap_pool(x):
    return lax.ppermute(x, "pool", [(0, 1), (1, 0)])


def swap_tp(x, bit):
    return lax.ppermute(x, "tp", [(i, i ^ bit) for i in range(4)])


def gather(x):
    pair = jnp.stack([x, shift(x, 2, 0)])
    far = {1: shift(pair, 0, 1), 3: shift(pair, 0, 3), 2: shift(pair, 0, 2)}
    rings = [pair, far[1], far[2], far[3]]
    column = jnp.stack([r[0] for r in rings])
    return column, shift(column, 1, 0), shift(column, 3, 0), rings


def per_device(
    span_hidden_states,
    span_token_queries,
    earlier_key_values,
    decode_hidden_states,
    decode_token_queries,
    decode_row_cache,
    key_value_weight,
    adapter_down_weight,
    adapter_up_weight,
    prompt_adapter,
    row_adapter_index,
    group_live_rows,
    cached_row_lengths,
    block_target_page,
):
    tp = lax.axis_index("tp")
    ctx = lax.axis_index("ctx")
    pool = lax.axis_index("pool")
    my_z, my_y = ctx // SIDE, ctx % SIDE

    prior_column, prior_up, prior_down, prior_rings = gather(earlier_key_values)

    for_core, kept = project(
        tp.astype(jnp.int32).reshape(1),
        row_adapter_index,
        prompt_adapter.reshape(1, TOKENS),
        span_hidden_states,
        decode_hidden_states,
        key_value_weight,
        adapter_down_weight,
        adapter_up_weight,
    )
    from_core = swap_tp(for_core, 1)
    from_chip = swap_tp(kept[2:] + from_core[2:], 2)
    span_kv, decode_kv, late_queries = finish(
        kept[:2] + from_core[:2], from_chip, span_token_queries, (prior_rings[0],)
    )

    column, up, down, rings = gather(span_kv)

    queries = decode_token_queries.reshape(ROWS, STEPS, 2, GROUP, HEAD_SIZE)
    queries = jnp.transpose(queries, (0, 2, 1, 3, 4)).reshape(ROWS, 2, STEPS * GROUP, HEAD_SIZE)
    decoded = decode_attend(cached_row_lengths, group_live_rows, queries, decode_row_cache, decode_kv, ())
    decoded = jnp.transpose(decoded.reshape(ROWS, 2, STEPS, GROUP, HEAD_SIZE), (0, 2, 1, 3, 4))
    decode_attention = decoded.reshape(ROWS, STEPS, 2 * GROUP * HEAD_SIZE)

    far = jnp.arange(SIDE, dtype=jnp.int32)
    shard_z, shard_y = jnp.mod(my_z - far, SIDE), jnp.mod(my_y - far, SIDE)
    place = shard_z[:, None] * SIDE + shard_y[None, :]
    partner_sees = ((place < ctx) | ((place == ctx) & (pool == 0))).astype(jnp.int32).reshape(-1)
    own_sees = (place <= ctx).astype(jnp.int32).reshape(-1)
    prior_pieces = [prior_up, prior_down] + prior_rings
    earlier = [(p, k, None) for p in range(2) for k in range(SIDE)]
    earlier += [(2 + k, j, None) for j in range(2) for k in range(SIDE)]

    def pairs(first):
        return [(first + k, j, 2 * j * SIDE + k) for j in range(2) for k in range(SIDE)]

    sides = [(p, k, (1 + 2 * p) * SIDE + k) for p in range(2) for k in range(SIDE)]
    both = (0, 1)
    partner_queries = swap_pool(late_queries)
    own_state = attend(
        own_sees, span_token_queries, prior_up, prior_pieces, (tuple(earlier[:8]), tuple(earlier[8:])), column, both
    )
    partner_state = attend(
        partner_sees,
        partner_queries,
        prior_up,
        prior_pieces + rings,
        (tuple(earlier[:12]), tuple(earlier[12:] + pairs(6))),
        own_state,
        both,
    )

    pages = TOKENS // BLK
    shard = ctx * 2 + pool
    partner_shard = ctx * 2 + 1 - pool
    page_ids = jnp.concatenate([shard * pages + jnp.arange(pages), partner_shard * pages + jnp.arange(pages)])
    block_ids = jnp.arange(block_target_page.shape[0], dtype=jnp.int32)
    source = jnp.sum(
        jnp.where(block_target_page[None, :] == page_ids[:, None], block_ids[None, :], 0), axis=1
    )
    source_shard = source // pages
    source_ctx = source_shard // 2
    where = jnp.stack(
        [
            jnp.mod(my_z - source_ctx // SIDE, SIDE),
            jnp.mod(my_y - source_ctx % SIDE, SIDE),
            source % pages,
        ]
    ).astype(jnp.int32)
    found = pick_pages(where, column, up, down, rings)
    from_partner = swap_pool(found[pages:])
    mine = (source_shard % 2 == pool)[:pages]
    handoff_pages = jnp.where(mine[:, None, None, None], found[:pages], from_partner)

    other = [
        swap_pool(
            attend(
                partner_sees,
                partner_queries,
                prior_up,
                [up, down],
                (tuple(sides),),
                None,
                (h,),
                state=partner_state,
                final=True,
                partner=True,
            )
        )
        for h in range(2)
    ]
    own = attend(
        own_sees,
        span_token_queries,
        prior_up,
        [up, down] + rings,
        (tuple(pairs(2)), tuple(sides)),
        None,
        both,
        diagonal=(2, 0, 0),
        state=own_state,
        final=True,
    )
    span_attention = combine(own, other)
    return (span_attention, handoff_pages, decode_attention)


def solution(mesh):
    in_specs = (
        P(("ctx", "pool"), "tp"),
        P(("ctx", "pool"), "tp"),
        P("tp", ("ctx", "pool"), None),
        P(("ctx", "pool"), None, "tp"),
        P(("ctx", "pool"), None, "tp"),
        P(("ctx", "pool"), "tp", None, None),
        P("tp", None),
        P("tp", None),
        P(),
        P(("ctx", "pool")),
        P(("ctx", "pool")),
        P(("ctx", "pool")),
        P(("ctx", "pool")),
        P(),
    )
    out_specs = (
        P(("ctx", "pool"), "tp"),
        P(("ctx", "pool"), "tp", None, None),
        P(("ctx", "pool"), None, "tp"),
    )
    return jax.shard_map(
        per_device, mesh=mesh, in_specs=in_specs, out_specs=out_specs, check_vma=False
    )
```

```python
import functools
import math

import jax
import jax.numpy as jnp
from jax import lax
from jax.experimental import pallas as pl
from jax.experimental.pallas import tpu as pltpu
from jax.sharding import PartitionSpec as P

HQ = 64
KEY_VALUE_HEADS = 8
HEAD_SIZE = 128
ADAPTER_RANK = 16
BLK = 16
STEPS = 4
GROUP = HQ // KEY_VALUE_HEADS
SHARDS = 16
SIDE = 4
TOKENS = 128
ROWS = 16
DECODE = ROWS * STEPS
ALL_ROWS = TOKENS + DECODE
LOG2_SCALE = math.log2(math.e) / math.sqrt(HEAD_SIZE)
neg_large = -1e30
MIB = 2**20
WIDTH = 2 * HEAD_SIZE


def estimate(us):
    return pl.CostEstimate(flops=int(us * 1.1e9), bytes_accessed=MIB, transcendentals=0)


def split3(x):
    hi = x.astype(jnp.bfloat16)
    rest = x - hi.astype(jnp.float32)
    mid = rest.astype(jnp.bfloat16)
    low = (rest - mid.astype(jnp.float32)).astype(jnp.bfloat16)
    return hi, mid, low

PROJECT_US, ATTEND_US, DECODE_US = 1, 3.4, 1
ATTEND_VMEM, PROJECT_VMEM, DECODE_VMEM = 24, 56, 24


CHUNKS = 4
OWNERS = (1, 3, 0, 2)


def project_kernel(
    tp_ref,
    row_adapter_ref,
    adapter_ref,
    span_ref,
    decode_ref,
    weight_ref,
    down_ref,
    up_ref,
    core_ref,
    kept_ref,
    hidden_ref,
    rank_ref,
    buffer_ref,
    decode_buffer,
    down_buffer,
    up_buffer,
    sems,
    small_sems,
):
    tp = tp_ref[0]
    depth = weight_ref.shape[0] // CHUNKS
    small = [
        pltpu.make_async_copy(span_ref, hidden_ref.at[pl.ds(0, TOKENS)], small_sems.at[0]),
        pltpu.make_async_copy(decode_ref, decode_buffer, small_sems.at[1]),
        pltpu.make_async_copy(down_ref, down_buffer, small_sems.at[2]),
        pltpu.make_async_copy(up_ref, up_buffer, small_sems.at[3]),
    ]
    for copy in small:
        copy.start()
    columns = [pl.multiple_of(jnp.bitwise_xor(tp, bit) * 2 * WIDTH, 2 * WIDTH) for bit in OWNERS]
    copies = [
        [
            pltpu.make_async_copy(
                weight_ref.at[pl.ds(k * depth, depth), pl.ds(column, 2 * WIDTH)],
                buffer_ref.at[i, pl.ds(k * depth, depth)],
                sems.at[i, k],
            )
            for k in range(CHUNKS)
        ]
        for i, column in enumerate(columns)
    ]
    for group in copies:
        for copy in group:
            copy.start()
    span_owner = jnp.transpose(jnp.broadcast_to(adapter_ref[...], (TOKENS, TOKENS)))
    row = lax.broadcasted_iota(jnp.int32, (DECODE, TOKENS), 0) // STEPS
    decode_owner = jnp.zeros((DECODE, TOKENS), jnp.int32)
    for r in range(ROWS):
        decode_owner = jnp.where(row == r, row_adapter_ref[r], decode_owner)
    owner = jnp.concatenate([span_owner, decode_owner], axis=0)
    column = lax.broadcasted_iota(jnp.int32, (ALL_ROWS, TOKENS), 1) // ADAPTER_RANK
    for copy in small:
        copy.wait()
    hidden_ref[TOKENS:, :] = decode_buffer[...].reshape(DECODE, decode_buffer.shape[2])
    narrow = jnp.dot(hidden_ref[...], down_buffer[...], preferred_element_type=jnp.float32)
    for part, piece in enumerate(split3(jnp.where(column == owner, narrow, 0.0))):
        rank_ref[:, part * TOKENS : (part + 1) * TOKENS] = piece
    for i, first in enumerate(columns):
        up = up_buffer[:, pl.ds(first, 2 * WIDTH)]
        out = jnp.dot(rank_ref[...], jnp.concatenate([up, up, up], axis=0), preferred_element_type=jnp.float32)
        for k in range(CHUNKS):
            copies[i][k].wait()
            here = slice(k * depth, (k + 1) * depth)
            out = out + jnp.dot(hidden_ref[:, here], buffer_ref[i, here, :], preferred_element_type=jnp.float32)
        out_ref = core_ref if i < 2 else kept_ref
        out_ref[2 * (i % 2)] = out[:, :WIDTH]
        out_ref[2 * (i % 2) + 1] = out[:, WIDTH:]


def project(tp, row_adapter, adapter, span, decode, weight, down, up):
    depth = span.shape[1]
    scalar = pl.BlockSpec(memory_space=pltpu.SMEM)
    local = pl.BlockSpec(memory_space=pltpu.VMEM)
    far = pl.BlockSpec(memory_space=pl.ANY)
    return pl.pallas_call(
        project_kernel,
        in_specs=[scalar, scalar, local] + [far] * 5,
        out_specs=[local] * 2,
        out_shape=[jax.ShapeDtypeStruct((4, ALL_ROWS, WIDTH), jnp.float32)] * 2,
        scratch_shapes=[
            pltpu.VMEM((ALL_ROWS, depth), jnp.bfloat16),
            pltpu.VMEM((ALL_ROWS, 3 * TOKENS), jnp.bfloat16),
            pltpu.VMEM((4, depth, 2 * WIDTH), jnp.bfloat16),
            pltpu.VMEM(decode.shape, jnp.bfloat16),
            pltpu.VMEM(down.shape, jnp.bfloat16),
            pltpu.VMEM(up.shape, jnp.bfloat16),
            pltpu.SemaphoreType.DMA((4, CHUNKS)),
            pltpu.SemaphoreType.DMA((4,)),
        ],
        compiler_params=pltpu.CompilerParams(vmem_limit_bytes=PROJECT_VMEM * MIB),
        cost_estimate=estimate(PROJECT_US),
        name="project",
    )(tp, row_adapter, adapter, span, decode, weight, down, up)


def finish_kernel(own_ref, chip_ref, queries_ref, *refs):
    span_ref, decode_ref, late_ref = refs[-3:]
    late_ref[...] = queries_ref[...]
    total = (own_ref[...] + chip_ref[...]).astype(jnp.bfloat16)
    span_ref[...] = total[:, :TOKENS]
    decode_ref[...] = total[:, TOKENS:]


def finish(own_sum, from_chip, queries, after):
    heads, _, width = from_chip.shape
    local = pl.BlockSpec(memory_space=pltpu.VMEM)
    return pl.pallas_call(
        finish_kernel,
        in_specs=[local] * 3 + [pl.BlockSpec(memory_space=pl.ANY)] * len(after),
        out_specs=[local] * 3,
        out_shape=[
            jax.ShapeDtypeStruct((heads, TOKENS, width), jnp.bfloat16),
            jax.ShapeDtypeStruct((heads, DECODE, width), jnp.bfloat16),
            jax.ShapeDtypeStruct(queries.shape, jnp.bfloat16),
        ],
        compiler_params=pltpu.CompilerParams(vmem_limit_bytes=8 * MIB),
        cost_estimate=estimate(0.5),
        name="finish",
    )(own_sum, from_chip, queries, *after)


TILE = 2
TILE_ROWS = TILE * TOKENS
TILES = GROUP // TILE
HEAD_ROWS = GROUP * TOKENS
HEAD_COLUMNS = GROUP * HEAD_SIZE


def pick_pages(where_ref, column_ref, up_ref, down_ref, ring_refs, own_ref, other_ref, at):
    count = own_ref.shape[0]
    for n in range(2 * count):
        dz, dy = where_ref[0, n], where_ref[1, n]
        rows = pl.ds(pl.multiple_of(where_ref[2, n] * BLK, BLK), BLK)
        for h in range(2):
            page = column_ref[dy, h, rows, :]
            page = jnp.where(dz == 1, up_ref[dy, h, rows, :], page)
            page = jnp.where(dz == 3, down_ref[dy, h, rows, :], page)
            for k in range(SIDE):
                page = jnp.where((dz == 2) & (dy == k), ring_refs[k][1, h, rows, :], page)
            if n < count:
                own_ref[n, h] = page
            else:
                here = slice((n - count) * BLK, (n - count + 1) * BLK)
                other_ref[0, here, at + h * WIDTH : at + (h + 1) * WIDTH] = page


def attend_kernel(
    heads, count, blocks, diagonal, has_state, final, partner, has_pages, visible_ref, q_ref, known_ref, *refs
):
    pieces, state_ref, refs = refs[:count], refs[count], refs[count + 1 :]
    out_ref = refs[-4] if has_pages else refs[-3]
    key_ref, ext_ref = refs[-2:]
    if has_pages:
        pick_pages(
            refs[0],
            refs[1],
            pieces[0],
            pieces[1],
            refs[2 : 2 + SIDE],
            refs[-3],
            out_ref,
            HEAD_COLUMNS + HEAD_SIZE,
        )
    wide = lax.broadcasted_iota(jnp.int32, (TILE_ROWS, HEAD_SIZE), 1)
    lane = wide[:TOKENS]
    one = jnp.ones((TOKENS, HEAD_SIZE), jnp.bfloat16)
    zero = jnp.zeros((TOKENS, HEAD_SIZE), jnp.bfloat16)
    bounds = [0]
    for shards in blocks:
        bounds.append(bounds[-1] + len(shards) * TOKENS)
    for slot, h in enumerate(heads):
        for b, shards in enumerate(blocks):
            for n, (piece, index, place) in enumerate(shards):
                kv = pieces[piece][index, h]
                keys, values, ones = kv[:, :HEAD_SIZE], kv[:, HEAD_SIZE:], one
                if place is not None:
                    seen = visible_ref[place] != 0
                    keys = jnp.where(seen, keys, known_ref[0, h, :, :HEAD_SIZE])
                    values = jnp.where(seen, values, zero)
                    ones = jnp.where(seen, one, zero)
                here = slice(bounds[b] + n * TOKENS, bounds[b] + (n + 1) * TOKENS)
                key_ref[slot, here, :] = keys
                ext_ref[slot, here, :HEAD_SIZE] = values
                ext_ref[slot, here, HEAD_SIZE:] = ones
        queries = [
            jnp.concatenate(
                [
                    q_ref[:, h * HEAD_COLUMNS + g * HEAD_SIZE : h * HEAD_COLUMNS + (g + 1) * HEAD_SIZE]
                    for g in range(i * TILE, (i + 1) * TILE)
                ],
                axis=0,
            )
            for i in range(TILES)
        ]

        def score(i, b):
            scores = lax.dot_general(
                queries[i],
                key_ref[slot, bounds[b] : bounds[b + 1], :],
                (((1,), (1,)), ((), ())),
                preferred_element_type=jnp.float32,
            )
            if diagonal is not None and diagonal in blocks[b]:
                at = blocks[b].index(diagonal) * TOKENS
                token = lax.broadcasted_iota(jnp.int32, (TILE_ROWS, TOKENS), 0) % TOKENS
                parts = [scores[:, :at]] if at else []
                parts.append(jnp.where(wide <= token, scores[:, at : at + TOKENS], neg_large))
                if at + TOKENS < scores.shape[1]:
                    parts.append(scores[:, at + TOKENS :])
                scores = jnp.concatenate(parts, axis=1)
            return scores, jnp.max(scores, axis=1, keepdims=True) * LOG2_SCALE

        steps = [(i, b) for i in range(TILES) for b in range(len(blocks))]
        if final:
            stats = jnp.zeros((TOKENS, HEAD_SIZE), out_ref.dtype)
        coming = score(*steps[0])
        for n, (i, b) in enumerate(steps):
            scores, top = coming
            if n + 1 < len(steps):
                coming = score(*steps[n + 1])
            here = slice(i * TILE_ROWS, (i + 1) * TILE_ROWS)
            if b or has_state:
                if not b:
                    top_before = state_ref[h, here, HEAD_SIZE : HEAD_SIZE + 1]
                    total = jnp.concatenate(
                        [
                            state_ref[h, here, :HEAD_SIZE],
                            jnp.broadcast_to(state_ref[h, here, WIDTH - 1 :], (TILE_ROWS, HEAD_SIZE)),
                        ],
                        axis=1,
                    )
                top = jnp.maximum(top_before, top)
                total = total * jnp.exp2(top_before - top)
            weights = jnp.exp2(scores * LOG2_SCALE - top).astype(jnp.bfloat16)
            added = jnp.dot(
                weights, ext_ref[slot, bounds[b] : bounds[b + 1], :], preferred_element_type=jnp.float32
            )
            total = total + added if b or has_state else added
            top_before = top
            if b < len(blocks) - 1:
                continue
            if not final:
                out_ref[slot, here, :HEAD_SIZE] = total[:, :HEAD_SIZE]
                out_ref[slot, here, HEAD_SIZE:] = jnp.where(wide < HEAD_SIZE // 2, top, total[:, HEAD_SIZE:])
                continue
            out = total[:, :HEAD_SIZE] / total[:, HEAD_SIZE:]
            level = top + jnp.log2(total[:, HEAD_SIZE:])
            for j in range(TILE):
                g = i * TILE + j
                own = slice(j * TOKENS, (j + 1) * TOKENS)
                out_ref[slot, :, g * HEAD_SIZE : (g + 1) * HEAD_SIZE] = out[own].astype(out_ref.dtype)
                parts = split3(level[own]) if partner else (level[own],)
                for part, piece in enumerate(parts):
                    stats = jnp.where(lane == part * GROUP + g, piece, stats)
        if final:
            out_ref[slot, :, HEAD_COLUMNS : HEAD_COLUMNS + HEAD_SIZE] = stats


def attend(
    visible,
    queries,
    known,
    pieces,
    blocks,
    after,
    heads,
    diagonal=None,
    state=None,
    final=False,
    partner=False,
    page_source=None,
    before=(),
):
    shards = sum(len(block) for block in blocks)
    count = len(heads)
    if final:
        out_shape = (count, TOKENS, HEAD_COLUMNS + HEAD_SIZE + (0 if page_source is None else 2 * WIDTH))
    else:
        out_shape = (count, HEAD_ROWS, WIDTH)
    local = pl.BlockSpec(memory_space=pltpu.VMEM)
    scalar = pl.BlockSpec(memory_space=pltpu.SMEM)
    out_shape = jax.ShapeDtypeStruct(out_shape, jnp.bfloat16 if partner and final else jnp.float32)
    out_specs = local
    more, more_specs = [], []
    if page_source is not None:
        own_pages = jax.ShapeDtypeStruct((TOKENS // BLK, 2, BLK, WIDTH), jnp.bfloat16)
        out_shape, out_specs = [out_shape, own_pages], [local, local]
        more, more_specs = list(page_source), [scalar] + [local] * (len(page_source) - 1)
    more += before
    more_specs += [pl.BlockSpec(memory_space=pl.ANY)] * len(before)
    return pl.pallas_call(
        functools.partial(
            attend_kernel,
            heads,
            len(pieces),
            blocks,
            diagonal,
            state is not None,
            final,
            partner,
            page_source is not None,
        ),
        in_specs=[scalar]
        + [local] * (2 + len(pieces))
        + [pl.BlockSpec(memory_space=pl.ANY) if state is None else local]
        + more_specs,
        out_specs=out_specs,
        scratch_shapes=[
            pltpu.VMEM((count, shards * TOKENS, HEAD_SIZE), jnp.bfloat16),
            pltpu.VMEM((count, shards * TOKENS, WIDTH), jnp.bfloat16),
        ],
        out_shape=out_shape,
        compiler_params=pltpu.CompilerParams(vmem_limit_bytes=ATTEND_VMEM * MIB),
        cost_estimate=estimate(ATTEND_US * count * shards / 16),
        name="attend_last" if final else "attend_first",
    )(visible, queries, known, *pieces, after if state is None else state, *more)


def combine_kernel(where_ref, own_ref, first_ref, second_ref, pages_ref, out_ref, handoff_ref):
    for n in range(handoff_ref.shape[0]):
        mine = where_ref[3, n] != 0
        for h in range(2):
            at = HEAD_COLUMNS + HEAD_SIZE + h * WIDTH
            theirs = first_ref[0, n * BLK : (n + 1) * BLK, at : at + WIDTH]
            handoff_ref[n, h] = jnp.where(mine, pages_ref[n, h], theirs)
    for h in range(2):
        other_ref = (first_ref, second_ref)[h]
        own_level = own_ref[h, :, HEAD_COLUMNS:]
        other_parts = other_ref[0, :, HEAD_COLUMNS : HEAD_COLUMNS + HEAD_SIZE].astype(jnp.float32)
        for g in range(GROUP):
            mine = own_level[:, g : g + 1]
            theirs = (
                other_parts[:, g : g + 1]
                + other_parts[:, GROUP + g : GROUP + g + 1]
                + other_parts[:, 2 * GROUP + g : 2 * GROUP + g + 1]
            )
            peak = jnp.maximum(mine, theirs)
            mine = jnp.exp2(mine - peak)
            theirs = jnp.exp2(theirs - peak)
            whole = mine + theirs
            columns = slice(g * HEAD_SIZE, (g + 1) * HEAD_SIZE)
            mixed = (mine / whole) * own_ref[h, :, columns] + (theirs / whole) * other_ref[0, :, columns].astype(
                jnp.float32
            )
            out_ref[:, h * HEAD_COLUMNS + g * HEAD_SIZE : h * HEAD_COLUMNS + (g + 1) * HEAD_SIZE] = mixed.astype(
                jnp.bfloat16
            )


def combine(where, own, other, own_pages):
    local = pl.BlockSpec(memory_space=pltpu.VMEM)
    return pl.pallas_call(
        combine_kernel,
        in_specs=[pl.BlockSpec(memory_space=pltpu.SMEM)] + [local] * 4,
        out_specs=[local] * 2,
        out_shape=[
            jax.ShapeDtypeStruct((TOKENS, 2 * HEAD_COLUMNS), jnp.bfloat16),
            jax.ShapeDtypeStruct(own_pages.shape, jnp.bfloat16),
        ],
        compiler_params=pltpu.CompilerParams(vmem_limit_bytes=16 * MIB),
        cost_estimate=estimate(1),
        name="combine",
    )(where, own, *other, own_pages)


ROW_BLOCK = 8


def decode_kernel(length_ref, live_ref, q_ref, cache_ref, fresh_ref, out_ref):
    first = pl.program_id(0) * ROW_BLOCK
    query_rows = STEPS * GROUP
    rows = ROW_BLOCK * query_rows
    contract = (((1,), (1,)), ((), ()))
    slot = lax.broadcasted_iota(jnp.int32, (query_rows, cache_ref.shape[2]), 1)
    fresh_row = lax.broadcasted_iota(jnp.int32, (rows, DECODE), 1) // STEPS
    fresh_step = lax.broadcasted_iota(jnp.int32, (rows, DECODE), 1) % STEPS
    row = lax.broadcasted_iota(jnp.int32, (rows, DECODE), 0) // query_rows
    step = lax.broadcasted_iota(jnp.int32, (rows, DECODE), 0) % STEPS
    fresh_seen = (fresh_row == row + first) & (fresh_step <= step)
    queries = q_ref[...].reshape(ROW_BLOCK * STEPS, q_ref.shape[2]).astype(jnp.float32)
    cached, fresh = [], []
    for h in range(2):
        of_head = []
        for n in range(ROW_BLOCK):
            of_row = jnp.concatenate(
                [
                    queries[n * STEPS : (n + 1) * STEPS, g * HEAD_SIZE : (g + 1) * HEAD_SIZE]
                    for g in range(h * GROUP, (h + 1) * GROUP)
                ],
                axis=0,
            ).astype(jnp.bfloat16)
            of_head.append(of_row)
            scores = lax.dot_general(
                of_row, cache_ref[n, h, :, :HEAD_SIZE], contract, preferred_element_type=jnp.float32
            )
            cached.append(jnp.where(slot < length_ref[first + n], scores, neg_large))
        scores = lax.dot_general(
            jnp.concatenate(of_head, axis=0),
            fresh_ref[h, :, :HEAD_SIZE],
            contract,
            preferred_element_type=jnp.float32,
        )
        fresh.append(jnp.where(fresh_seen, scores, neg_large))
    cached = jnp.concatenate(cached, axis=0)
    fresh = jnp.concatenate(fresh, axis=0)
    top = jnp.maximum(jnp.max(cached, axis=1, keepdims=True), jnp.max(fresh, axis=1, keepdims=True))
    cached = jnp.exp2((cached - top) * LOG2_SCALE)
    fresh = jnp.exp2((fresh - top) * LOG2_SCALE)
    total = jnp.sum(cached, axis=1, keepdims=True) + jnp.sum(fresh, axis=1, keepdims=True)
    cached = cached.astype(jnp.bfloat16)
    fresh = fresh.astype(jnp.bfloat16)
    for h in range(2):
        of_fresh = jnp.dot(
            fresh[h * rows : (h + 1) * rows], fresh_ref[h, :, HEAD_SIZE:], preferred_element_type=jnp.float32
        )
        for n in range(ROW_BLOCK):
            here = slice(h * rows + n * query_rows, h * rows + (n + 1) * query_rows)
            out = jnp.dot(cached[here], cache_ref[n, h, :, HEAD_SIZE:], preferred_element_type=jnp.float32)
            out = (out + of_fresh[n * query_rows : (n + 1) * query_rows]) / total[here]
            out = jnp.where(first + n < live_ref[0], out, 0.0)
            for g in range(GROUP):
                columns = slice((h * GROUP + g) * HEAD_SIZE, (h * GROUP + g + 1) * HEAD_SIZE)
                out_ref[n, :, columns] = out[g * STEPS : (g + 1) * STEPS].astype(jnp.bfloat16)


def decode_attend(lengths, live, queries, cache, fresh):
    rows, heads, cache_size, _ = cache.shape
    block = pl.BlockSpec((ROW_BLOCK,) + queries.shape[1:], lambda i, *_: (i, 0, 0))
    return pl.pallas_call(
        decode_kernel,
        grid_spec=pltpu.PrefetchScalarGridSpec(
            num_scalar_prefetch=2,
            grid=(rows // ROW_BLOCK,),
            in_specs=[
                block,
                pl.BlockSpec((ROW_BLOCK, heads, cache_size, WIDTH), lambda i, *_: (i, 0, 0, 0)),
                pl.BlockSpec((heads, DECODE, WIDTH), lambda i, *_: (0, 0, 0)),
            ],
            out_specs=block,
        ),
        out_shape=jax.ShapeDtypeStruct(queries.shape, jnp.bfloat16),
        compiler_params=pltpu.CompilerParams(vmem_limit_bytes=DECODE_VMEM * MIB),
        cost_estimate=estimate(DECODE_US),
        name="decode",
    )(lengths, live, queries, cache, fresh)


def stack_kernel(*refs):
    out_ref = refs[-1]
    for y in range(SIDE):
        out_ref[y] = refs[y][0]


def stack_column(rings, after):
    local = pl.BlockSpec(memory_space=pltpu.VMEM)
    return pl.pallas_call(
        stack_kernel,
        in_specs=[local] * SIDE + [pl.BlockSpec(memory_space=pl.ANY)] * len(after),
        out_specs=local,
        out_shape=jax.ShapeDtypeStruct((SIDE,) + rings[0].shape[1:], jnp.bfloat16),
        compiler_params=pltpu.CompilerParams(vmem_limit_bytes=8 * MIB),
        cost_estimate=estimate(0.5),
        name="stack",
    )(*rings, *after)


def shift(x, dz, dy):
    perm = [
        (z * SIDE + y, ((z + dz) % SIDE) * SIDE + (y + dy) % SIDE) for z in range(SIDE) for y in range(SIDE)
    ]
    return lax.ppermute(x, "ctx", perm)


def swap_pool(x):
    return lax.ppermute(x, "pool", [(0, 1), (1, 0)])


def swap_tp(x, bit):
    return lax.ppermute(x, "tp", [(i, i ^ bit) for i in range(4)])


def ring(x):
    pair = jnp.stack([x, shift(x, 2, 0)])
    far = {1: shift(pair, 0, 1), 3: shift(pair, 0, 3), 2: shift(pair, 0, 2)}
    return [pair, far[1], far[2], far[3]]


def sides(column):
    return shift(column, 1, 0), shift(column, 3, 0)


def per_device(
    span_hidden_states,
    span_token_queries,
    earlier_key_values,
    decode_hidden_states,
    decode_token_queries,
    decode_row_cache,
    key_value_weight,
    adapter_down_weight,
    adapter_up_weight,
    prompt_adapter,
    row_adapter_index,
    group_live_rows,
    cached_row_lengths,
    block_target_page,
):
    tp = lax.axis_index("tp")
    ctx = lax.axis_index("ctx")
    pool = lax.axis_index("pool")
    my_z, my_y = ctx // SIDE, ctx % SIDE

    prior_rings = ring(earlier_key_values)

    for_core, kept = project(
        tp.astype(jnp.int32).reshape(1),
        row_adapter_index,
        prompt_adapter.reshape(1, TOKENS),
        span_hidden_states,
        decode_hidden_states,
        key_value_weight,
        adapter_down_weight,
        adapter_up_weight,
    )
    from_core = swap_tp(for_core, 1)
    from_chip = swap_tp(kept[2:] + from_core[2:], 2)
    span_kv, decode_kv, late_queries = finish(
        kept[:2] + from_core[:2], from_chip, span_token_queries, (prior_rings[0],)
    )

    rings = ring(span_kv)

    decode_attention = decode_attend(
        cached_row_lengths, group_live_rows, decode_token_queries, decode_row_cache, decode_kv
    )

    far = jnp.arange(SIDE, dtype=jnp.int32)
    shard_z, shard_y = jnp.mod(my_z - far, SIDE), jnp.mod(my_y - far, SIDE)
    place = shard_z[:, None] * SIDE + shard_y[None, :]
    partner_sees = ((place < ctx) | ((place == ctx) & (pool == 0))).astype(jnp.int32).reshape(-1)
    own_sees = (place <= ctx).astype(jnp.int32).reshape(-1)
    earlier_sides = [(p, k, None) for p in range(2) for k in range(SIDE)]

    def earlier_pairs(first):
        return [(first + k, j, None) for j in range(2) for k in range(SIDE)]

    def pairs(first):
        return [(first + k, j, 2 * j * SIDE + k) for j in range(2) for k in range(SIDE)]

    beside = [(p, k, (1 + 2 * p) * SIDE + k) for p in range(2) for k in range(SIDE)]
    both = (0, 1)
    partner_queries = swap_pool(late_queries)
    own_state = attend(
        own_sees,
        span_token_queries,
        prior_rings[0],
        prior_rings,
        (tuple(earlier_pairs(0)),),
        row_adapter_index,
        both,
    )

    prior_up, prior_down = sides(stack_column(prior_rings, (decode_attention, rings[0])))
    column = stack_column(rings, (own_state, partner_queries))
    up, down = sides(column)
    partner_state = attend(
        partner_sees,
        partner_queries,
        prior_up,
        [prior_up, prior_down] + prior_rings + rings,
        (tuple(earlier_sides + earlier_pairs(2)[:4]), tuple(earlier_pairs(2)[4:] + pairs(6))),
        column,
        both,
    )

    pages = TOKENS // BLK
    shard = ctx * 2 + pool
    partner_shard = ctx * 2 + 1 - pool
    page_ids = jnp.concatenate([shard * pages + jnp.arange(pages), partner_shard * pages + jnp.arange(pages)])
    block_ids = jnp.arange(block_target_page.shape[0], dtype=jnp.int32)
    source = jnp.sum(
        jnp.where(block_target_page[None, :] == page_ids[:, None], block_ids[None, :], 0), axis=1
    )
    source_shard = source // pages
    source_ctx = source_shard // 2
    where = jnp.stack(
        [
            jnp.mod(my_z - source_ctx // SIDE, SIDE),
            jnp.mod(my_y - source_ctx % SIDE, SIDE),
            source % pages,
            (source_shard % 2 == pool).astype(jnp.int32),
        ]
    ).astype(jnp.int32)

    def attend_partner(h, page_source, before):
        return attend(
            partner_sees,
            partner_queries,
            prior_up,
            [up, down],
            (tuple(beside),),
            None,
            (h,),
            state=partner_state,
            final=True,
            partner=True,
            page_source=page_source,
            before=before,
        )

    sent, own_pages = attend_partner(0, [where, column] + rings, [])
    second = attend_partner(1, None, [sent])
    other = [swap_pool(sent), swap_pool(second)]
    own = attend(
        own_sees,
        span_token_queries,
        prior_up,
        [up, down] + rings + [prior_up, prior_down],
        (
            tuple((6 + p, k, None) for p, k, _ in earlier_sides) + tuple(pairs(2)[:4]),
            tuple(pairs(2)[4:] + beside),
        ),
        None,
        both,
        diagonal=(2, 0, 0),
        state=own_state,
        final=True,
        before=[second],
    )
    span_attention, handoff_pages = combine(where, own, other, own_pages)
    return (span_attention, handoff_pages, decode_attention)


def solution(mesh):
    in_specs = (
        P(("ctx", "pool"), "tp"),
        P(("ctx", "pool"), "tp"),
        P("tp", ("ctx", "pool"), None),
        P(("ctx", "pool"), None, "tp"),
        P(("ctx", "pool"), None, "tp"),
        P(("ctx", "pool"), "tp", None, None),
        P("tp", None),
        P("tp", None),
        P(),
        P(("ctx", "pool")),
        P(("ctx", "pool")),
        P(("ctx", "pool")),
        P(("ctx", "pool")),
        P(),
    )
    out_specs = (
        P(("ctx", "pool"), "tp"),
        P(("ctx", "pool"), "tp", None, None),
        P(("ctx", "pool"), None, "tp"),
    )
    return jax.shard_map(
        per_device, mesh=mesh, in_specs=in_specs, out_specs=out_specs, check_vma=False
    )
```

```python
import functools
import math

import jax
import jax.numpy as jnp
from jax import lax
from jax.experimental import pallas as pl
from jax.experimental.pallas import tpu as pltpu
from jax.sharding import PartitionSpec as P

HQ = 64
KEY_VALUE_HEADS = 8
HEAD_SIZE = 128
ADAPTER_RANK = 16
BLK = 16
STEPS = 4
GROUP = HQ // KEY_VALUE_HEADS
SHARDS = 16
SIDE = 4
TOKENS = 128
ROWS = 16
DECODE = ROWS * STEPS
ALL_ROWS = TOKENS + DECODE
LOG2_SCALE = math.log2(math.e) / math.sqrt(HEAD_SIZE)
neg_large = -1e30
MIB = 2**20
WIDTH = 2 * HEAD_SIZE


def estimate(us):
    return pl.CostEstimate(flops=int(us * 1.1e9), bytes_accessed=MIB, transcendentals=0)


def split3(x):
    hi = x.astype(jnp.bfloat16)
    rest = x - hi.astype(jnp.float32)
    mid = rest.astype(jnp.bfloat16)
    low = (rest - mid.astype(jnp.float32)).astype(jnp.bfloat16)
    return hi, mid, low

PROJECT_US, ATTEND_US, DECODE_US = 1, 3.4, 1
ATTEND_VMEM, PROJECT_VMEM, DECODE_VMEM = 24, 56, 24


CHUNKS = 4
OWNERS = (1, 3, 0, 2)


def project_kernel(
    row_adapter_hbm,
    adapter_hbm,
    span_ref,
    decode_ref,
    weight_ref,
    down_ref,
    up_ref,
    core_hbm,
    kept_hbm,
    row_adapter_ref,
    adapter_ref,
    core_ref,
    kept_ref,
    hidden_ref,
    rank_ref,
    buffer_ref,
    decode_buffer,
    down_buffer,
    up_buffer,
    sems,
    small_sems,
    out_sems,
):
    tp = lax.axis_index("tp")
    depth = weight_ref.shape[0] // CHUNKS
    small = [
        pltpu.make_async_copy(row_adapter_hbm, row_adapter_ref, small_sems.at[4]),
        pltpu.make_async_copy(adapter_hbm, adapter_ref, small_sems.at[5]),
        pltpu.make_async_copy(span_ref, hidden_ref.at[pl.ds(0, TOKENS)], small_sems.at[0]),
        pltpu.make_async_copy(decode_ref, decode_buffer, small_sems.at[1]),
        pltpu.make_async_copy(down_ref, down_buffer, small_sems.at[2]),
        pltpu.make_async_copy(up_ref, up_buffer, small_sems.at[3]),
    ]
    for copy in small:
        copy.start()
    columns = [pl.multiple_of(jnp.bitwise_xor(tp, bit) * 2 * WIDTH, 2 * WIDTH) for bit in OWNERS]
    copies = [
        [
            pltpu.make_async_copy(
                weight_ref.at[pl.ds(k * depth, depth), pl.ds(column, 2 * WIDTH)],
                buffer_ref.at[i, pl.ds(k * depth, depth)],
                sems.at[i, k],
            )
            for k in range(CHUNKS)
        ]
        for i, column in enumerate(columns)
    ]
    for group in copies:
        for copy in group:
            copy.start()
    for copy in small[:2]:
        copy.wait()
    span_owner = jnp.transpose(jnp.broadcast_to(adapter_ref[...], (TOKENS, TOKENS)))
    row = lax.broadcasted_iota(jnp.int32, (DECODE, TOKENS), 0) // STEPS
    decode_owner = jnp.zeros((DECODE, TOKENS), jnp.int32)
    for r in range(ROWS):
        decode_owner = jnp.where(row == r, row_adapter_ref[r], decode_owner)
    owner = jnp.concatenate([span_owner, decode_owner], axis=0)
    column = lax.broadcasted_iota(jnp.int32, (ALL_ROWS, TOKENS), 1) // ADAPTER_RANK
    for copy in small[2:]:
        copy.wait()
    hidden_ref[TOKENS:, :] = decode_buffer[...].reshape(DECODE, decode_buffer.shape[2])
    narrow = jnp.dot(hidden_ref[...], down_buffer[...], preferred_element_type=jnp.float32)
    for part, piece in enumerate(split3(jnp.where(column == owner, narrow, 0.0))):
        rank_ref[:, part * TOKENS : (part + 1) * TOKENS] = piece
    flushes = []
    for i, first in enumerate(columns):
        up = up_buffer[:, pl.ds(first, 2 * WIDTH)]
        out = jnp.dot(rank_ref[...], jnp.concatenate([up, up, up], axis=0), preferred_element_type=jnp.float32)
        for k in range(CHUNKS):
            copies[i][k].wait()
            here = slice(k * depth, (k + 1) * depth)
            out = out + jnp.dot(hidden_ref[:, here], buffer_ref[i, here, :], preferred_element_type=jnp.float32)
        out_ref, out_hbm = (core_ref, core_hbm) if i < 2 else (kept_ref, kept_hbm)
        out_ref[2 * (i % 2)] = out[:, :WIDTH]
        out_ref[2 * (i % 2) + 1] = out[:, WIDTH:]
        part = pl.ds(2 * (i % 2), 2)
        flush = pltpu.make_async_copy(out_ref.at[part], out_hbm.at[part], out_sems.at[i])
        flush.start()
        flushes.append(flush)
    for flush in flushes:
        flush.wait()


def project(row_adapter, adapter, span, decode, weight, down, up):
    depth = span.shape[1]
    far = pl.BlockSpec(memory_space=pl.ANY)
    return pl.pallas_call(
        project_kernel,
        in_specs=[far] * 7,
        out_specs=[far] * 2,
        out_shape=[jax.ShapeDtypeStruct((4, ALL_ROWS, WIDTH), jnp.float32)] * 2,
        scratch_shapes=[
            pltpu.SMEM(row_adapter.shape, jnp.int32),
            pltpu.VMEM(adapter.shape, jnp.int32),
            pltpu.VMEM((4, ALL_ROWS, WIDTH), jnp.float32),
            pltpu.VMEM((4, ALL_ROWS, WIDTH), jnp.float32),
            pltpu.VMEM((ALL_ROWS, depth), jnp.bfloat16),
            pltpu.VMEM((ALL_ROWS, 3 * TOKENS), jnp.bfloat16),
            pltpu.VMEM((4, depth, 2 * WIDTH), jnp.bfloat16),
            pltpu.VMEM(decode.shape, jnp.bfloat16),
            pltpu.VMEM(down.shape, jnp.bfloat16),
            pltpu.VMEM(up.shape, jnp.bfloat16),
            pltpu.SemaphoreType.DMA((4, CHUNKS)),
            pltpu.SemaphoreType.DMA((6,)),
            pltpu.SemaphoreType.DMA((4,)),
        ],
        compiler_params=pltpu.CompilerParams(vmem_limit_bytes=PROJECT_VMEM * MIB),
        cost_estimate=estimate(PROJECT_US),
        name="project",
    )(row_adapter, adapter, span, decode, weight, down, up)


def finish_kernel(own_ref, chip_ref, queries_ref, *refs):
    span_ref, decode_ref, late_ref = refs[-3:]
    late_ref[...] = queries_ref[...]
    total = (own_ref[...] + chip_ref[...]).astype(jnp.bfloat16)
    span_ref[...] = total[:, :TOKENS]
    decode_ref[...] = total[:, TOKENS:]


def finish(own_sum, from_chip, queries, after):
    heads, _, width = from_chip.shape
    local = pl.BlockSpec(memory_space=pltpu.VMEM)
    return pl.pallas_call(
        finish_kernel,
        in_specs=[local] * 3 + [pl.BlockSpec(memory_space=pl.ANY)] * len(after),
        out_specs=[local] * 3,
        out_shape=[
            jax.ShapeDtypeStruct((heads, TOKENS, width), jnp.bfloat16),
            jax.ShapeDtypeStruct((heads, DECODE, width), jnp.bfloat16),
            jax.ShapeDtypeStruct(queries.shape, jnp.bfloat16),
        ],
        compiler_params=pltpu.CompilerParams(vmem_limit_bytes=8 * MIB),
        cost_estimate=estimate(0.5),
        name="finish",
    )(own_sum, from_chip, queries, *after)


TILE = 2
TILE_ROWS = TILE * TOKENS
TILES = GROUP // TILE
HEAD_ROWS = GROUP * TOKENS
HEAD_COLUMNS = GROUP * HEAD_SIZE


def pick_pages(where_ref, column_ref, up_ref, down_ref, ring_refs, own_ref, other_ref, at):
    count = own_ref.shape[0]
    for n in range(2 * count):
        dz, dy = where_ref[0, n], where_ref[1, n]
        rows = pl.ds(pl.multiple_of(where_ref[2, n] * BLK, BLK), BLK)
        for h in range(2):
            page = column_ref[dy, h, rows, :]
            page = jnp.where(dz == 1, up_ref[dy, h, rows, :], page)
            page = jnp.where(dz == 3, down_ref[dy, h, rows, :], page)
            for k in range(SIDE):
                page = jnp.where((dz == 2) & (dy == k), ring_refs[k][1, h, rows, :], page)
            if n < count:
                own_ref[n, h] = page
            else:
                here = slice((n - count) * BLK, (n - count + 1) * BLK)
                other_ref[0, here, at + h * WIDTH : at + (h + 1) * WIDTH] = page


def attend_kernel(
    heads, count, blocks, diagonal, has_state, final, partner, has_pages, visible_ref, q_ref, known_ref, *refs
):
    pieces, state_ref, refs = refs[:count], refs[count], refs[count + 1 :]
    out_ref = refs[-4] if has_pages else refs[-3]
    key_ref, ext_ref = refs[-2:]
    if has_pages:
        pick_pages(
            refs[0],
            refs[1],
            pieces[0],
            pieces[1],
            refs[2 : 2 + SIDE],
            refs[-3],
            out_ref,
            HEAD_COLUMNS + HEAD_SIZE,
        )
    wide = lax.broadcasted_iota(jnp.int32, (TILE_ROWS, HEAD_SIZE), 1)
    lane = wide[:TOKENS]
    one = jnp.ones((TOKENS, HEAD_SIZE), jnp.bfloat16)
    zero = jnp.zeros((TOKENS, HEAD_SIZE), jnp.bfloat16)
    bounds = [0]
    for shards in blocks:
        bounds.append(bounds[-1] + len(shards) * TOKENS)
    for slot, h in enumerate(heads):
        for b, shards in enumerate(blocks):
            for n, (piece, index, place) in enumerate(shards):
                kv = pieces[piece][index, h]
                keys, values, ones = kv[:, :HEAD_SIZE], kv[:, HEAD_SIZE:], one
                if place is not None:
                    seen = visible_ref[place] != 0
                    keys = jnp.where(seen, keys, known_ref[0, h, :, :HEAD_SIZE])
                    values = jnp.where(seen, values, zero)
                    ones = jnp.where(seen, one, zero)
                here = slice(bounds[b] + n * TOKENS, bounds[b] + (n + 1) * TOKENS)
                key_ref[slot, here, :] = keys
                ext_ref[slot, here, :HEAD_SIZE] = values
                ext_ref[slot, here, HEAD_SIZE:] = ones
        queries = [
            jnp.concatenate(
                [
                    q_ref[:, h * HEAD_COLUMNS + g * HEAD_SIZE : h * HEAD_COLUMNS + (g + 1) * HEAD_SIZE]
                    for g in range(i * TILE, (i + 1) * TILE)
                ],
                axis=0,
            )
            for i in range(TILES)
        ]

        def score(i, b):
            scores = lax.dot_general(
                queries[i],
                key_ref[slot, bounds[b] : bounds[b + 1], :],
                (((1,), (1,)), ((), ())),
                preferred_element_type=jnp.float32,
            )
            if diagonal is not None and diagonal in blocks[b]:
                at = blocks[b].index(diagonal) * TOKENS
                token = lax.broadcasted_iota(jnp.int32, (TILE_ROWS, TOKENS), 0) % TOKENS
                parts = [scores[:, :at]] if at else []
                parts.append(jnp.where(wide <= token, scores[:, at : at + TOKENS], neg_large))
                if at + TOKENS < scores.shape[1]:
                    parts.append(scores[:, at + TOKENS :])
                scores = jnp.concatenate(parts, axis=1)
            return scores, jnp.max(scores, axis=1, keepdims=True) * LOG2_SCALE

        steps = [(i, b) for i in range(TILES) for b in range(len(blocks))]
        if final:
            stats = jnp.zeros((TOKENS, HEAD_SIZE), out_ref.dtype)
        coming = score(*steps[0])
        for n, (i, b) in enumerate(steps):
            scores, top = coming
            if n + 1 < len(steps):
                coming = score(*steps[n + 1])
            here = slice(i * TILE_ROWS, (i + 1) * TILE_ROWS)
            if b or has_state:
                if not b:
                    top_before = state_ref[h, here, HEAD_SIZE : HEAD_SIZE + 1]
                    total = jnp.concatenate(
                        [
                            state_ref[h, here, :HEAD_SIZE],
                            jnp.broadcast_to(state_ref[h, here, WIDTH - 1 :], (TILE_ROWS, HEAD_SIZE)),
                        ],
                        axis=1,
                    )
                top = jnp.maximum(top_before, top)
                total = total * jnp.exp2(top_before - top)
            weights = jnp.exp2(scores * LOG2_SCALE - top).astype(jnp.bfloat16)
            added = jnp.dot(
                weights, ext_ref[slot, bounds[b] : bounds[b + 1], :], preferred_element_type=jnp.float32
            )
            total = total + added if b or has_state else added
            top_before = top
            if b < len(blocks) - 1:
                continue
            if not final:
                out_ref[slot, here, :HEAD_SIZE] = total[:, :HEAD_SIZE]
                out_ref[slot, here, HEAD_SIZE:] = jnp.where(wide < HEAD_SIZE // 2, top, total[:, HEAD_SIZE:])
                continue
            out = total[:, :HEAD_SIZE] / total[:, HEAD_SIZE:]
            level = top + jnp.log2(total[:, HEAD_SIZE:])
            for j in range(TILE):
                g = i * TILE + j
                own = slice(j * TOKENS, (j + 1) * TOKENS)
                out_ref[slot, :, g * HEAD_SIZE : (g + 1) * HEAD_SIZE] = out[own].astype(out_ref.dtype)
                parts = split3(level[own]) if partner else (level[own],)
                for part, piece in enumerate(parts):
                    stats = jnp.where(lane == part * GROUP + g, piece, stats)
        if final:
            out_ref[slot, :, HEAD_COLUMNS : HEAD_COLUMNS + HEAD_SIZE] = stats


def attend(
    visible,
    queries,
    known,
    pieces,
    blocks,
    after,
    heads,
    diagonal=None,
    state=None,
    final=False,
    partner=False,
    page_source=None,
    before=(),
):
    shards = sum(len(block) for block in blocks)
    count = len(heads)
    if final:
        out_shape = (count, TOKENS, HEAD_COLUMNS + HEAD_SIZE + (0 if page_source is None else 2 * WIDTH))
    else:
        out_shape = (count, HEAD_ROWS, WIDTH)
    local = pl.BlockSpec(memory_space=pltpu.VMEM)
    scalar = pl.BlockSpec(memory_space=pltpu.SMEM)
    out_shape = jax.ShapeDtypeStruct(out_shape, jnp.bfloat16 if partner and final else jnp.float32)
    out_specs = local
    more, more_specs = [], []
    if page_source is not None:
        own_pages = jax.ShapeDtypeStruct((TOKENS // BLK, 2, BLK, WIDTH), jnp.bfloat16)
        out_shape, out_specs = [out_shape, own_pages], [local, local]
        more, more_specs = list(page_source), [scalar] + [local] * (len(page_source) - 1)
    more += before
    more_specs += [pl.BlockSpec(memory_space=pl.ANY)] * len(before)
    return pl.pallas_call(
        functools.partial(
            attend_kernel,
            heads,
            len(pieces),
            blocks,
            diagonal,
            state is not None,
            final,
            partner,
            page_source is not None,
        ),
        in_specs=[scalar]
        + [local] * (2 + len(pieces))
        + [pl.BlockSpec(memory_space=pl.ANY) if state is None else local]
        + more_specs,
        out_specs=out_specs,
        scratch_shapes=[
            pltpu.VMEM((count, shards * TOKENS, HEAD_SIZE), jnp.bfloat16),
            pltpu.VMEM((count, shards * TOKENS, WIDTH), jnp.bfloat16),
        ],
        out_shape=out_shape,
        compiler_params=pltpu.CompilerParams(vmem_limit_bytes=ATTEND_VMEM * MIB),
        cost_estimate=estimate(ATTEND_US * count * shards / 16),
        name="attend_last" if final else "attend_first",
    )(visible, queries, known, *pieces, after if state is None else state, *more)


def combine_kernel(where_ref, own_ref, first_ref, second_ref, pages_ref, out_ref, handoff_ref):
    for n in range(handoff_ref.shape[0]):
        mine = where_ref[3, n] != 0
        for h in range(2):
            at = HEAD_COLUMNS + HEAD_SIZE + h * WIDTH
            theirs = first_ref[0, n * BLK : (n + 1) * BLK, at : at + WIDTH]
            handoff_ref[n, h] = jnp.where(mine, pages_ref[n, h], theirs)
    for h in range(2):
        other_ref = (first_ref, second_ref)[h]
        at = HEAD_COLUMNS
        mine = own_ref[h, :, at : at + GROUP]
        parts = other_ref[0, :, at : at + HEAD_SIZE].astype(jnp.float32)
        theirs = parts[:, :GROUP] + parts[:, GROUP : 2 * GROUP] + parts[:, 2 * GROUP : 3 * GROUP]
        peak = jnp.maximum(mine, theirs)
        mine = jnp.exp2(mine - peak)
        theirs = jnp.exp2(theirs - peak)
        whole = mine + theirs
        mine, theirs = mine / whole, theirs / whole
        for g in range(GROUP):
            columns = slice(g * HEAD_SIZE, (g + 1) * HEAD_SIZE)
            mixed = mine[:, g : g + 1] * own_ref[h, :, columns] + theirs[:, g : g + 1] * other_ref[
                0, :, columns
            ].astype(jnp.float32)
            at = h * HEAD_COLUMNS + g * HEAD_SIZE
            out_ref[:, at : at + HEAD_SIZE] = mixed.astype(jnp.bfloat16)


def combine(where, own, other, own_pages):
    local = pl.BlockSpec(memory_space=pltpu.VMEM)
    return pl.pallas_call(
        combine_kernel,
        in_specs=[pl.BlockSpec(memory_space=pltpu.SMEM)] + [local] * 4,
        out_specs=[local] * 2,
        out_shape=[
            jax.ShapeDtypeStruct((TOKENS, 2 * HEAD_COLUMNS), jnp.bfloat16),
            jax.ShapeDtypeStruct(own_pages.shape, jnp.bfloat16),
        ],
        compiler_params=pltpu.CompilerParams(vmem_limit_bytes=16 * MIB),
        cost_estimate=estimate(1),
        name="combine",
    )(where, own, *other, own_pages)


ROW_BLOCK = 8


def decode_kernel(length_ref, live_ref, q_ref, cache_ref, fresh_ref, out_ref):
    first = pl.program_id(0) * ROW_BLOCK
    query_rows = STEPS * GROUP
    rows = ROW_BLOCK * query_rows
    contract = (((1,), (1,)), ((), ()))
    slot = lax.broadcasted_iota(jnp.int32, (query_rows, cache_ref.shape[2]), 1)
    fresh_row = lax.broadcasted_iota(jnp.int32, (rows, DECODE), 1) // STEPS
    fresh_step = lax.broadcasted_iota(jnp.int32, (rows, DECODE), 1) % STEPS
    row = lax.broadcasted_iota(jnp.int32, (rows, DECODE), 0) // query_rows
    step = lax.broadcasted_iota(jnp.int32, (rows, DECODE), 0) % STEPS
    fresh_seen = (fresh_row == row + first) & (fresh_step <= step)
    queries = q_ref[...].reshape(ROW_BLOCK * STEPS, q_ref.shape[2]).astype(jnp.float32)
    cached, fresh = [], []
    for h in range(2):
        of_head = []
        for n in range(ROW_BLOCK):
            of_row = jnp.concatenate(
                [
                    queries[n * STEPS : (n + 1) * STEPS, g * HEAD_SIZE : (g + 1) * HEAD_SIZE]
                    for g in range(h * GROUP, (h + 1) * GROUP)
                ],
                axis=0,
            ).astype(jnp.bfloat16)
            of_head.append(of_row)
            scores = lax.dot_general(
                of_row, cache_ref[n, h, :, :HEAD_SIZE], contract, preferred_element_type=jnp.float32
            )
            cached.append(jnp.where(slot < length_ref[first + n], scores, neg_large))
        scores = lax.dot_general(
            jnp.concatenate(of_head, axis=0),
            fresh_ref[h, :, :HEAD_SIZE],
            contract,
            preferred_element_type=jnp.float32,
        )
        fresh.append(jnp.where(fresh_seen, scores, neg_large))
    cached = jnp.concatenate(cached, axis=0)
    fresh = jnp.concatenate(fresh, axis=0)
    top = jnp.maximum(jnp.max(cached, axis=1, keepdims=True), jnp.max(fresh, axis=1, keepdims=True))
    cached = jnp.exp2((cached - top) * LOG2_SCALE)
    fresh = jnp.exp2((fresh - top) * LOG2_SCALE)
    total = jnp.sum(cached, axis=1, keepdims=True) + jnp.sum(fresh, axis=1, keepdims=True)
    cached = cached.astype(jnp.bfloat16)
    fresh = fresh.astype(jnp.bfloat16)
    for h in range(2):
        of_fresh = jnp.dot(
            fresh[h * rows : (h + 1) * rows], fresh_ref[h, :, HEAD_SIZE:], preferred_element_type=jnp.float32
        )
        for n in range(ROW_BLOCK):
            here = slice(h * rows + n * query_rows, h * rows + (n + 1) * query_rows)
            out = jnp.dot(cached[here], cache_ref[n, h, :, HEAD_SIZE:], preferred_element_type=jnp.float32)
            out = (out + of_fresh[n * query_rows : (n + 1) * query_rows]) / total[here]
            out = jnp.where(first + n < live_ref[0], out, 0.0)
            for g in range(GROUP):
                columns = slice((h * GROUP + g) * HEAD_SIZE, (h * GROUP + g + 1) * HEAD_SIZE)
                out_ref[n, :, columns] = out[g * STEPS : (g + 1) * STEPS].astype(jnp.bfloat16)


def decode_attend(lengths, live, queries, cache, fresh):
    rows, heads, cache_size, _ = cache.shape
    block = pl.BlockSpec((ROW_BLOCK,) + queries.shape[1:], lambda i, *_: (i, 0, 0))
    return pl.pallas_call(
        decode_kernel,
        grid_spec=pltpu.PrefetchScalarGridSpec(
            num_scalar_prefetch=2,
            grid=(rows // ROW_BLOCK,),
            in_specs=[
                block,
                pl.BlockSpec((ROW_BLOCK, heads, cache_size, WIDTH), lambda i, *_: (i, 0, 0, 0)),
                pl.BlockSpec((heads, DECODE, WIDTH), lambda i, *_: (0, 0, 0)),
            ],
            out_specs=block,
        ),
        out_shape=jax.ShapeDtypeStruct(queries.shape, jnp.bfloat16),
        compiler_params=pltpu.CompilerParams(vmem_limit_bytes=DECODE_VMEM * MIB),
        cost_estimate=estimate(DECODE_US),
        name="decode",
    )(lengths, live, queries, cache, fresh)


def stack_kernel(*refs):
    out_ref = refs[-1]
    for y in range(SIDE):
        out_ref[y] = refs[y][0]


def stack_column(rings, after):
    local = pl.BlockSpec(memory_space=pltpu.VMEM)
    return pl.pallas_call(
        stack_kernel,
        in_specs=[local] * SIDE + [pl.BlockSpec(memory_space=pl.ANY)] * len(after),
        out_specs=local,
        out_shape=jax.ShapeDtypeStruct((SIDE,) + rings[0].shape[1:], jnp.bfloat16),
        compiler_params=pltpu.CompilerParams(vmem_limit_bytes=8 * MIB),
        cost_estimate=estimate(0.5),
        name="stack",
    )(*rings, *after)


def shift(x, dz, dy):
    perm = [
        (z * SIDE + y, ((z + dz) % SIDE) * SIDE + (y + dy) % SIDE) for z in range(SIDE) for y in range(SIDE)
    ]
    return lax.ppermute(x, "ctx", perm)


def swap_pool(x):
    return lax.ppermute(x, "pool", [(0, 1), (1, 0)])


def swap_tp(x, bit):
    return lax.ppermute(x, "tp", [(i, i ^ bit) for i in range(4)])


def ring(x):
    pair = jnp.stack([x, shift(x, 2, 0)])
    far = {1: shift(pair, 0, 1), 3: shift(pair, 0, 3), 2: shift(pair, 0, 2)}
    return [pair, far[1], far[2], far[3]]


def sides(column):
    return shift(column, 1, 0), shift(column, 3, 0)


def per_device(
    span_hidden_states,
    span_token_queries,
    earlier_key_values,
    decode_hidden_states,
    decode_token_queries,
    decode_row_cache,
    key_value_weight,
    adapter_down_weight,
    adapter_up_weight,
    prompt_adapter,
    row_adapter_index,
    group_live_rows,
    cached_row_lengths,
    block_target_page,
):
    ctx = lax.axis_index("ctx")
    pool = lax.axis_index("pool")
    my_z, my_y = ctx // SIDE, ctx % SIDE

    prior_rings = ring(earlier_key_values)

    for_core, kept = project(
        row_adapter_index,
        prompt_adapter.reshape(1, TOKENS),
        span_hidden_states,
        decode_hidden_states,
        key_value_weight,
        adapter_down_weight,
        adapter_up_weight,
    )
    from_core = swap_tp(for_core, 1)
    from_chip = swap_tp(kept[2:] + from_core[2:], 2)
    span_kv, decode_kv, late_queries = finish(
        kept[:2] + from_core[:2], from_chip, span_token_queries, (prior_rings[0],)
    )

    rings = ring(span_kv)

    decode_attention = decode_attend(
        cached_row_lengths, group_live_rows, decode_token_queries, decode_row_cache, decode_kv
    )

    far = jnp.arange(SIDE, dtype=jnp.int32)
    shard_z, shard_y = jnp.mod(my_z - far, SIDE), jnp.mod(my_y - far, SIDE)
    place = shard_z[:, None] * SIDE + shard_y[None, :]
    partner_sees = ((place < ctx) | ((place == ctx) & (pool == 0))).astype(jnp.int32).reshape(-1)
    own_sees = (place <= ctx).astype(jnp.int32).reshape(-1)
    earlier_sides = [(p, k, None) for p in range(2) for k in range(SIDE)]

    def earlier_pairs(first):
        return [(first + k, j, None) for j in range(2) for k in range(SIDE)]

    def pairs(first):
        return [(first + k, j, 2 * j * SIDE + k) for j in range(2) for k in range(SIDE)]

    beside = [(p, k, (1 + 2 * p) * SIDE + k) for p in range(2) for k in range(SIDE)]
    both = (0, 1)
    partner_queries = swap_pool(late_queries)
    own_state = attend(
        own_sees,
        span_token_queries,
        prior_rings[0],
        prior_rings,
        (tuple(earlier_pairs(0)),),
        row_adapter_index,
        both,
    )

    prior_up, prior_down = sides(stack_column(prior_rings, (decode_attention, rings[0])))
    column = stack_column(rings, (own_state, partner_queries))
    up, down = sides(column)
    partner_state = attend(
        partner_sees,
        partner_queries,
        prior_up,
        [prior_up, prior_down] + prior_rings + rings,
        (tuple(earlier_sides + earlier_pairs(2)[:4]), tuple(earlier_pairs(2)[4:] + pairs(6))),
        column,
        both,
    )

    pages = TOKENS // BLK
    shard = ctx * 2 + pool
    partner_shard = ctx * 2 + 1 - pool
    page_ids = jnp.concatenate([shard * pages + jnp.arange(pages), partner_shard * pages + jnp.arange(pages)])
    block_ids = jnp.arange(block_target_page.shape[0], dtype=jnp.int32)
    source = jnp.sum(
        jnp.where(block_target_page[None, :] == page_ids[:, None], block_ids[None, :], 0), axis=1
    )
    source_shard = source // pages
    source_ctx = source_shard // 2
    where = jnp.stack(
        [
            jnp.mod(my_z - source_ctx // SIDE, SIDE),
            jnp.mod(my_y - source_ctx % SIDE, SIDE),
            source % pages,
            (source_shard % 2 == pool).astype(jnp.int32),
        ]
    ).astype(jnp.int32)

    def attend_partner(h, page_source, before):
        return attend(
            partner_sees,
            partner_queries,
            prior_up,
            [up, down],
            (tuple(beside),),
            None,
            (h,),
            state=partner_state,
            final=True,
            partner=True,
            page_source=page_source,
            before=before,
        )

    sent, own_pages = attend_partner(0, [where, column] + rings, [])
    second = attend_partner(1, None, [sent])
    other = [swap_pool(sent), swap_pool(second)]
    own = attend(
        own_sees,
        span_token_queries,
        prior_up,
        [up, down] + rings + [prior_up, prior_down],
        (
            tuple((6 + p, k, None) for p, k, _ in earlier_sides) + tuple(pairs(2)[:4]),
            tuple(pairs(2)[4:] + beside),
        ),
        None,
        both,
        diagonal=(2, 0, 0),
        state=own_state,
        final=True,
        before=[second],
    )
    span_attention, handoff_pages = combine(where, own, other, own_pages)
    return (span_attention, handoff_pages, decode_attention)


def solution(mesh):
    in_specs = (
        P(("ctx", "pool"), "tp"),
        P(("ctx", "pool"), "tp"),
        P("tp", ("ctx", "pool"), None),
        P(("ctx", "pool"), None, "tp"),
        P(("ctx", "pool"), None, "tp"),
        P(("ctx", "pool"), "tp", None, None),
        P("tp", None),
        P("tp", None),
        P(),
        P(("ctx", "pool")),
        P(("ctx", "pool")),
        P(("ctx", "pool")),
        P(("ctx", "pool")),
        P(),
    )
    out_specs = (
        P(("ctx", "pool"), "tp"),
        P(("ctx", "pool"), "tp", None, None),
        P(("ctx", "pool"), None, "tp"),
    )
    return jax.shard_map(
        per_device, mesh=mesh, in_specs=in_specs, out_specs=out_specs, check_vma=False
    )
```

```python
import functools
import math

import jax
import jax.numpy as jnp
from jax import lax
from jax.experimental import pallas as pl
from jax.experimental.pallas import tpu as pltpu
from jax.sharding import PartitionSpec as P

HQ = 64
KEY_VALUE_HEADS = 8
HEAD_SIZE = 128
ADAPTER_RANK = 16
BLK = 16
STEPS = 4
GROUP = HQ // KEY_VALUE_HEADS
SHARDS = 16
SIDE = 4
TOKENS = 128
ROWS = 16
DECODE = ROWS * STEPS
ALL_ROWS = TOKENS + DECODE
LOG2_SCALE = math.log2(math.e) / math.sqrt(HEAD_SIZE)
neg_large = -1e30
MIB = 2**20
WIDTH = 2 * HEAD_SIZE


def estimate(us):
    return pl.CostEstimate(flops=int(us * 1.1e9), bytes_accessed=MIB, transcendentals=0)


def split3(x):
    hi = x.astype(jnp.bfloat16)
    rest = x - hi.astype(jnp.float32)
    mid = rest.astype(jnp.bfloat16)
    low = (rest - mid.astype(jnp.float32)).astype(jnp.bfloat16)
    return hi, mid, low

PROJECT_US, ATTEND_US, DECODE_US = 1, 0.3, 0.1
ATTEND_VMEM, PROJECT_VMEM, DECODE_VMEM = 24, 56, 24


CHUNKS = 4
OWNERS = (1, 3, 0, 2)


def project_kernel(
    row_adapter_hbm,
    adapter_hbm,
    span_ref,
    decode_ref,
    weight_ref,
    down_ref,
    up_ref,
    core_hbm,
    kept_hbm,
    row_adapter_ref,
    adapter_ref,
    core_ref,
    kept_ref,
    hidden_ref,
    rank_ref,
    buffer_ref,
    decode_buffer,
    down_buffer,
    up_buffer,
    sems,
    small_sems,
    out_sems,
):
    tp = lax.axis_index("tp")
    depth = weight_ref.shape[0] // CHUNKS
    small = [
        pltpu.make_async_copy(row_adapter_hbm, row_adapter_ref, small_sems.at[4]),
        pltpu.make_async_copy(adapter_hbm, adapter_ref, small_sems.at[5]),
        pltpu.make_async_copy(span_ref, hidden_ref.at[pl.ds(0, TOKENS)], small_sems.at[0]),
        pltpu.make_async_copy(decode_ref, decode_buffer, small_sems.at[1]),
        pltpu.make_async_copy(down_ref, down_buffer, small_sems.at[2]),
        pltpu.make_async_copy(up_ref, up_buffer, small_sems.at[3]),
    ]
    for copy in small:
        copy.start()
    columns = [pl.multiple_of(jnp.bitwise_xor(tp, bit) * 2 * WIDTH, 2 * WIDTH) for bit in OWNERS]
    copies = [
        [
            pltpu.make_async_copy(
                weight_ref.at[pl.ds(k * depth, depth), pl.ds(column, 2 * WIDTH)],
                buffer_ref.at[i, pl.ds(k * depth, depth)],
                sems.at[i, k],
            )
            for k in range(CHUNKS)
        ]
        for i, column in enumerate(columns)
    ]
    for group in copies:
        for copy in group:
            copy.start()
    for copy in small[:2]:
        copy.wait()
    span_owner = jnp.transpose(jnp.broadcast_to(adapter_ref[...], (TOKENS, TOKENS)))
    row = lax.broadcasted_iota(jnp.int32, (DECODE, TOKENS), 0) // STEPS
    decode_owner = jnp.zeros((DECODE, TOKENS), jnp.int32)
    for r in range(ROWS):
        decode_owner = jnp.where(row == r, row_adapter_ref[r], decode_owner)
    owner = jnp.concatenate([span_owner, decode_owner], axis=0)
    column = lax.broadcasted_iota(jnp.int32, (ALL_ROWS, TOKENS), 1) // ADAPTER_RANK
    for copy in small[2:]:
        copy.wait()
    hidden_ref[TOKENS:, :] = decode_buffer[...].reshape(DECODE, decode_buffer.shape[2])
    narrow = jnp.dot(hidden_ref[...], down_buffer[...], preferred_element_type=jnp.float32)
    for part, piece in enumerate(split3(jnp.where(column == owner, narrow, 0.0))):
        rank_ref[:, part * TOKENS : (part + 1) * TOKENS] = piece
    flushes = []
    for i, first in enumerate(columns):
        up = up_buffer[:, pl.ds(first, 2 * WIDTH)]
        out = jnp.dot(rank_ref[...], jnp.concatenate([up, up, up], axis=0), preferred_element_type=jnp.float32)
        for k in range(CHUNKS):
            copies[i][k].wait()
            here = slice(k * depth, (k + 1) * depth)
            out = out + jnp.dot(hidden_ref[:, here], buffer_ref[i, here, :], preferred_element_type=jnp.float32)
        out_ref, out_hbm = (core_ref, core_hbm) if i < 2 else (kept_ref, kept_hbm)
        out_ref[2 * (i % 2)] = out[:, :WIDTH]
        out_ref[2 * (i % 2) + 1] = out[:, WIDTH:]
        part = pl.ds(2 * (i % 2), 2)
        flush = pltpu.make_async_copy(out_ref.at[part], out_hbm.at[part], out_sems.at[i])
        flush.start()
        flushes.append(flush)
    for flush in flushes:
        flush.wait()


def project(row_adapter, adapter, span, decode, weight, down, up):
    depth = span.shape[1]
    far = pl.BlockSpec(memory_space=pl.ANY)
    return pl.pallas_call(
        project_kernel,
        in_specs=[far] * 7,
        out_specs=[far] * 2,
        out_shape=[jax.ShapeDtypeStruct((4, ALL_ROWS, WIDTH), jnp.float32)] * 2,
        scratch_shapes=[
            pltpu.SMEM(row_adapter.shape, jnp.int32),
            pltpu.VMEM(adapter.shape, jnp.int32),
            pltpu.VMEM((4, ALL_ROWS, WIDTH), jnp.float32),
            pltpu.VMEM((4, ALL_ROWS, WIDTH), jnp.float32),
            pltpu.VMEM((ALL_ROWS, depth), jnp.bfloat16),
            pltpu.VMEM((ALL_ROWS, 3 * TOKENS), jnp.bfloat16),
            pltpu.VMEM((4, depth, 2 * WIDTH), jnp.bfloat16),
            pltpu.VMEM(decode.shape, jnp.bfloat16),
            pltpu.VMEM(down.shape, jnp.bfloat16),
            pltpu.VMEM(up.shape, jnp.bfloat16),
            pltpu.SemaphoreType.DMA((4, CHUNKS)),
            pltpu.SemaphoreType.DMA((6,)),
            pltpu.SemaphoreType.DMA((4,)),
        ],
        compiler_params=pltpu.CompilerParams(vmem_limit_bytes=PROJECT_VMEM * MIB),
        cost_estimate=estimate(PROJECT_US),
        name="project",
    )(row_adapter, adapter, span, decode, weight, down, up)


def finish_kernel(own_ref, chip_ref, queries_ref, *refs):
    span_ref, decode_ref, late_ref = refs[-3:]
    late_ref[...] = queries_ref[...]
    total = (own_ref[...] + chip_ref[...]).astype(jnp.bfloat16)
    span_ref[...] = total[:, :TOKENS]
    decode_ref[...] = total[:, TOKENS:]


def finish(own_sum, from_chip, queries, after):
    heads, _, width = from_chip.shape
    local = pl.BlockSpec(memory_space=pltpu.VMEM)
    return pl.pallas_call(
        finish_kernel,
        in_specs=[local] * 3 + [pl.BlockSpec(memory_space=pl.ANY)] * len(after),
        out_specs=[local] * 3,
        out_shape=[
            jax.ShapeDtypeStruct((heads, TOKENS, width), jnp.bfloat16),
            jax.ShapeDtypeStruct((heads, DECODE, width), jnp.bfloat16),
            jax.ShapeDtypeStruct(queries.shape, jnp.bfloat16),
        ],
        compiler_params=pltpu.CompilerParams(vmem_limit_bytes=8 * MIB),
        cost_estimate=estimate(0.02),
        name="finish",
    )(own_sum, from_chip, queries, *after)


TILE = 2
TILE_ROWS = TILE * TOKENS
TILES = GROUP // TILE
HEAD_ROWS = GROUP * TOKENS
HEAD_COLUMNS = GROUP * HEAD_SIZE


def pick_pages(where_ref, column_ref, up_ref, down_ref, ring_refs, own_ref, other_ref, at):
    count = own_ref.shape[0]
    for n in range(2 * count):
        dz, dy = where_ref[0, n], where_ref[1, n]
        rows = pl.ds(pl.multiple_of(where_ref[2, n] * BLK, BLK), BLK)
        for h in range(2):
            page = column_ref[dy, h, rows, :]
            page = jnp.where(dz == 1, up_ref[dy, h, rows, :], page)
            page = jnp.where(dz == 3, down_ref[dy, h, rows, :], page)
            for k in range(SIDE):
                page = jnp.where((dz == 2) & (dy == k), ring_refs[k][1, h, rows, :], page)
            if n < count:
                own_ref[n, h] = page
            else:
                here = slice((n - count) * BLK, (n - count + 1) * BLK)
                other_ref[0, here, at + h * WIDTH : at + (h + 1) * WIDTH] = page


def attend_kernel(
    heads, count, blocks, diagonal, has_state, final, partner, has_pages, visible_ref, q_ref, known_ref, *refs
):
    pieces, state_ref, refs = refs[:count], refs[count], refs[count + 1 :]
    out_ref = refs[-4] if has_pages else refs[-3]
    key_ref, ext_ref = refs[-2:]
    if has_pages:
        pick_pages(
            refs[0],
            refs[1],
            pieces[0],
            pieces[1],
            refs[2 : 2 + SIDE],
            refs[-3],
            out_ref,
            HEAD_COLUMNS + HEAD_SIZE,
        )
    wide = lax.broadcasted_iota(jnp.int32, (TILE_ROWS, HEAD_SIZE), 1)
    lane = wide[:TOKENS]
    one = jnp.ones((TOKENS, HEAD_SIZE), jnp.bfloat16)
    zero = jnp.zeros((TOKENS, HEAD_SIZE), jnp.bfloat16)
    bounds = [0]
    for shards in blocks:
        bounds.append(bounds[-1] + len(shards) * TOKENS)
    for slot, h in enumerate(heads):
        for b, shards in enumerate(blocks):
            for n, (piece, index, place) in enumerate(shards):
                kv = pieces[piece][index, h]
                keys, values, ones = kv[:, :HEAD_SIZE], kv[:, HEAD_SIZE:], one
                if place is not None:
                    seen = visible_ref[place] != 0
                    keys = jnp.where(seen, keys, known_ref[0, h, :, :HEAD_SIZE])
                    values = jnp.where(seen, values, zero)
                    ones = jnp.where(seen, one, zero)
                here = slice(bounds[b] + n * TOKENS, bounds[b] + (n + 1) * TOKENS)
                key_ref[slot, here, :] = keys
                ext_ref[slot, here, :HEAD_SIZE] = values
                ext_ref[slot, here, HEAD_SIZE:] = ones
        queries = [
            jnp.concatenate(
                [
                    q_ref[:, h * HEAD_COLUMNS + g * HEAD_SIZE : h * HEAD_COLUMNS + (g + 1) * HEAD_SIZE]
                    for g in range(i * TILE, (i + 1) * TILE)
                ],
                axis=0,
            )
            for i in range(TILES)
        ]

        def score(i, b):
            scores = lax.dot_general(
                queries[i],
                key_ref[slot, bounds[b] : bounds[b + 1], :],
                (((1,), (1,)), ((), ())),
                preferred_element_type=jnp.float32,
            )
            if diagonal is not None and diagonal in blocks[b]:
                at = blocks[b].index(diagonal) * TOKENS
                token = lax.broadcasted_iota(jnp.int32, (TILE_ROWS, TOKENS), 0) % TOKENS
                parts = [scores[:, :at]] if at else []
                parts.append(jnp.where(wide <= token, scores[:, at : at + TOKENS], neg_large))
                if at + TOKENS < scores.shape[1]:
                    parts.append(scores[:, at + TOKENS :])
                scores = jnp.concatenate(parts, axis=1)
            return scores, jnp.max(scores, axis=1, keepdims=True) * LOG2_SCALE

        steps = [(i, b) for i in range(TILES) for b in range(len(blocks))]
        if final:
            stats = jnp.zeros((TOKENS, HEAD_SIZE), out_ref.dtype)
        coming = score(*steps[0])
        for n, (i, b) in enumerate(steps):
            scores, top = coming
            if n + 1 < len(steps):
                coming = score(*steps[n + 1])
            here = slice(i * TILE_ROWS, (i + 1) * TILE_ROWS)
            if b or has_state:
                if not b:
                    top_before = state_ref[h, here, HEAD_SIZE : HEAD_SIZE + 1]
                    total = jnp.concatenate(
                        [
                            state_ref[h, here, :HEAD_SIZE],
                            jnp.broadcast_to(state_ref[h, here, WIDTH - 1 :], (TILE_ROWS, HEAD_SIZE)),
                        ],
                        axis=1,
                    )
                top = jnp.maximum(top_before, top)
                total = total * jnp.exp2(top_before - top)
            weights = jnp.exp2(scores * LOG2_SCALE - top).astype(jnp.bfloat16)
            added = jnp.dot(
                weights, ext_ref[slot, bounds[b] : bounds[b + 1], :], preferred_element_type=jnp.float32
            )
            total = total + added if b or has_state else added
            top_before = top
            if b < len(blocks) - 1:
                continue
            if not final:
                out_ref[slot, here, :HEAD_SIZE] = total[:, :HEAD_SIZE]
                out_ref[slot, here, HEAD_SIZE:] = jnp.where(wide < HEAD_SIZE // 2, top, total[:, HEAD_SIZE:])
                continue
            out = total[:, :HEAD_SIZE] / total[:, HEAD_SIZE:]
            level = top + jnp.log2(total[:, HEAD_SIZE:])
            for j in range(TILE):
                g = i * TILE + j
                own = slice(j * TOKENS, (j + 1) * TOKENS)
                out_ref[slot, :, g * HEAD_SIZE : (g + 1) * HEAD_SIZE] = out[own].astype(out_ref.dtype)
                parts = split3(level[own]) if partner else (level[own],)
                for part, piece in enumerate(parts):
                    stats = jnp.where(lane == part * GROUP + g, piece, stats)
        if final:
            out_ref[slot, :, HEAD_COLUMNS : HEAD_COLUMNS + HEAD_SIZE] = stats


def attend(
    visible,
    queries,
    known,
    pieces,
    blocks,
    after,
    heads,
    diagonal=None,
    state=None,
    final=False,
    partner=False,
    page_source=None,
    before=(),
):
    shards = sum(len(block) for block in blocks)
    count = len(heads)
    if final:
        out_shape = (count, TOKENS, HEAD_COLUMNS + HEAD_SIZE + (0 if page_source is None else 2 * WIDTH))
    else:
        out_shape = (count, HEAD_ROWS, WIDTH)
    local = pl.BlockSpec(memory_space=pltpu.VMEM)
    scalar = pl.BlockSpec(memory_space=pltpu.SMEM)
    out_shape = jax.ShapeDtypeStruct(out_shape, jnp.bfloat16 if partner and final else jnp.float32)
    out_specs = local
    more, more_specs = [], []
    if page_source is not None:
        own_pages = jax.ShapeDtypeStruct((TOKENS // BLK, 2, BLK, WIDTH), jnp.bfloat16)
        out_shape, out_specs = [out_shape, own_pages], [local, local]
        more, more_specs = list(page_source), [scalar] + [local] * (len(page_source) - 1)
    more += before
    more_specs += [pl.BlockSpec(memory_space=pl.ANY)] * len(before)
    return pl.pallas_call(
        functools.partial(
            attend_kernel,
            heads,
            len(pieces),
            blocks,
            diagonal,
            state is not None,
            final,
            partner,
            page_source is not None,
        ),
        in_specs=[scalar]
        + [local] * (2 + len(pieces))
        + [pl.BlockSpec(memory_space=pl.ANY) if state is None else local]
        + more_specs,
        out_specs=out_specs,
        scratch_shapes=[
            pltpu.VMEM((count, shards * TOKENS, HEAD_SIZE), jnp.bfloat16),
            pltpu.VMEM((count, shards * TOKENS, WIDTH), jnp.bfloat16),
        ],
        out_shape=out_shape,
        compiler_params=pltpu.CompilerParams(vmem_limit_bytes=ATTEND_VMEM * MIB),
        cost_estimate=estimate(ATTEND_US * count * shards / 16),
        name="attend_last" if final else "attend_first",
    )(visible, queries, known, *pieces, after if state is None else state, *more)


def combine_kernel(where_ref, own_ref, first_ref, second_ref, pages_ref, out_ref, handoff_ref):
    for n in range(handoff_ref.shape[0]):
        mine = where_ref[3, n] != 0
        for h in range(2):
            at = HEAD_COLUMNS + HEAD_SIZE + h * WIDTH
            theirs = first_ref[0, n * BLK : (n + 1) * BLK, at : at + WIDTH]
            handoff_ref[n, h] = jnp.where(mine, pages_ref[n, h], theirs)
    for h in range(2):
        other_ref = (first_ref, second_ref)[h]
        at = HEAD_COLUMNS
        mine = own_ref[h, :, at : at + GROUP]
        parts = other_ref[0, :, at : at + HEAD_SIZE].astype(jnp.float32)
        theirs = parts[:, :GROUP] + parts[:, GROUP : 2 * GROUP] + parts[:, 2 * GROUP : 3 * GROUP]
        peak = jnp.maximum(mine, theirs)
        mine = jnp.exp2(mine - peak)
        theirs = jnp.exp2(theirs - peak)
        whole = mine + theirs
        mine, theirs = mine / whole, theirs / whole
        for g in range(GROUP):
            columns = slice(g * HEAD_SIZE, (g + 1) * HEAD_SIZE)
            mixed = mine[:, g : g + 1] * own_ref[h, :, columns] + theirs[:, g : g + 1] * other_ref[
                0, :, columns
            ].astype(jnp.float32)
            at = h * HEAD_COLUMNS + g * HEAD_SIZE
            out_ref[:, at : at + HEAD_SIZE] = mixed.astype(jnp.bfloat16)


def combine(where, own, other, own_pages):
    local = pl.BlockSpec(memory_space=pltpu.VMEM)
    return pl.pallas_call(
        combine_kernel,
        in_specs=[pl.BlockSpec(memory_space=pltpu.SMEM)] + [local] * 4,
        out_specs=[local] * 2,
        out_shape=[
            jax.ShapeDtypeStruct((TOKENS, 2 * HEAD_COLUMNS), jnp.bfloat16),
            jax.ShapeDtypeStruct(own_pages.shape, jnp.bfloat16),
        ],
        compiler_params=pltpu.CompilerParams(vmem_limit_bytes=16 * MIB),
        cost_estimate=estimate(1),
        name="combine",
    )(where, own, *other, own_pages)


ROW_BLOCK = 8


def decode_kernel(length_ref, live_ref, q_ref, cache_ref, fresh_ref, *refs):
    out_ref = refs[-1]
    first = pl.program_id(0) * ROW_BLOCK
    query_rows = STEPS * GROUP
    rows = ROW_BLOCK * query_rows
    contract = (((1,), (1,)), ((), ()))
    slot = lax.broadcasted_iota(jnp.int32, (query_rows, cache_ref.shape[2]), 1)
    fresh_row = lax.broadcasted_iota(jnp.int32, (rows, DECODE), 1) // STEPS
    fresh_step = lax.broadcasted_iota(jnp.int32, (rows, DECODE), 1) % STEPS
    row = lax.broadcasted_iota(jnp.int32, (rows, DECODE), 0) // query_rows
    step = lax.broadcasted_iota(jnp.int32, (rows, DECODE), 0) % STEPS
    fresh_seen = (fresh_row == row + first) & (fresh_step <= step)
    queries = q_ref[...].reshape(ROW_BLOCK * STEPS, q_ref.shape[2]).astype(jnp.float32)
    cached, fresh = [], []
    for h in range(2):
        of_head = []
        for n in range(ROW_BLOCK):
            of_row = jnp.concatenate(
                [
                    queries[n * STEPS : (n + 1) * STEPS, g * HEAD_SIZE : (g + 1) * HEAD_SIZE]
                    for g in range(h * GROUP, (h + 1) * GROUP)
                ],
                axis=0,
            ).astype(jnp.bfloat16)
            of_head.append(of_row)
            scores = lax.dot_general(
                of_row, cache_ref[n, h, :, :HEAD_SIZE], contract, preferred_element_type=jnp.float32
            )
            cached.append(jnp.where(slot < length_ref[first + n], scores, neg_large))
        scores = lax.dot_general(
            jnp.concatenate(of_head, axis=0),
            fresh_ref[h, :, :HEAD_SIZE],
            contract,
            preferred_element_type=jnp.float32,
        )
        fresh.append(jnp.where(fresh_seen, scores, neg_large))
    cached = jnp.concatenate(cached, axis=0)
    fresh = jnp.concatenate(fresh, axis=0)
    top = jnp.maximum(jnp.max(cached, axis=1, keepdims=True), jnp.max(fresh, axis=1, keepdims=True))
    cached = jnp.exp2((cached - top) * LOG2_SCALE)
    fresh = jnp.exp2((fresh - top) * LOG2_SCALE)
    total = jnp.sum(cached, axis=1, keepdims=True) + jnp.sum(fresh, axis=1, keepdims=True)
    cached = cached.astype(jnp.bfloat16)
    fresh = fresh.astype(jnp.bfloat16)
    for h in range(2):
        of_fresh = jnp.dot(
            fresh[h * rows : (h + 1) * rows], fresh_ref[h, :, HEAD_SIZE:], preferred_element_type=jnp.float32
        )
        for n in range(ROW_BLOCK):
            here = slice(h * rows + n * query_rows, h * rows + (n + 1) * query_rows)
            out = jnp.dot(cached[here], cache_ref[n, h, :, HEAD_SIZE:], preferred_element_type=jnp.float32)
            out = (out + of_fresh[n * query_rows : (n + 1) * query_rows]) / total[here]
            out = jnp.where(first + n < live_ref[0], out, 0.0)
            for g in range(GROUP):
                columns = slice((h * GROUP + g) * HEAD_SIZE, (h * GROUP + g + 1) * HEAD_SIZE)
                out_ref[n, :, columns] = out[g * STEPS : (g + 1) * STEPS].astype(jnp.bfloat16)


def decode_attend(lengths, live, queries, cache, fresh, after):
    rows, heads, cache_size, _ = cache.shape
    block = pl.BlockSpec((ROW_BLOCK,) + queries.shape[1:], lambda i, *_: (i, 0, 0))
    return pl.pallas_call(
        decode_kernel,
        grid_spec=pltpu.PrefetchScalarGridSpec(
            num_scalar_prefetch=2,
            grid=(rows // ROW_BLOCK,),
            in_specs=[
                block,
                pl.BlockSpec((ROW_BLOCK, heads, cache_size, WIDTH), lambda i, *_: (i, 0, 0, 0)),
                pl.BlockSpec((heads, DECODE, WIDTH), lambda i, *_: (0, 0, 0)),
            ]
            + [pl.BlockSpec(memory_space=pl.ANY)] * len(after),
            out_specs=block,
        ),
        out_shape=jax.ShapeDtypeStruct(queries.shape, jnp.bfloat16),
        compiler_params=pltpu.CompilerParams(vmem_limit_bytes=DECODE_VMEM * MIB),
        cost_estimate=estimate(DECODE_US),
        name="decode",
    )(lengths, live, queries, cache, fresh, *after)


def stack_kernel(*refs):
    out_ref = refs[-1]
    for y in range(SIDE):
        out_ref[y] = refs[y][0]


def stack_column(rings, after):
    local = pl.BlockSpec(memory_space=pltpu.VMEM)
    return pl.pallas_call(
        stack_kernel,
        in_specs=[local] * SIDE + [pl.BlockSpec(memory_space=pl.ANY)] * len(after),
        out_specs=local,
        out_shape=jax.ShapeDtypeStruct((SIDE,) + rings[0].shape[1:], jnp.bfloat16),
        compiler_params=pltpu.CompilerParams(vmem_limit_bytes=8 * MIB),
        cost_estimate=estimate(0.02),
        name="stack",
    )(*rings, *after)


def shift(x, dz, dy):
    perm = [
        (z * SIDE + y, ((z + dz) % SIDE) * SIDE + (y + dy) % SIDE) for z in range(SIDE) for y in range(SIDE)
    ]
    return lax.ppermute(x, "ctx", perm)


def swap_pool(x):
    return lax.ppermute(x, "pool", [(0, 1), (1, 0)])


def swap_tp(x, bit):
    return lax.ppermute(x, "tp", [(i, i ^ bit) for i in range(4)])


def ring(x):
    pair = jnp.stack([x, shift(x, 2, 0)])
    far = {1: shift(pair, 0, 1), 3: shift(pair, 0, 3), 2: shift(pair, 0, 2)}
    return [pair, far[1], far[2], far[3]]


def sides(column):
    return shift(column, 1, 0), shift(column, 3, 0)


def per_device(
    span_hidden_states,
    span_token_queries,
    earlier_key_values,
    decode_hidden_states,
    decode_token_queries,
    decode_row_cache,
    key_value_weight,
    adapter_down_weight,
    adapter_up_weight,
    prompt_adapter,
    row_adapter_index,
    group_live_rows,
    cached_row_lengths,
    block_target_page,
):
    ctx = lax.axis_index("ctx")
    pool = lax.axis_index("pool")
    my_z, my_y = ctx // SIDE, ctx % SIDE

    prior_rings = ring(earlier_key_values)

    for_core, kept = project(
        row_adapter_index,
        prompt_adapter.reshape(1, TOKENS),
        span_hidden_states,
        decode_hidden_states,
        key_value_weight,
        adapter_down_weight,
        adapter_up_weight,
    )
    from_core = swap_tp(for_core, 1)
    from_chip = swap_tp(kept[2:] + from_core[2:], 2)
    span_kv, decode_kv, late_queries = finish(
        kept[:2] + from_core[:2], from_chip, span_token_queries, (prior_rings[0],)
    )

    rings = ring(span_kv)

    prior_column = stack_column(prior_rings, (rings[0],))
    prior_up, prior_down = sides(prior_column)

    partner_queries = swap_pool(late_queries)

    decode_attention = decode_attend(
        cached_row_lengths,
        group_live_rows,
        decode_token_queries,
        decode_row_cache,
        decode_kv,
        (prior_column, partner_queries),
    )

    far = jnp.arange(SIDE, dtype=jnp.int32)
    shard_z, shard_y = jnp.mod(my_z - far, SIDE), jnp.mod(my_y - far, SIDE)
    place = shard_z[:, None] * SIDE + shard_y[None, :]
    partner_sees = ((place < ctx) | ((place == ctx) & (pool == 0))).astype(jnp.int32).reshape(-1)
    own_sees = (place <= ctx).astype(jnp.int32).reshape(-1)
    earlier_sides = [(p, k, None) for p in range(2) for k in range(SIDE)]

    def earlier_pairs(first):
        return [(first + k, j, None) for j in range(2) for k in range(SIDE)]

    def pairs(first):
        return [(first + k, j, 2 * j * SIDE + k) for j in range(2) for k in range(SIDE)]

    beside = [(p, k, (1 + 2 * p) * SIDE + k) for p in range(2) for k in range(SIDE)]
    both = (0, 1)
    own_state = attend(
        own_sees,
        span_token_queries,
        prior_rings[0],
        prior_rings,
        (tuple(earlier_pairs(0)),),
        decode_attention,
        both,
    )

    column = stack_column(rings, (own_state, partner_queries, decode_attention))
    up, down = sides(column)
    partner_state = attend(
        partner_sees,
        partner_queries,
        prior_up,
        [prior_up, prior_down] + prior_rings + rings,
        (tuple(earlier_sides + earlier_pairs(2)[:4]), tuple(earlier_pairs(2)[4:] + pairs(6))),
        column,
        both,
    )

    pages = TOKENS // BLK
    shard = ctx * 2 + pool
    partner_shard = ctx * 2 + 1 - pool
    page_ids = jnp.concatenate([shard * pages + jnp.arange(pages), partner_shard * pages + jnp.arange(pages)])
    block_ids = jnp.arange(block_target_page.shape[0], dtype=jnp.int32)
    source = jnp.sum(
        jnp.where(block_target_page[None, :] == page_ids[:, None], block_ids[None, :], 0), axis=1
    )
    source_shard = source // pages
    source_ctx = source_shard // 2
    where = jnp.stack(
        [
            jnp.mod(my_z - source_ctx // SIDE, SIDE),
            jnp.mod(my_y - source_ctx % SIDE, SIDE),
            source % pages,
            (source_shard % 2 == pool).astype(jnp.int32),
        ]
    ).astype(jnp.int32)

    def attend_partner(h, page_source, before):
        return attend(
            partner_sees,
            partner_queries,
            prior_up,
            [up, down],
            (tuple(beside),),
            None,
            (h,),
            state=partner_state,
            final=True,
            partner=True,
            page_source=page_source,
            before=before,
        )

    sent, own_pages = attend_partner(0, [where, column] + rings, [])
    second = attend_partner(1, None, [sent])
    other = [swap_pool(sent), swap_pool(second)]
    own = attend(
        own_sees,
        span_token_queries,
        prior_up,
        [up, down] + rings + [prior_up, prior_down],
        (
            tuple((6 + p, k, None) for p, k, _ in earlier_sides) + tuple(pairs(2)[:4]),
            tuple(pairs(2)[4:] + beside),
        ),
        None,
        both,
        diagonal=(2, 0, 0),
        state=own_state,
        final=True,
        before=[second],
    )
    span_attention, handoff_pages = combine(where, own, other, own_pages)
    return (span_attention, handoff_pages, decode_attention)


def solution(mesh):
    in_specs = (
        P(("ctx", "pool"), "tp"),
        P(("ctx", "pool"), "tp"),
        P("tp", ("ctx", "pool"), None),
        P(("ctx", "pool"), None, "tp"),
        P(("ctx", "pool"), None, "tp"),
        P(("ctx", "pool"), "tp", None, None),
        P("tp", None),
        P("tp", None),
        P(),
        P(("ctx", "pool")),
        P(("ctx", "pool")),
        P(("ctx", "pool")),
        P(("ctx", "pool")),
        P(),
    )
    out_specs = (
        P(("ctx", "pool"), "tp"),
        P(("ctx", "pool"), "tp", None, None),
        P(("ctx", "pool"), None, "tp"),
    )
    return jax.shard_map(
        per_device, mesh=mesh, in_specs=in_specs, out_specs=out_specs, check_vma=False
    )
```

```python
import functools
import math

import jax
import jax.numpy as jnp
from jax import lax
from jax.experimental import pallas as pl
from jax.experimental.pallas import tpu as pltpu
from jax.sharding import PartitionSpec as P

HQ = 64
KEY_VALUE_HEADS = 8
HEAD_SIZE = 128
ADAPTER_RANK = 16
BLK = 16
STEPS = 4
GROUP = HQ // KEY_VALUE_HEADS
SHARDS = 16
SIDE = 4
TOKENS = 128
ROWS = 16
DECODE = ROWS * STEPS
ALL_ROWS = TOKENS + DECODE
LOG2_SCALE = math.log2(math.e) / math.sqrt(HEAD_SIZE)
neg_large = -1e30
MIB = 2**20
WIDTH = 2 * HEAD_SIZE


def estimate(us):
    return pl.CostEstimate(flops=int(us * 1.1e9), bytes_accessed=MIB, transcendentals=0)


def split3(x):
    hi = x.astype(jnp.bfloat16)
    rest = x - hi.astype(jnp.float32)
    mid = rest.astype(jnp.bfloat16)
    low = (rest - mid.astype(jnp.float32)).astype(jnp.bfloat16)
    return hi, mid, low

PROJECT_US, ATTEND_US, DECODE_US = 1, 1.7, 1
ATTEND_VMEM, PROJECT_VMEM, DECODE_VMEM = 24, 56, 24


CHUNKS = 4
OWNERS = (1, 3, 0, 2)


def project_kernel(
    row_adapter_hbm,
    adapter_hbm,
    span_ref,
    decode_ref,
    weight_ref,
    down_ref,
    up_ref,
    core_hbm,
    kept_hbm,
    row_adapter_ref,
    adapter_ref,
    core_ref,
    kept_ref,
    hidden_ref,
    rank_ref,
    buffer_ref,
    decode_buffer,
    down_buffer,
    up_buffer,
    sems,
    small_sems,
    out_sems,
):
    tp = lax.axis_index("tp")
    depth = weight_ref.shape[0] // CHUNKS
    small = [
        pltpu.make_async_copy(row_adapter_hbm, row_adapter_ref, small_sems.at[4]),
        pltpu.make_async_copy(adapter_hbm, adapter_ref, small_sems.at[5]),
        pltpu.make_async_copy(span_ref, hidden_ref.at[pl.ds(0, TOKENS)], small_sems.at[0]),
        pltpu.make_async_copy(decode_ref, decode_buffer, small_sems.at[1]),
        pltpu.make_async_copy(down_ref, down_buffer, small_sems.at[2]),
        pltpu.make_async_copy(up_ref, up_buffer, small_sems.at[3]),
    ]
    for copy in small:
        copy.start()
    columns = [pl.multiple_of(jnp.bitwise_xor(tp, bit) * 2 * WIDTH, 2 * WIDTH) for bit in OWNERS]
    copies = [
        [
            pltpu.make_async_copy(
                weight_ref.at[pl.ds(k * depth, depth), pl.ds(column, 2 * WIDTH)],
                buffer_ref.at[i, pl.ds(k * depth, depth)],
                sems.at[i, k],
            )
            for k in range(CHUNKS)
        ]
        for i, column in enumerate(columns)
    ]
    for group in copies:
        for copy in group:
            copy.start()
    for copy in small[:2]:
        copy.wait()
    span_owner = jnp.transpose(jnp.broadcast_to(adapter_ref[...], (TOKENS, TOKENS)))
    row = lax.broadcasted_iota(jnp.int32, (DECODE, TOKENS), 0) // STEPS
    decode_owner = jnp.zeros((DECODE, TOKENS), jnp.int32)
    for r in range(ROWS):
        decode_owner = jnp.where(row == r, row_adapter_ref[r], decode_owner)
    owner = jnp.concatenate([span_owner, decode_owner], axis=0)
    column = lax.broadcasted_iota(jnp.int32, (ALL_ROWS, TOKENS), 1) // ADAPTER_RANK
    for copy in small[2:]:
        copy.wait()
    hidden_ref[TOKENS:, :] = decode_buffer[...].reshape(DECODE, decode_buffer.shape[2])
    narrow = jnp.dot(hidden_ref[...], down_buffer[...], preferred_element_type=jnp.float32)
    for part, piece in enumerate(split3(jnp.where(column == owner, narrow, 0.0))):
        rank_ref[:, part * TOKENS : (part + 1) * TOKENS] = piece
    flushes = []
    for i, first in enumerate(columns):
        up = up_buffer[:, pl.ds(first, 2 * WIDTH)]
        out = jnp.dot(rank_ref[...], jnp.concatenate([up, up, up], axis=0), preferred_element_type=jnp.float32)
        for k in range(CHUNKS):
            copies[i][k].wait()
            here = slice(k * depth, (k + 1) * depth)
            out = out + jnp.dot(hidden_ref[:, here], buffer_ref[i, here, :], preferred_element_type=jnp.float32)
        out_ref, out_hbm = (core_ref, core_hbm) if i < 2 else (kept_ref, kept_hbm)
        out_ref[2 * (i % 2)] = out[:, :WIDTH]
        out_ref[2 * (i % 2) + 1] = out[:, WIDTH:]
        part = pl.ds(2 * (i % 2), 2)
        flush = pltpu.make_async_copy(out_ref.at[part], out_hbm.at[part], out_sems.at[i])
        flush.start()
        flushes.append(flush)
    for flush in flushes:
        flush.wait()


def project(row_adapter, adapter, span, decode, weight, down, up):
    depth = span.shape[1]
    far = pl.BlockSpec(memory_space=pl.ANY)
    return pl.pallas_call(
        project_kernel,
        in_specs=[far] * 7,
        out_specs=[far] * 2,
        out_shape=[jax.ShapeDtypeStruct((4, ALL_ROWS, WIDTH), jnp.float32)] * 2,
        scratch_shapes=[
            pltpu.SMEM(row_adapter.shape, jnp.int32),
            pltpu.VMEM(adapter.shape, jnp.int32),
            pltpu.VMEM((4, ALL_ROWS, WIDTH), jnp.float32),
            pltpu.VMEM((4, ALL_ROWS, WIDTH), jnp.float32),
            pltpu.VMEM((ALL_ROWS, depth), jnp.bfloat16),
            pltpu.VMEM((ALL_ROWS, 3 * TOKENS), jnp.bfloat16),
            pltpu.VMEM((4, depth, 2 * WIDTH), jnp.bfloat16),
            pltpu.VMEM(decode.shape, jnp.bfloat16),
            pltpu.VMEM(down.shape, jnp.bfloat16),
            pltpu.VMEM(up.shape, jnp.bfloat16),
            pltpu.SemaphoreType.DMA((4, CHUNKS)),
            pltpu.SemaphoreType.DMA((6,)),
            pltpu.SemaphoreType.DMA((4,)),
        ],
        compiler_params=pltpu.CompilerParams(vmem_limit_bytes=PROJECT_VMEM * MIB),
        cost_estimate=estimate(PROJECT_US),
        name="project",
    )(row_adapter, adapter, span, decode, weight, down, up)


def finish_kernel(own_ref, chip_ref, queries_ref, *refs):
    span_ref, decode_ref, late_ref = refs[-3:]
    late_ref[...] = queries_ref[...]
    total = (own_ref[...] + chip_ref[...]).astype(jnp.bfloat16)
    span_ref[...] = total[:, :TOKENS]
    decode_ref[...] = total[:, TOKENS:]


def finish(own_sum, from_chip, queries, after):
    heads, _, width = from_chip.shape
    local = pl.BlockSpec(memory_space=pltpu.VMEM)
    return pl.pallas_call(
        finish_kernel,
        in_specs=[local] * 3 + [pl.BlockSpec(memory_space=pl.ANY)] * len(after),
        out_specs=[local] * 3,
        out_shape=[
            jax.ShapeDtypeStruct((heads, TOKENS, width), jnp.bfloat16),
            jax.ShapeDtypeStruct((heads, DECODE, width), jnp.bfloat16),
            jax.ShapeDtypeStruct(queries.shape, jnp.bfloat16),
        ],
        compiler_params=pltpu.CompilerParams(vmem_limit_bytes=8 * MIB),
        cost_estimate=estimate(0.5),
        name="finish",
    )(own_sum, from_chip, queries, *after)


TILE = 2
TILE_ROWS = TILE * TOKENS
TILES = GROUP // TILE
HEAD_ROWS = GROUP * TOKENS
HEAD_COLUMNS = GROUP * HEAD_SIZE


def pick_pages(where_ref, column_ref, up_ref, down_ref, ring_refs, own_ref, other_ref, at):
    count = own_ref.shape[0]
    for n in range(2 * count):
        dz, dy = where_ref[0, n], where_ref[1, n]
        rows = pl.ds(pl.multiple_of(where_ref[2, n] * BLK, BLK), BLK)
        for h in range(2):
            page = column_ref[dy, h, rows, :]
            page = jnp.where(dz == 1, up_ref[dy, h, rows, :], page)
            page = jnp.where(dz == 3, down_ref[dy, h, rows, :], page)
            for k in range(SIDE):
                page = jnp.where((dz == 2) & (dy == k), ring_refs[k][1, h, rows, :], page)
            if n < count:
                own_ref[n, h] = page
            else:
                here = slice((n - count) * BLK, (n - count + 1) * BLK)
                other_ref[0, here, at + h * WIDTH : at + (h + 1) * WIDTH] = page


def attend_kernel(
    heads, count, blocks, diagonal, has_state, final, partner, has_pages, visible_ref, q_ref, known_ref, *refs
):
    pieces, state_ref, refs = refs[:count], refs[count], refs[count + 1 :]
    out_ref = refs[-4] if has_pages else refs[-3]
    key_ref, ext_ref = refs[-2:]
    if has_pages:
        pick_pages(
            refs[0],
            refs[1],
            pieces[0],
            pieces[1],
            refs[2 : 2 + SIDE],
            refs[-3],
            out_ref,
            HEAD_COLUMNS + HEAD_SIZE,
        )
    wide = lax.broadcasted_iota(jnp.int32, (TILE_ROWS, HEAD_SIZE), 1)
    lane = wide[:TOKENS]
    one = jnp.ones((TOKENS, HEAD_SIZE), jnp.bfloat16)
    zero = jnp.zeros((TOKENS, HEAD_SIZE), jnp.bfloat16)
    bounds = [0]
    for shards in blocks:
        bounds.append(bounds[-1] + len(shards) * TOKENS)
    for slot, h in enumerate(heads):
        for b, shards in enumerate(blocks):
            for n, (piece, index, place) in enumerate(shards):
                kv = pieces[piece][index, h]
                keys, values, ones = kv[:, :HEAD_SIZE], kv[:, HEAD_SIZE:], one
                if place is not None:
                    seen = visible_ref[place] != 0
                    keys = jnp.where(seen, keys, known_ref[0, h, :, :HEAD_SIZE])
                    values = jnp.where(seen, values, zero)
                    ones = jnp.where(seen, one, zero)
                here = slice(bounds[b] + n * TOKENS, bounds[b] + (n + 1) * TOKENS)
                key_ref[slot, here, :] = keys
                ext_ref[slot, here, :HEAD_SIZE] = values
                ext_ref[slot, here, HEAD_SIZE:] = ones
        queries = [
            jnp.concatenate(
                [
                    q_ref[:, h * HEAD_COLUMNS + g * HEAD_SIZE : h * HEAD_COLUMNS + (g + 1) * HEAD_SIZE]
                    for g in range(i * TILE, (i + 1) * TILE)
                ],
                axis=0,
            )
            for i in range(TILES)
        ]

        def score(i, b):
            scores = lax.dot_general(
                queries[i],
                key_ref[slot, bounds[b] : bounds[b + 1], :],
                (((1,), (1,)), ((), ())),
                preferred_element_type=jnp.float32,
            )
            if diagonal is not None and diagonal in blocks[b]:
                at = blocks[b].index(diagonal) * TOKENS
                token = lax.broadcasted_iota(jnp.int32, (TILE_ROWS, TOKENS), 0) % TOKENS
                parts = [scores[:, :at]] if at else []
                parts.append(jnp.where(wide <= token, scores[:, at : at + TOKENS], neg_large))
                if at + TOKENS < scores.shape[1]:
                    parts.append(scores[:, at + TOKENS :])
                scores = jnp.concatenate(parts, axis=1)
            return scores, jnp.max(scores, axis=1, keepdims=True) * LOG2_SCALE

        steps = [(i, b) for i in range(TILES) for b in range(len(blocks))]
        if final:
            stats = jnp.zeros((TOKENS, HEAD_SIZE), out_ref.dtype)
        coming = score(*steps[0])
        for n, (i, b) in enumerate(steps):
            scores, top = coming
            if n + 1 < len(steps):
                coming = score(*steps[n + 1])
            here = slice(i * TILE_ROWS, (i + 1) * TILE_ROWS)
            if b or has_state:
                if not b:
                    top_before = state_ref[h, here, HEAD_SIZE : HEAD_SIZE + 1]
                    total = jnp.concatenate(
                        [
                            state_ref[h, here, :HEAD_SIZE],
                            jnp.broadcast_to(state_ref[h, here, WIDTH - 1 :], (TILE_ROWS, HEAD_SIZE)),
                        ],
                        axis=1,
                    )
                top = jnp.maximum(top_before, top)
                total = total * jnp.exp2(top_before - top)
            weights = jnp.exp2(scores * LOG2_SCALE - top).astype(jnp.bfloat16)
            added = jnp.dot(
                weights, ext_ref[slot, bounds[b] : bounds[b + 1], :], preferred_element_type=jnp.float32
            )
            total = total + added if b or has_state else added
            top_before = top
            if b < len(blocks) - 1:
                continue
            if not final:
                out_ref[slot, here, :HEAD_SIZE] = total[:, :HEAD_SIZE]
                out_ref[slot, here, HEAD_SIZE:] = jnp.where(wide < HEAD_SIZE // 2, top, total[:, HEAD_SIZE:])
                continue
            out = total[:, :HEAD_SIZE] / total[:, HEAD_SIZE:]
            level = top + jnp.log2(total[:, HEAD_SIZE:])
            for j in range(TILE):
                g = i * TILE + j
                own = slice(j * TOKENS, (j + 1) * TOKENS)
                out_ref[slot, :, g * HEAD_SIZE : (g + 1) * HEAD_SIZE] = out[own].astype(out_ref.dtype)
                parts = split3(level[own]) if partner else (level[own],)
                for part, piece in enumerate(parts):
                    stats = jnp.where(lane == part * GROUP + g, piece, stats)
        if final:
            out_ref[slot, :, HEAD_COLUMNS : HEAD_COLUMNS + HEAD_SIZE] = stats


def attend(
    visible,
    queries,
    known,
    pieces,
    blocks,
    after,
    heads,
    diagonal=None,
    state=None,
    final=False,
    partner=False,
    page_source=None,
    before=(),
):
    shards = sum(len(block) for block in blocks)
    count = len(heads)
    if final:
        out_shape = (count, TOKENS, HEAD_COLUMNS + HEAD_SIZE + (0 if page_source is None else 2 * WIDTH))
    else:
        out_shape = (count, HEAD_ROWS, WIDTH)
    local = pl.BlockSpec(memory_space=pltpu.VMEM)
    scalar = pl.BlockSpec(memory_space=pltpu.SMEM)
    out_shape = jax.ShapeDtypeStruct(out_shape, jnp.bfloat16 if partner and final else jnp.float32)
    out_specs = local
    more, more_specs = [], []
    if page_source is not None:
        own_pages = jax.ShapeDtypeStruct((TOKENS // BLK, 2, BLK, WIDTH), jnp.bfloat16)
        out_shape, out_specs = [out_shape, own_pages], [local, local]
        more, more_specs = list(page_source), [scalar] + [local] * (len(page_source) - 1)
    more += before
    more_specs += [pl.BlockSpec(memory_space=pl.ANY)] * len(before)
    return pl.pallas_call(
        functools.partial(
            attend_kernel,
            heads,
            len(pieces),
            blocks,
            diagonal,
            state is not None,
            final,
            partner,
            page_source is not None,
        ),
        in_specs=[scalar]
        + [local] * (2 + len(pieces))
        + [pl.BlockSpec(memory_space=pl.ANY) if state is None else local]
        + more_specs,
        out_specs=out_specs,
        scratch_shapes=[
            pltpu.VMEM((count, shards * TOKENS, HEAD_SIZE), jnp.bfloat16),
            pltpu.VMEM((count, shards * TOKENS, WIDTH), jnp.bfloat16),
        ],
        out_shape=out_shape,
        compiler_params=pltpu.CompilerParams(vmem_limit_bytes=ATTEND_VMEM * MIB),
        cost_estimate=estimate(ATTEND_US * count * shards / 16),
        name="attend_last" if final else "attend_first",
    )(visible, queries, known, *pieces, after if state is None else state, *more)


def combine_kernel(where_ref, own_ref, first_ref, second_ref, pages_ref, out_ref, handoff_ref):
    for n in range(handoff_ref.shape[0]):
        mine = where_ref[3, n] != 0
        for h in range(2):
            at = HEAD_COLUMNS + HEAD_SIZE + h * WIDTH
            theirs = first_ref[0, n * BLK : (n + 1) * BLK, at : at + WIDTH]
            handoff_ref[n, h] = jnp.where(mine, pages_ref[n, h], theirs)
    for h in range(2):
        other_ref = (first_ref, second_ref)[h]
        at = HEAD_COLUMNS
        mine = own_ref[h, :, at : at + GROUP]
        parts = other_ref[0, :, at : at + HEAD_SIZE].astype(jnp.float32)
        theirs = parts[:, :GROUP] + parts[:, GROUP : 2 * GROUP] + parts[:, 2 * GROUP : 3 * GROUP]
        peak = jnp.maximum(mine, theirs)
        mine = jnp.exp2(mine - peak)
        theirs = jnp.exp2(theirs - peak)
        whole = mine + theirs
        mine, theirs = mine / whole, theirs / whole
        for g in range(GROUP):
            columns = slice(g * HEAD_SIZE, (g + 1) * HEAD_SIZE)
            mixed = mine[:, g : g + 1] * own_ref[h, :, columns] + theirs[:, g : g + 1] * other_ref[
                0, :, columns
            ].astype(jnp.float32)
            at = h * HEAD_COLUMNS + g * HEAD_SIZE
            out_ref[:, at : at + HEAD_SIZE] = mixed.astype(jnp.bfloat16)


def combine(where, own, other, own_pages):
    local = pl.BlockSpec(memory_space=pltpu.VMEM)
    return pl.pallas_call(
        combine_kernel,
        in_specs=[pl.BlockSpec(memory_space=pltpu.SMEM)] + [local] * 4,
        out_specs=[local] * 2,
        out_shape=[
            jax.ShapeDtypeStruct((TOKENS, 2 * HEAD_COLUMNS), jnp.bfloat16),
            jax.ShapeDtypeStruct(own_pages.shape, jnp.bfloat16),
        ],
        compiler_params=pltpu.CompilerParams(vmem_limit_bytes=16 * MIB),
        cost_estimate=estimate(1),
        name="combine",
    )(where, own, *other, own_pages)


ROW_BLOCK = 8


def decode_kernel(length_ref, live_ref, q_ref, cache_ref, fresh_ref, out_ref):
    first = pl.program_id(0) * ROW_BLOCK
    query_rows = STEPS * GROUP
    rows = ROW_BLOCK * query_rows
    contract = (((1,), (1,)), ((), ()))
    slot = lax.broadcasted_iota(jnp.int32, (query_rows, cache_ref.shape[2]), 1)
    fresh_row = lax.broadcasted_iota(jnp.int32, (rows, DECODE), 1) // STEPS
    fresh_step = lax.broadcasted_iota(jnp.int32, (rows, DECODE), 1) % STEPS
    row = lax.broadcasted_iota(jnp.int32, (rows, DECODE), 0) // query_rows
    step = lax.broadcasted_iota(jnp.int32, (rows, DECODE), 0) % STEPS
    fresh_seen = (fresh_row == row + first) & (fresh_step <= step)
    queries = q_ref[...].reshape(ROW_BLOCK * STEPS, q_ref.shape[2]).astype(jnp.float32)
    cached, fresh = [], []
    for h in range(2):
        of_head = []
        for n in range(ROW_BLOCK):
            of_row = jnp.concatenate(
                [
                    queries[n * STEPS : (n + 1) * STEPS, g * HEAD_SIZE : (g + 1) * HEAD_SIZE]
                    for g in range(h * GROUP, (h + 1) * GROUP)
                ],
                axis=0,
            ).astype(jnp.bfloat16)
            of_head.append(of_row)
            scores = lax.dot_general(
                of_row, cache_ref[n, h, :, :HEAD_SIZE], contract, preferred_element_type=jnp.float32
            )
            cached.append(jnp.where(slot < length_ref[first + n], scores, neg_large))
        scores = lax.dot_general(
            jnp.concatenate(of_head, axis=0),
            fresh_ref[h, :, :HEAD_SIZE],
            contract,
            preferred_element_type=jnp.float32,
        )
        fresh.append(jnp.where(fresh_seen, scores, neg_large))
    cached = jnp.concatenate(cached, axis=0)
    fresh = jnp.concatenate(fresh, axis=0)
    top = jnp.maximum(jnp.max(cached, axis=1, keepdims=True), jnp.max(fresh, axis=1, keepdims=True))
    cached = jnp.exp2((cached - top) * LOG2_SCALE)
    fresh = jnp.exp2((fresh - top) * LOG2_SCALE)
    total = jnp.sum(cached, axis=1, keepdims=True) + jnp.sum(fresh, axis=1, keepdims=True)
    cached = cached.astype(jnp.bfloat16)
    fresh = fresh.astype(jnp.bfloat16)
    for h in range(2):
        of_fresh = jnp.dot(
            fresh[h * rows : (h + 1) * rows], fresh_ref[h, :, HEAD_SIZE:], preferred_element_type=jnp.float32
        )
        for n in range(ROW_BLOCK):
            here = slice(h * rows + n * query_rows, h * rows + (n + 1) * query_rows)
            out = jnp.dot(cached[here], cache_ref[n, h, :, HEAD_SIZE:], preferred_element_type=jnp.float32)
            out = (out + of_fresh[n * query_rows : (n + 1) * query_rows]) / total[here]
            out = jnp.where(first + n < live_ref[0], out, 0.0)
            for g in range(GROUP):
                columns = slice((h * GROUP + g) * HEAD_SIZE, (h * GROUP + g + 1) * HEAD_SIZE)
                out_ref[n, :, columns] = out[g * STEPS : (g + 1) * STEPS].astype(jnp.bfloat16)


def decode_attend(lengths, live, queries, cache, fresh):
    rows, heads, cache_size, _ = cache.shape
    block = pl.BlockSpec((ROW_BLOCK,) + queries.shape[1:], lambda i, *_: (i, 0, 0))
    return pl.pallas_call(
        decode_kernel,
        grid_spec=pltpu.PrefetchScalarGridSpec(
            num_scalar_prefetch=2,
            grid=(rows // ROW_BLOCK,),
            in_specs=[
                block,
                pl.BlockSpec((ROW_BLOCK, heads, cache_size, WIDTH), lambda i, *_: (i, 0, 0, 0)),
                pl.BlockSpec((heads, DECODE, WIDTH), lambda i, *_: (0, 0, 0)),
            ],
            out_specs=block,
        ),
        out_shape=jax.ShapeDtypeStruct(queries.shape, jnp.bfloat16),
        compiler_params=pltpu.CompilerParams(vmem_limit_bytes=DECODE_VMEM * MIB),
        cost_estimate=estimate(DECODE_US),
        name="decode",
    )(lengths, live, queries, cache, fresh)


def stack_kernel(*refs):
    out_ref = refs[-1]
    for y in range(SIDE):
        out_ref[y] = refs[y][0]


def stack_column(rings, after):
    local = pl.BlockSpec(memory_space=pltpu.VMEM)
    return pl.pallas_call(
        stack_kernel,
        in_specs=[local] * SIDE + [pl.BlockSpec(memory_space=pl.ANY)] * len(after),
        out_specs=local,
        out_shape=jax.ShapeDtypeStruct((SIDE,) + rings[0].shape[1:], jnp.bfloat16),
        compiler_params=pltpu.CompilerParams(vmem_limit_bytes=8 * MIB),
        cost_estimate=estimate(0.5),
        name="stack",
    )(*rings, *after)


def shift(x, dz, dy):
    perm = [
        (z * SIDE + y, ((z + dz) % SIDE) * SIDE + (y + dy) % SIDE) for z in range(SIDE) for y in range(SIDE)
    ]
    return lax.ppermute(x, "ctx", perm)


def swap_pool(x):
    return lax.ppermute(x, "pool", [(0, 1), (1, 0)])


def swap_tp(x, bit):
    return lax.ppermute(x, "tp", [(i, i ^ bit) for i in range(4)])


def ring(x):
    pair = jnp.stack([x, shift(x, 2, 0)])
    far = {1: shift(pair, 0, 1), 3: shift(pair, 0, 3), 2: shift(pair, 0, 2)}
    return [pair, far[1], far[2], far[3]]


def sides(column):
    return shift(column, 1, 0), shift(column, 3, 0)


def per_device(
    span_hidden_states,
    span_token_queries,
    earlier_key_values,
    decode_hidden_states,
    decode_token_queries,
    decode_row_cache,
    key_value_weight,
    adapter_down_weight,
    adapter_up_weight,
    prompt_adapter,
    row_adapter_index,
    group_live_rows,
    cached_row_lengths,
    block_target_page,
):
    ctx = lax.axis_index("ctx")
    pool = lax.axis_index("pool")
    my_z, my_y = ctx // SIDE, ctx % SIDE

    prior_rings = ring(earlier_key_values)

    for_core, kept = project(
        row_adapter_index,
        prompt_adapter.reshape(1, TOKENS),
        span_hidden_states,
        decode_hidden_states,
        key_value_weight,
        adapter_down_weight,
        adapter_up_weight,
    )
    from_core = swap_tp(for_core, 1)
    from_chip = swap_tp(kept[2:] + from_core[2:], 2)
    span_kv, decode_kv, late_queries = finish(
        kept[:2] + from_core[:2], from_chip, span_token_queries, (prior_rings[0],)
    )

    rings = ring(span_kv)

    decode_attention = decode_attend(
        cached_row_lengths, group_live_rows, decode_token_queries, decode_row_cache, decode_kv
    )

    far = jnp.arange(SIDE, dtype=jnp.int32)
    shard_z, shard_y = jnp.mod(my_z - far, SIDE), jnp.mod(my_y - far, SIDE)
    place = shard_z[:, None] * SIDE + shard_y[None, :]
    partner_sees = ((place < ctx) | ((place == ctx) & (pool == 0))).astype(jnp.int32).reshape(-1)
    own_sees = (place <= ctx).astype(jnp.int32).reshape(-1)
    earlier_sides = [(p, k, None) for p in range(2) for k in range(SIDE)]

    def earlier_pairs(first):
        return [(first + k, j, None) for j in range(2) for k in range(SIDE)]

    def pairs(first):
        return [(first + k, j, 2 * j * SIDE + k) for j in range(2) for k in range(SIDE)]

    beside = [(p, k, (1 + 2 * p) * SIDE + k) for p in range(2) for k in range(SIDE)]
    both = (0, 1)
    partner_queries = swap_pool(late_queries)
    own_state = attend(
        own_sees,
        span_token_queries,
        prior_rings[0],
        prior_rings,
        (tuple(earlier_pairs(0)),),
        row_adapter_index,
        both,
    )

    partner_first = attend(
        partner_sees,
        partner_queries,
        prior_rings[0],
        prior_rings,
        (tuple(earlier_pairs(0)),),
        own_state,
        both,
    )

    prior_up, prior_down = sides(stack_column(prior_rings, (decode_attention, rings[0])))
    column = stack_column(rings, (own_state, partner_first))
    up, down = sides(column)
    partner_state = attend(
        partner_sees,
        partner_queries,
        prior_up,
        [prior_up, prior_down] + rings,
        (tuple(earlier_sides), tuple(pairs(2))),
        None,
        both,
        state=partner_first,
        before=[column],
    )

    pages = TOKENS // BLK
    shard = ctx * 2 + pool
    partner_shard = ctx * 2 + 1 - pool
    page_ids = jnp.concatenate([shard * pages + jnp.arange(pages), partner_shard * pages + jnp.arange(pages)])
    block_ids = jnp.arange(block_target_page.shape[0], dtype=jnp.int32)
    source = jnp.sum(
        jnp.where(block_target_page[None, :] == page_ids[:, None], block_ids[None, :], 0), axis=1
    )
    source_shard = source // pages
    source_ctx = source_shard // 2
    where = jnp.stack(
        [
            jnp.mod(my_z - source_ctx // SIDE, SIDE),
            jnp.mod(my_y - source_ctx % SIDE, SIDE),
            source % pages,
            (source_shard % 2 == pool).astype(jnp.int32),
        ]
    ).astype(jnp.int32)

    def attend_partner(h, page_source, before):
        return attend(
            partner_sees,
            partner_queries,
            prior_up,
            [up, down],
            (tuple(beside),),
            None,
            (h,),
            state=partner_state,
            final=True,
            partner=True,
            page_source=page_source,
            before=before,
        )

    sent, own_pages = attend_partner(0, [where, column] + rings, [])
    second = attend_partner(1, None, [sent])
    other = [swap_pool(sent), swap_pool(second)]
    own = attend(
        own_sees,
        span_token_queries,
        prior_up,
        [up, down] + rings + [prior_up, prior_down],
        (
            tuple((6 + p, k, None) for p, k, _ in earlier_sides) + tuple(pairs(2)[:4]),
            tuple(pairs(2)[4:] + beside),
        ),
        None,
        both,
        diagonal=(2, 0, 0),
        state=own_state,
        final=True,
        before=[second],
    )
    span_attention, handoff_pages = combine(where, own, other, own_pages)
    return (span_attention, handoff_pages, decode_attention)


def solution(mesh):
    in_specs = (
        P(("ctx", "pool"), "tp"),
        P(("ctx", "pool"), "tp"),
        P("tp", ("ctx", "pool"), None),
        P(("ctx", "pool"), None, "tp"),
        P(("ctx", "pool"), None, "tp"),
        P(("ctx", "pool"), "tp", None, None),
        P("tp", None),
        P("tp", None),
        P(),
        P(("ctx", "pool")),
        P(("ctx", "pool")),
        P(("ctx", "pool")),
        P(("ctx", "pool")),
        P(),
    )
    out_specs = (
        P(("ctx", "pool"), "tp"),
        P(("ctx", "pool"), "tp", None, None),
        P(("ctx", "pool"), None, "tp"),
    )
    return jax.shard_map(
        per_device, mesh=mesh, in_specs=in_specs, out_specs=out_specs, check_vma=False
    )
```
